256 devices in a mesh: lat: 8 (over x_hi, y), lon: 32 (over z, x_lo, core).
Axes of the slice: x: 4 (x_hi: 2, x_lo: 2; x = x_hi * 2 + x_lo), y: 4, z: 8, core: 2. Of those that a mesh axis runs over, the one named last changes fastest.
Arguments:
- tokens: bfloat16 [1, 96, 384, 2, 512], P(None, 'lat', 'lon'), may hold values from -6 to 6
- layer_norm_gain: float32 [512], replicated, may hold values from 0.25 to 1.75
- cotangent: bfloat16 [1, 96, 384, 2, 512], P(None, 'lat', 'lon'), may hold values from -6 to 6
- w_qkv: bfloat16 [512, 1536], replicated, may hold values from -2 to 2
- w_out: bfloat16 [512, 512], replicated, may hold values from -0.25 to 0.25
Outputs:
- mixed: bfloat16 [1, 96, 384, 2, 512], P(None, 'lat', 'lon')
- grad_tokens: bfloat16 [1, 96, 384, 2, 512], P(None, 'lat', 'lon')
- gain_gradient: float32 [512], replicated
- grad_qkv: bfloat16 [512, 1536], replicated
- grad_out: bfloat16 [512, 512], replicated
The draws below stay inside these ranges and needn't reach their ends.
All inputs are finite; a program needn't handle non-finite values.
Results may differ from the reference program's by a relative error of at most 0.02.
Values may be sent and summed in bfloat16 or wider, within the bound.
No kernel may reach another device: no remote copies, remote signals or barrier semaphores. Data moves between devices by JAX's collectives and lax.ppermute only.
A program may use at most 64 MiB of HBM per device.

```python
import math
import jax
import jax.numpy as jnp
from jax import lax

D = 512
HEADS = 16
WIN = 12
SHIFT = 6
LEV = 2
BATCH = 1
NLAT = 96
NLON = 384


def draw_w_qkv(key, part):
    key = jax.random.fold_in(key, 7)
    base_key = jax.random.fold_in(key, 0)
    return (jnp.clip(jax.random.normal(base_key, (D, 3 * D), jnp.float32), -4.0, 4.0) * D ** (-0.5)).astype(jnp.bfloat16)


def block_scale(stream_key, shape, cuts, least, high):
    factor_of = 1.0
    for position, parts in cuts:
        draws = jax.random.uniform(jax.random.fold_in(jax.random.fold_in(stream_key, 6), position), (parts,), jnp.float32, least / len(cuts), high / len(cuts))
        factor_of = factor_of * jnp.repeat(jnp.exp(draws), shape[position] // parts).reshape((-1,) + (1,) * (len(shape) - 1 - position))
    return factor_of


def centred(own_key, extent, deviation, most, cuts=(), kind=jnp.bfloat16):
    values = deviation * jax.random.normal(own_key, extent, jnp.float32)
    if cuts:
        values = values * block_scale(own_key, extent, cuts, -0.22, 0.18)
    return jnp.clip(values, -most, most).astype(kind)


def setup_inputs(seed: int = 0) -> dict:
    splits = jax.random.split(jax.random.key(seed), 6)
    tokens = centred(splits[0], (BATCH, NLAT, NLON, LEV, D), 1.0, 6.0, ((1, 8), (2, 32)))
    layer_norm_gain = jnp.clip(1.0 + 0.15 * jax.random.normal(splits[1], (D,), jnp.float32), 0.25, 1.75)
    cotangent = centred(splits[2], (BATCH, NLAT, NLON, LEV, D), 1.0, 6.0, ((1, 8), (2, 32)))
    w_qkv = draw_w_qkv(jax.random.fold_in(splits[5], 71), 0)
    w_out = centred(splits[4], (D, D), D ** -0.5, 0.25)
    return {"tokens": tokens, "layer_norm_gain": layer_norm_gain, "cotangent": cotangent, "w_qkv": w_qkv, "w_out": w_out}


EPS = 1e-05
MASKED = -1e+30

def to_windows(block):
    samples, lat_rows, lon_cols, levels, channels = block.shape
    parted = block.reshape(samples, lat_rows // WIN, WIN, lon_cols // WIN, WIN, levels, channels)
    parted = parted.transpose(0, 1, 3, 2, 4, 5, 6)
    return parted.reshape(samples * (lat_rows // WIN) * (lon_cols // WIN), WIN * WIN * levels, channels)

def from_windows(windows, leading):
    samples, lat_rows, lon_cols, levels = leading
    channels = windows.shape[-1]
    parted = windows.reshape(samples, lat_rows // WIN, lon_cols // WIN, WIN, WIN, levels, channels)
    return parted.transpose(0, 1, 3, 2, 4, 5, 6).reshape(samples, lat_rows, lon_cols, levels, channels)

def lowered(array):
    return lax.optimization_barrier(array.astype(jnp.bfloat16)).astype(jnp.float32)

def window_pass(window_item):
    qkv_rows, grad_attn, labels = window_item
    win_tokens = qkv_rows.shape[0]
    features = qkv_rows.shape[1] // 3
    head_size = features // HEADS
    inv_root = 1.0 / math.sqrt(head_size)
    queries = qkv_rows[:, :features].astype(jnp.float32).reshape(win_tokens, HEADS, head_size)
    key_rows = qkv_rows[:, features:2 * features].astype(jnp.float32).reshape(win_tokens, HEADS, head_size)
    values = qkv_rows[:, 2 * features:].astype(jnp.float32).reshape(win_tokens, HEADS, head_size)
    scores = jnp.einsum('qhd,khd->hqk', queries, key_rows) * inv_root
    allow = labels[:, None] == labels[None, :]
    scores = jnp.where(allow[None], scores, MASKED)
    row_max = lax.optimization_barrier(jnp.max(scores, -1, keepdims=True))
    exponent = jnp.exp(scores - row_max)
    attn_probs = exponent / lax.optimization_barrier(jnp.sum(exponent, -1, keepdims=True))
    probs_low = lowered(attn_probs)
    heads_out = jnp.einsum('hqk,khd->qhd', probs_low, values).astype(jnp.bfloat16).reshape(win_tokens, features)
    grad_heads = grad_attn.astype(jnp.float32).reshape(win_tokens, HEADS, head_size)
    grad_probs = jnp.einsum('qhd,khd->hqk', grad_heads, values)
    grad_values = jnp.einsum('hqk,qhd->khd', probs_low, grad_heads).astype(jnp.bfloat16)
    grad_scores = attn_probs * (grad_probs - lax.optimization_barrier(jnp.sum(grad_probs * attn_probs, -1, keepdims=True))) * inv_root
    scores_low = lowered(grad_scores)
    grad_queries = jnp.einsum('hqk,khd->qhd', scores_low, key_rows).astype(jnp.bfloat16)
    grad_keys = jnp.einsum('hqk,qhd->khd', scores_low, queries).astype(jnp.bfloat16)
    grad_qkv = jnp.concatenate([grad_queries.reshape(win_tokens, features), grad_keys.reshape(win_tokens, features), grad_values.reshape(win_tokens, features)], 1)
    return (heads_out, grad_qkv)

def reference(tokens, layer_norm_gain, cotangent, w_qkv, w_out):
    full_shape = tokens.shape
    leading = full_shape[:-1]
    features = full_shape[-1]
    tokens_wide = tokens.astype(jnp.float32)
    average = lax.optimization_barrier(jnp.mean(tokens_wide, -1, keepdims=True))
    mean_removed = tokens_wide - average
    inverse_deviation = lax.rsqrt(lax.optimization_barrier(jnp.mean(mean_removed * mean_removed, -1, keepdims=True)) + EPS)
    standardized_input = mean_removed * inverse_deviation
    gain_vector = layer_norm_gain.astype(jnp.float32)
    normalized_input = (standardized_input * gain_vector).astype(jnp.bfloat16)
    rolled = jnp.roll(normalized_input, (-SHIFT, -SHIFT), (1, 2))
    g_rolled = jnp.roll(cotangent, (-SHIFT, -SHIFT), (1, 2))
    flat_rows = rolled.reshape(-1, features)
    g_flat = g_rolled.reshape(-1, features)
    qkv_rows = jnp.dot(flat_rows, w_qkv, preferred_element_type=jnp.float32).astype(jnp.bfloat16)
    grad_attn = jnp.dot(g_flat, w_out.T, preferred_element_type=jnp.float32).astype(jnp.bfloat16)
    region = (jnp.arange(NLAT) >= NLAT - SHIFT).astype(jnp.int32)
    labels = jnp.broadcast_to(region[None, :, None, None, None], leading + (1,))
    attn_win, dqkv_win = lax.map(window_pass, (to_windows(qkv_rows.reshape(leading + (3 * features,))), to_windows(grad_attn.reshape(full_shape)), to_windows(labels)[:, :, 0]))
    attn = from_windows(attn_win, leading)
    back = jnp.roll(attn, (SHIFT, SHIFT), (1, 2))
    mixed = (tokens_wide + jnp.dot(back.reshape(-1, features), w_out, preferred_element_type=jnp.float32).reshape(full_shape)).astype(jnp.bfloat16)
    gradient_factor = 1.0 / math.sqrt(BATCH * NLAT * NLON * LEV)
    grad_out = (jnp.dot(attn.reshape(-1, features).T, g_flat, preferred_element_type=jnp.float32) * gradient_factor).astype(jnp.bfloat16)
    dqkv_rows = from_windows(dqkv_win, leading).reshape(-1, 3 * features)
    grad_qkv = (jnp.dot(flat_rows.T, dqkv_rows, preferred_element_type=jnp.float32) * gradient_factor).astype(jnp.bfloat16)
    d_rolled = jnp.dot(dqkv_rows, w_qkv.T, preferred_element_type=jnp.float32).astype(jnp.bfloat16).reshape(full_shape)
    normalized_gradient = jnp.roll(d_rolled, (SHIFT, SHIFT), (1, 2)).astype(jnp.float32)
    gain_gradient = lax.optimization_barrier(jnp.sum(normalized_gradient * standardized_input, axis=(0, 1, 2, 3))) * gradient_factor
    scaled_output = normalized_gradient * gain_vector
    inner_product = scaled_output - lax.optimization_barrier(jnp.mean(scaled_output, -1, keepdims=True)) - standardized_input * lax.optimization_barrier(jnp.mean(scaled_output * standardized_input, -1, keepdims=True))
    grad_tokens = (cotangent.astype(jnp.float32) + inverse_deviation * inner_product).astype(jnp.bfloat16)
    return (mixed, grad_tokens, gain_gradient, grad_qkv, grad_out)
```

```python
import math

import jax
import jax.numpy as jnp
from jax import lax
from jax.experimental import pallas as pl
from jax.experimental.pallas import tpu as pltpu
from jax.sharding import Mesh
from jax.sharding import PartitionSpec as P

HEADS = 16
WIN = 12
SHIFT = 6
EPS = 1e-05
MASKED = -1e30
F32 = jnp.float32
BF16 = jnp.bfloat16

LAT = ("xh", "y")
LON = ("z", "xl", "core")
CHIPS = ("xh", "y", "z", "xl")
EVERY = LAT + LON


def dot(a, b, dims=((1,), (0,))):
    return lax.dot_general(a, b, (dims, ((), ())), preferred_element_type=F32)


def normalise(tok):
    mean = jnp.mean(tok, -1, keepdims=True)
    centred = tok - mean
    inv = lax.rsqrt(jnp.mean(centred * centred, -1, keepdims=True) + EPS)
    return centred * inv, inv


def gather_quads(refs, which, out):
    rows = refs[0].shape[1]
    for j, ref in enumerate(refs):
        out[j * rows : (j + 1) * rows, :] = ref[which].astype(F32)


def grads_kernel(
    ids, q0, q1, q2, q3, gain, wqkv, wqkv_t, wout,
    keep, send, attn_t, d_t,
    wide, normed, g_low, qkv_t, kv, do_t,
):
    quads = (q0, q1, q2, q3)
    tokens, feat = normed.shape
    size = feat // HEADS
    per = 128 // size
    gather_quads(quads, 1, wide)
    g_low[...] = wide[...].astype(BF16)
    do_t[...] = dot(wout[...], g_low[...], ((1,), (1,))).astype(BF16)
    gather_quads(quads, 0, wide)
    xhat, _ = normalise(wide[...])
    normed[...] = (xhat * gain[...]).astype(BF16)
    qkv_t[...] = dot(wqkv_t[...], normed[...], ((1,), (1,))).astype(BF16)
    kv[...] = dot(normed[...], wqkv[:, feat:]).astype(BF16)

    half = tokens // 2
    lane = lax.broadcasted_iota(jnp.int32, (1, tokens), 1)
    edge = ids[0] == 1
    top = jnp.where(jnp.logical_and(edge, lane >= half), MASKED, 0.0).astype(F32)
    low = jnp.where(jnp.logical_and(edge, lane < half), MASKED, 0.0).astype(F32)
    inv_root = 1.0 / math.sqrt(size)
    to_exp2 = inv_root * math.log2(math.e)

    def spread(block, h):
        parts = []
        if h > 0:
            parts.append(jnp.zeros((h * size, tokens), BF16))
        parts.append(block)
        if h < per - 1:
            parts.append(jnp.zeros(((per - 1 - h) * size, tokens), BF16))
        return jnp.concatenate(parts, 0)

    def group(i, carry):
        at = pl.multiple_of(i * 128, 128)
        k4 = kv[:, pl.ds(at, 128)]
        v4 = kv[:, pl.ds(pl.multiple_of(feat + at, 128), 128)]
        for h in range(per):
            row = pl.multiple_of(at + h * size, size)
            q_h = qkv_t[pl.ds(row, size), :]
            k_h = qkv_t[pl.ds(pl.multiple_of(feat + row, size), size), :]
            v_h = qkv_t[pl.ds(pl.multiple_of(2 * feat + row, size), size), :]
            do_h = do_t[pl.ds(row, size), :]
            s = dot(k4, spread(q_h, h))
            s = jnp.concatenate([s[:half] + top, s[half:] + low], 0)
            e = jnp.exp2((s - jnp.max(s, 0, keepdims=True)) * to_exp2)
            p = e * (1.0 / jnp.sum(e, 0, keepdims=True))
            p_low = p.astype(BF16)
            dp = dot(v4, spread(do_h, h))
            delta = jnp.sum(dp * p, 0, keepdims=True)
            ds = (p * (dp - delta) * inv_root).astype(BF16)
            attn_t[pl.ds(row, size), :] = dot(v_h, p_low).astype(BF16)
            d_t[pl.ds(row, size), :] = dot(k_h, ds).astype(BF16)
            d_t[pl.ds(pl.multiple_of(feat + row, size), size), :] = dot(
                q_h, ds, ((1,), (1,))
            ).astype(BF16)
            d_t[pl.ds(pl.multiple_of(2 * feat + row, size), size), :] = dot(
                do_h, p_low, ((1,), (1,))
            ).astype(BF16)
        return carry

    lax.fori_loop(0, HEADS // per, group, 0)

    normed_t = normed[...].T
    core = ids[1]

    def emit(block, value):
        value = value.astype(BF16)
        at = (block % 2) * feat

        @pl.when(core == block // 2)
        def _():
            keep[at : at + feat, :] = value

        @pl.when(core != block // 2)
        def _():
            send[at : at + feat, :] = value

    for block in range(3):
        emit(block, dot(normed_t, d_t[block * feat : (block + 1) * feat, :], ((1,), (1,))))
    emit(3, dot(attn_t[...], g_low[...]))


def tokens_kernel(
    q0, q1, q2, q3, gain, wqkv, wout, attn_t, d_t, o0, o1, o2, o3, wide, back
):
    quads, outs = (q0, q1, q2, q3), (o0, o1, o2, o3)
    rows = q0.shape[1]
    gather_quads(quads, 0, wide)
    tok = wide[...]
    mixed = tok + dot(attn_t[...], wout[...], ((0,), (0,)))
    for j, out in enumerate(outs):
        out[0] = mixed[j * rows : (j + 1) * rows].astype(BF16)
    xhat, inv = normalise(tok)
    back[...] = dot(wqkv[...], d_t[...]).astype(BF16).astype(F32).T
    scaled = back[...] * gain[...]
    inner = (
        scaled
        - jnp.mean(scaled, -1, keepdims=True)
        - xhat * jnp.mean(scaled * xhat, -1, keepdims=True)
    )
    gather_quads(quads, 1, wide)
    grad = wide[...] + inv * inner
    for j, out in enumerate(outs):
        out[1] = grad[j * rows : (j + 1) * rows].astype(BF16)


def shards(tokens, layer_norm_gain, cotangent, w_qkv, w_out):
    _, lat_rows, lon_cols, levels, feat = tokens.shape
    lat_n, lon_n = lax.axis_size(LAT), lax.axis_size(LON)
    quad_tokens = SHIFT * SHIFT * levels
    n_tokens = 4 * quad_tokens
    keep_part, go_part = slice(SHIFT, lat_rows), slice(0, SHIFT)

    def pairs(d_lat, d_lon):
        return [
            (a * lon_n + o, (a + d_lat) % lat_n * lon_n + (o + d_lon) % lon_n)
            for a in range(lat_n)
            for o in range(lon_n)
        ]

    def quad(rows, cols):
        both = jnp.stack([tokens[0, rows, cols], cotangent[0, rows, cols]])
        return both.reshape(2, quad_tokens, feat)

    shifts = ((0, 0), (0, 1), (1, 0), (1, 1))
    cuts = [(go_part if a else keep_part, go_part if o else keep_part) for a, o in shifts]
    with jax.named_scope("window_in"):
        quads = [quad(*cut) for cut in cuts]
        quads = [
            q if s == (0, 0) else lax.ppermute(q, EVERY, pairs(-s[0], -s[1]))
            for q, s in zip(quads, shifts)
        ]
    gain_row = layer_norm_gain[None, :]
    core = lax.axis_index("core")
    ids = jnp.stack([(lax.axis_index(LAT) == lat_n - 1).astype(jnp.int32), core.astype(jnp.int32)])
    vmem = pl.BlockSpec(memory_space=pltpu.VMEM)
    smem = pl.BlockSpec(memory_space=pltpu.SMEM)
    params = pltpu.CompilerParams(vmem_limit_bytes=40 * 1024 * 1024)
    with jax.named_scope("window_grads"):
        keep, send, attn_t, d_t = pl.pallas_call(
            grads_kernel,
            in_specs=[smem] + [vmem] * 8,
            out_specs=[vmem] * 4,
            out_shape=[
                jax.ShapeDtypeStruct((2 * feat, feat), BF16),
                jax.ShapeDtypeStruct((2 * feat, feat), BF16),
                jax.ShapeDtypeStruct((feat, n_tokens), BF16),
                jax.ShapeDtypeStruct((3 * feat, n_tokens), BF16),
            ],
            scratch_shapes=[
                pltpu.VMEM((n_tokens, feat), F32),
                pltpu.VMEM((n_tokens, feat), BF16),
                pltpu.VMEM((n_tokens, feat), BF16),
                pltpu.VMEM((3 * feat, n_tokens), BF16),
                pltpu.VMEM((n_tokens, 2 * feat), BF16),
                pltpu.VMEM((feat, n_tokens), BF16),
            ],
            compiler_params=params,
        )(ids, *quads, gain_row, w_qkv, w_qkv.T, w_out)
    swap = [(0, 1), (1, 0)]
    with jax.named_scope("sum_cores"):
        other = lax.ppermute(send, "core", swap)
    with jax.named_scope("window_tokens"):
        outs = pl.pallas_call(
            tokens_kernel,
            in_specs=[vmem] * 9,
            out_specs=[vmem] * 4,
            out_shape=[jax.ShapeDtypeStruct((2, quad_tokens, feat), BF16)] * 4,
            scratch_shapes=[
                pltpu.VMEM((n_tokens, feat), F32),
                pltpu.VMEM((n_tokens, feat), F32),
            ],
            compiler_params=params,
        )(*quads, gain_row, w_qkv, w_out, attn_t, d_t)
    with jax.named_scope("window_out"):
        outs = [
            q if s == (0, 0) else lax.ppermute(q, EVERY, pairs(s[0], s[1]))
            for q, s in zip(outs, shifts)
        ]
        blocks = [o.reshape(2, SHIFT, SHIFT, levels, feat) for o in outs]
        lower = jnp.concatenate([blocks[1], blocks[0]], 2)
        upper = jnp.concatenate([blocks[3], blocks[2]], 2)
        both = jnp.concatenate([upper, lower], 1)
        mixed, grad_tokens = both[0][None], both[1][None]
    chips = lax.axis_size(CHIPS)
    factor = 1.0 / math.sqrt(lat_n * lat_rows * lon_n * lon_cols * levels)
    with jax.named_scope("sum_chips"):
        pair_sum = (keep.astype(F32) + other.astype(F32)).astype(BF16)
        pieces = lax.all_to_all(pair_sum.reshape(chips, -1, feat), CHIPS, 0, 0)
        piece = (jnp.sum(pieces.astype(F32), 0) * factor).astype(BF16)
    with jax.named_scope("share"):
        mine = lax.all_to_all(jnp.broadcast_to(piece[None], (chips,) + piece.shape), CHIPS, 0, 0)
        mine = mine.reshape(2, feat, feat)
        theirs = lax.ppermute(mine, "core", swap)
        first = jnp.where(core == 0, mine, theirs)
        second = jnp.where(core == 0, theirs, mine)
        grad_qkv = jnp.concatenate([first[0], first[1], second[0]], 1)
        grad_out = second[1]
    gain_gradient = (
        jnp.sum(grad_qkv.astype(F32) * w_qkv.astype(F32), 1) / layer_norm_gain
    )
    return mixed, grad_tokens, gain_gradient, grad_qkv, grad_out


def solution(mesh):
    fine = Mesh(mesh.devices.reshape(2, 4, 8, 2, 2), EVERY)
    grid = P(None, LAT, LON, None, None)
    return jax.shard_map(
        shards,
        mesh=fine,
        in_specs=(grid, P(), grid, P(), P()),
        out_specs=(grid, grid, P(), P(), P()),
        check_vma=False,
    )
```

```python
import functools
import math

import jax
import jax.numpy as jnp
from jax import lax
from jax.experimental import pallas as pl
from jax.experimental.pallas import tpu as pltpu
from jax.sharding import Mesh
from jax.sharding import PartitionSpec as P

HEADS = 16
WIN = 12
SHIFT = 6
EPS = 1e-05
MASKED = -1e30
F32 = jnp.float32
BF16 = jnp.bfloat16

LAT = ("xh", "y")
LON = ("zh", "zl", "xl", "core")
NEAR = ("xh", "y", "zl", "xl")
FAR = "zh"
EVERY = LAT + LON


def dot(a, b, dims=((1,), (0,))):
    return lax.dot_general(a, b, (dims, ((), ())), preferred_element_type=F32)


def normalise(tok):
    mean = jnp.mean(tok, -1, keepdims=True)
    centred = tok - mean
    inv = lax.rsqrt(jnp.mean(centred * centred, -1, keepdims=True) + EPS)
    return centred * inv, inv


def gather_quads(refs, which, out):
    rows = refs[0].shape[1]
    for j, ref in enumerate(refs):
        out[j * rows : (j + 1) * rows, :] = ref[which].astype(F32)


def lanes(shape):
    return lax.broadcasted_iota(jnp.int32, shape, len(shape) - 1)


def split_low(value, terms):
    lane = lanes(value.shape)
    out = jnp.zeros_like(value)
    rest = value
    for i in range(terms):
        part = rest.astype(BF16).astype(F32)
        out = jnp.where(lane == i, part, out)
        rest = rest - part
    return out.astype(BF16)


def grads_kernel(
    ids, q0, q1, q2, q3, gain, wqkv, wqkv_t, wout,
    keep, send, attn_t, back,
    wide, normed, g_low, qkv_t, kv, do_t, d_t, normed_t, gain_col,
):
    quads = (q0, q1, q2, q3)
    tokens, feat = normed.shape
    size = feat // HEADS
    per = 128 // size
    gather_quads(quads, 1, wide)
    g_low[...] = wide[...].astype(BF16)
    do_t[...] = dot(wout[...], g_low[...], ((1,), (1,))).astype(BF16)
    gather_quads(quads, 0, wide)
    xhat, _ = normalise(wide[...])
    wide[...] = xhat
    normed[...] = (xhat * gain[...]).astype(BF16)
    normed_t[...] = normed[...].T
    qkv_t[...] = dot(wqkv_t[...], normed[...], ((1,), (1,))).astype(BF16)
    kv[...] = dot(normed[...], wqkv[:, feat:]).astype(BF16)

    half = tokens // 2
    lane = lanes((1, tokens))
    edge = ids[0] == 1
    top = jnp.where(jnp.logical_and(edge, lane >= half), MASKED, 0.0).astype(F32)
    low = jnp.where(jnp.logical_and(edge, lane < half), MASKED, 0.0).astype(F32)
    inv_root = 1.0 / math.sqrt(size)
    to_exp2 = inv_root * math.log2(math.e)

    def spread(block, h):
        parts = []
        if h > 0:
            parts.append(jnp.zeros((h * size, tokens), BF16))
        parts.append(block)
        if h < per - 1:
            parts.append(jnp.zeros(((per - 1 - h) * size, tokens), BF16))
        return jnp.concatenate(parts, 0)

    def group(i, carry):
        at = pl.multiple_of(i * 128, 128)
        k4 = kv[:, pl.ds(at, 128)]
        v4 = kv[:, pl.ds(pl.multiple_of(feat + at, 128), 128)]
        for h in range(per):
            row = pl.multiple_of(at + h * size, size)
            q_h = qkv_t[pl.ds(row, size), :]
            k_h = qkv_t[pl.ds(pl.multiple_of(feat + row, size), size), :]
            v_h = qkv_t[pl.ds(pl.multiple_of(2 * feat + row, size), size), :]
            do_h = do_t[pl.ds(row, size), :]
            s = dot(k4, spread(q_h, h))
            s = jnp.concatenate([s[:half] + top, s[half:] + low], 0)
            e = jnp.exp2((s - jnp.max(s, 0, keepdims=True)) * to_exp2)
            p = e * (1.0 / jnp.sum(e, 0, keepdims=True))
            p_low = p.astype(BF16)
            dp = dot(v4, spread(do_h, h))
            delta = jnp.sum(dp * p, 0, keepdims=True)
            ds = (p * (dp - delta) * inv_root).astype(BF16)
            attn_t[pl.ds(row, size), :] = dot(v_h, p_low).astype(BF16)
            d_t[pl.ds(row, size), :] = dot(k_h, ds).astype(BF16)
            d_t[pl.ds(pl.multiple_of(feat + row, size), size), :] = dot(
                q_h, ds, ((1,), (1,))
            ).astype(BF16)
            d_t[pl.ds(pl.multiple_of(2 * feat + row, size), size), :] = dot(
                do_h, p_low, ((1,), (1,))
            ).astype(BF16)
        return carry

    lax.fori_loop(0, HEADS // per, group, 0)

    back[...] = dot(wqkv[...], d_t[...]).astype(BF16).astype(F32).T.astype(BF16)
    part_gain = jnp.sum(back[...].astype(F32) * wide[...], 0, keepdims=True)
    column = jnp.broadcast_to(part_gain, (128, feat)).T
    gain_col[...] = jnp.where(lanes(column.shape) == 0, column, 0.0)

    rows = feat // 2
    mine = pl.multiple_of(ids[1] * rows, rows)
    theirs = pl.multiple_of((1 - ids[1]) * rows, rows)
    for block in range(3):
        at = slice(block * feat, (block + 1) * feat)
        send[:, at] = dot(normed_t[pl.ds(theirs, rows), :], d_t[at, :], ((1,), (1,))).astype(BF16)
        keep[:, at] = dot(normed_t[pl.ds(mine, rows), :], d_t[at, :], ((1,), (1,)))
    at = slice(3 * feat, 4 * feat)
    send[:, at] = dot(attn_t[pl.ds(theirs, rows), :], g_low[...]).astype(BF16)
    keep[:, at] = dot(attn_t[pl.ds(mine, rows), :], g_low[...])
    send[:, 4 * feat :] = split_low(gain_col[pl.ds(theirs, rows), :], 2)
    keep[:, 4 * feat :] = gain_col[pl.ds(mine, rows), :]


def tokens_kernel(q0, q1, q2, q3, gain, wout, attn_t, back, o0, o1, o2, o3, wide):
    quads, outs = (q0, q1, q2, q3), (o0, o1, o2, o3)
    rows = q0.shape[1]
    gather_quads(quads, 0, wide)
    tok = wide[...]
    mixed = tok + dot(attn_t[...], wout[...], ((0,), (0,)))
    for j, out in enumerate(outs):
        out[0] = mixed[j * rows : (j + 1) * rows].astype(BF16)
    xhat, inv = normalise(tok)
    scaled = back[...].astype(F32) * gain[...]
    inner = (
        scaled
        - jnp.mean(scaled, -1, keepdims=True)
        - xhat * jnp.mean(scaled * xhat, -1, keepdims=True)
    )
    gather_quads(quads, 1, wide)
    grad = wide[...] + inv * inner
    for j, out in enumerate(outs):
        out[1] = grad[j * rows : (j + 1) * rows].astype(BF16)


def gain_total(tile):
    return jnp.where(lanes(tile.shape) == 0, jnp.sum(tile, -1, keepdims=True), 0.0)


def pair_kernel(keep, other, out):
    main = keep.shape[1] - 128
    out[:, :main] = (keep[:, :main] + other[:, :main].astype(F32)).astype(BF16)
    out[:, main:] = split_low(gain_total(keep[:, main:] + other[:, main:].astype(F32)), 2)


def piece_kernel(pieces, out):
    out[...] = jnp.sum(pieces[...].astype(F32), 0)


def final_piece_kernel(factor, mine, p1, p2, p3, out):
    main = mine.shape[1] - 128
    total = (mine[...] + p1[...] + p2[...] + p3[...]) * factor
    out[:, :main] = total[:, :main].astype(BF16)
    out[:, main:] = split_low(gain_total(total[:, main:]), 3)


def finish_kernel(ids, mine, theirs, grad_qkv, grad_out, gain_grad, sems):
    rows = mine.shape[0]
    wide = grad_qkv.shape[1]
    main = wide + grad_out.shape[1]
    copies = []
    for n, ref in enumerate((mine, theirs)):
        at = pl.multiple_of((ids[1] if n == 0 else 1 - ids[1]) * rows, rows)
        for m, (dst, cols) in enumerate(
            ((grad_qkv, slice(0, wide)), (grad_out, slice(wide, main)))
        ):
            copy = pltpu.make_async_copy(
                ref.at[:, cols], dst.at[pl.ds(at, rows), :], sems.at[2 * n + m]
            )
            copy.start()
            copies.append(copy)
        column = ref[:, main:].astype(F32).T
        gain_grad[:, pl.ds(at, rows)] = column[0:1] + column[1:2] + column[2:3]
    for copy in copies:
        copy.wait()


def shards(tokens, layer_norm_gain, cotangent, w_qkv, w_out):
    _, lat_rows, lon_cols, levels, feat = tokens.shape
    lat_n, lon_n = lax.axis_size(LAT), lax.axis_size(LON)
    quad_tokens = SHIFT * SHIFT * levels
    n_tokens = 4 * quad_tokens
    keep_part, go_part = slice(SHIFT, lat_rows), slice(0, SHIFT)

    def pairs(d_lat, d_lon):
        return [
            (a * lon_n + o, (a + d_lat) % lat_n * lon_n + (o + d_lon) % lon_n)
            for a in range(lat_n)
            for o in range(lon_n)
        ]

    def quad(rows, cols):
        both = jnp.stack([tokens[0, rows, cols], cotangent[0, rows, cols]])
        return both.reshape(2, quad_tokens, feat)

    shifts = ((0, 0), (0, 1), (1, 0), (1, 1))
    cuts = [(go_part if a else keep_part, go_part if o else keep_part) for a, o in shifts]
    with jax.named_scope("window_in"):
        quads = [quad(*cut) for cut in cuts]
        quads = [
            q if s == (0, 0) else lax.ppermute(q, EVERY, pairs(-s[0], -s[1]))
            for q, s in zip(quads, shifts)
        ]
    gain_row = layer_norm_gain[None, :]
    core = lax.axis_index("core")
    ids = jnp.stack([(lax.axis_index(LAT) == lat_n - 1).astype(jnp.int32), core.astype(jnp.int32)])
    vmem = pl.BlockSpec(memory_space=pltpu.VMEM)
    smem = pl.BlockSpec(memory_space=pltpu.SMEM)
    hbm = pl.BlockSpec(memory_space=pl.ANY)
    params = pltpu.CompilerParams(vmem_limit_bytes=40 * 1024 * 1024)
    rows, width = feat // 2, 4 * feat + 128
    with jax.named_scope("window_grads"):
        keep, send, attn_t, back = pl.pallas_call(
            grads_kernel,
            in_specs=[smem] + [vmem] * 8,
            out_specs=[vmem] * 4,
            out_shape=[
                jax.ShapeDtypeStruct((rows, width), F32),
                jax.ShapeDtypeStruct((rows, width), BF16),
                jax.ShapeDtypeStruct((feat, n_tokens), BF16),
                jax.ShapeDtypeStruct((n_tokens, feat), BF16),
            ],
            scratch_shapes=[
                pltpu.VMEM((n_tokens, feat), F32),
                pltpu.VMEM((n_tokens, feat), BF16),
                pltpu.VMEM((n_tokens, feat), BF16),
                pltpu.VMEM((3 * feat, n_tokens), BF16),
                pltpu.VMEM((n_tokens, 2 * feat), BF16),
                pltpu.VMEM((feat, n_tokens), BF16),
                pltpu.VMEM((3 * feat, n_tokens), BF16),
                pltpu.VMEM((feat, n_tokens), BF16),
                pltpu.VMEM((feat, 128), F32),
            ],
            compiler_params=params,
        )(ids, *quads, gain_row, w_qkv, w_qkv.T, w_out)
    swap = [(0, 1), (1, 0)]
    with jax.named_scope("sum_cores"):
        other = lax.ppermute(send, "core", swap)
    with jax.named_scope("window_tokens"):
        outs = pl.pallas_call(
            tokens_kernel,
            in_specs=[vmem] * 8,
            out_specs=[vmem] * 4,
            out_shape=[jax.ShapeDtypeStruct((2, quad_tokens, feat), BF16)] * 4,
            scratch_shapes=[pltpu.VMEM((n_tokens, feat), F32)],
            compiler_params=params,
        )(*quads, gain_row, w_out, attn_t, back)
    with jax.named_scope("sum_cores"):
        pair_sum = pl.pallas_call(
            pair_kernel,
            in_specs=[vmem] * 2,
            out_specs=vmem,
            out_shape=jax.ShapeDtypeStruct((rows, width), BF16),
            compiler_params=params,
        )(keep, other)
    pair_sum, *outs = lax.optimization_barrier((pair_sum, *outs))
    with jax.named_scope("window_out"):
        outs = [
            q if s == (0, 0) else lax.ppermute(q, EVERY, pairs(s[0], s[1]))
            for q, s in zip(outs, shifts)
        ]
    near, far = lax.axis_size(NEAR), lax.axis_size(FAR)
    factor = 1.0 / math.sqrt(lat_n * lat_rows * lon_n * lon_cols * levels)
    with jax.named_scope("sum_near"):
        pieces = lax.all_to_all(pair_sum.reshape(near, rows // near, width), NEAR, 0, 0)
        pieces, *outs = lax.optimization_barrier((pieces, *outs))
        piece = pl.pallas_call(
            piece_kernel,
            in_specs=[vmem],
            out_specs=vmem,
            out_shape=jax.ShapeDtypeStruct((rows // near, width), F32),
            compiler_params=params,
        )(pieces)
    with jax.named_scope("window_out"):
        blocks = [o.reshape(2, SHIFT, SHIFT, levels, feat) for o in outs]
        lower = jnp.concatenate([blocks[1], blocks[0]], 2)
        upper = jnp.concatenate([blocks[3], blocks[2]], 2)
        both = jnp.concatenate([upper, lower], 1)
        mixed, grad_tokens = both[0][None], both[1][None]
    with jax.named_scope("sum_far"):
        others = [
            lax.ppermute(piece, FAR, [(i, (i + by) % far) for i in range(far)])
            for by in range(1, far)
        ]
        piece = pl.pallas_call(
            functools.partial(final_piece_kernel, factor),
            in_specs=[vmem] * far,
            out_specs=vmem,
            out_shape=jax.ShapeDtypeStruct((rows // near, width), BF16),
            compiler_params=params,
        )(piece, *others)
    with jax.named_scope("share"):
        mine = lax.all_to_all(jnp.broadcast_to(piece[None], (near,) + piece.shape), NEAR, 0, 0)
        mine = mine.reshape(rows, width)
        theirs = lax.ppermute(mine, "core", swap)
    with jax.named_scope("finish"):
        grad_qkv, grad_out, gain_gradient = pl.pallas_call(
            finish_kernel,
            in_specs=[smem, vmem, vmem],
            out_specs=[hbm, hbm, vmem],
            out_shape=[
                jax.ShapeDtypeStruct((feat, 3 * feat), BF16),
                jax.ShapeDtypeStruct((feat, feat), BF16),
                jax.ShapeDtypeStruct((1, feat), F32),
            ],
            scratch_shapes=[pltpu.SemaphoreType.DMA((4,))],
            compiler_params=params,
        )(ids, mine, theirs)
    return mixed, grad_tokens, gain_gradient[0], grad_qkv, grad_out


def solution(mesh):
    fine = Mesh(mesh.devices.reshape(2, 4, 4, 2, 2, 2), EVERY)
    grid = P(None, LAT, LON, None, None)
    return jax.shard_map(
        shards,
        mesh=fine,
        in_specs=(grid, P(), grid, P(), P()),
        out_specs=(grid, grid, P(), P(), P()),
        check_vma=False,
    )
```

```python
import functools
import math

import jax
import jax.numpy as jnp
from jax import lax
from jax.experimental import pallas as pl
from jax.experimental.pallas import tpu as pltpu
from jax.sharding import Mesh
from jax.sharding import PartitionSpec as P

HEADS = 16
WIN = 12
SHIFT = 6
EPS = 1e-05
MASKED = -1e30
F32 = jnp.float32
BF16 = jnp.bfloat16

LAT = ("xh", "y")
LON = ("zh", "zl", "xl", "core")
NEAR = ("xh", "y", "zl", "xl")
FAR = "zh"
EVERY = LAT + LON


def dot(a, b, dims=((1,), (0,))):
    return lax.dot_general(a, b, (dims, ((), ())), preferred_element_type=F32)


def normalise(tok):
    mean = jnp.mean(tok, -1, keepdims=True)
    centred = tok - mean
    inv = lax.rsqrt(jnp.mean(centred * centred, -1, keepdims=True) + EPS)
    return centred * inv, inv


def gather_quads(refs, which, out):
    rows = refs[0].shape[1]
    for j, ref in enumerate(refs):
        out[j * rows : (j + 1) * rows, :] = ref[which].astype(F32)


def lanes(shape):
    return lax.broadcasted_iota(jnp.int32, shape, len(shape) - 1)


def split_low(value, terms):
    lane = lanes(value.shape)
    out = jnp.zeros_like(value)
    rest = value
    for i in range(terms):
        part = rest.astype(BF16).astype(F32)
        out = jnp.where(lane == i, part, out)
        rest = rest - part
    return out.astype(BF16)


def weights_kernel(wqkv, wout, wqkv_t, wout_near):
    wqkv_t[...] = wqkv[...].T
    wout_near[...] = wout[...]


def grads_kernel(
    ids, q0, q1, q2, q3, gain, wqkv, wqkv_t, wout,
    keep, send, attn_t, back,
    wide, normed, normed_t, g_low, q_t, kv_t, kv, do_t, dq_t, dkv_t, gain_col,
    diag, side, bias, scores, d_probs, p_low, d_low, acc,
):
    quads = (q0, q1, q2, q3)
    tokens, feat = wide.shape
    main = tokens // 128 * 128
    left = tokens - main
    ext = normed.shape[0]
    size = feat // HEADS
    per = 128 // size
    half = tokens // 2
    inv_root = 1.0 / math.sqrt(size)
    to_exp2 = inv_root * math.log2(math.e)

    def repeat_left(ref):
        for j in range(1, per):
            ref[tokens + (j - 1) * left : tokens + j * left, :] = ref[main:tokens, :]

    gather_quads(quads, 1, wide)
    g_low[:tokens, :] = wide[...].astype(BF16)
    repeat_left(g_low)
    do_t[...] = dot(wout[...], g_low[...], ((1,), (1,))).astype(BF16)
    gather_quads(quads, 0, wide)
    xhat, _ = normalise(wide[...])
    wide[...] = xhat
    normed[:tokens, :] = (xhat * gain[...]).astype(BF16)
    repeat_left(normed)
    q_t[...] = dot(wqkv_t[:feat, :], normed[...], ((1,), (1,))).astype(BF16)
    kv_t[...] = dot(wqkv_t[feat:, :], normed[:tokens, :], ((1,), (1,))).astype(BF16)
    kv[...] = dot(normed[:tokens, :], wqkv[:, feat:]).astype(BF16)
    normed_t[...] = normed[...].T

    row_head = lax.broadcasted_iota(jnp.int32, (128, 128), 0) // size
    diag[...] = jnp.where(row_head == lanes((128, 128)) // left, 1.0, 0.0).astype(BF16)
    late_key = lax.broadcasted_iota(jnp.int32, (tokens, 128), 0) >= half
    lane = lanes((tokens, 128))
    side[...] = jnp.where(
        jnp.logical_or(
            jnp.logical_and(lane == 0, late_key),
            jnp.logical_and(lane == 1, jnp.logical_not(late_key)),
        ),
        1.0,
        0.0,
    ).astype(BF16)
    which = lax.broadcasted_iota(jnp.int32, (128, ext), 0)
    late_query = lanes((128, ext)) >= half
    blocked = jnp.logical_or(
        jnp.logical_and(which == 0, jnp.logical_not(late_query)),
        jnp.logical_and(which == 1, late_query),
    )
    bias[...] = jnp.where(jnp.logical_and(blocked, ids[0] == 1), MASKED, 0.0).astype(BF16)

    def spread(block, h):
        parts = []
        if h > 0:
            parts.append(jnp.zeros((h * size, block.shape[1]), BF16))
        parts.append(block)
        if h < per - 1:
            parts.append(jnp.zeros(((per - 1 - h) * size, block.shape[1]), BF16))
        return jnp.concatenate(parts, 0)

    def operand(ref, g, h):
        rows = slice(128 * g, 128 * (g + 1))
        if h is None:
            return ref[rows, main:ext] * diag[...]
        return spread(ref[128 * g + size * h : 128 * g + size * (h + 1), :main], h)

    def score(slot, g, h):
        cols = slice(128 * g, 128 * (g + 1))
        at, width = (slice(main, ext), ext - main) if h is None else (slice(0, main), main)
        keys = jnp.concatenate([kv[:, cols], side[...]], 1)
        queries = jnp.concatenate([operand(q_t, g, h), bias[:, at]], 0)
        scores[slot, :, :width] = dot(keys, queries)
        values = kv[:, feat + 128 * g : feat + 128 * (g + 1)]
        d_probs[slot, :, :width] = dot(values, operand(do_t, g, h))

    step = 32

    def soften(slot, h):
        width = ext - main if h is None else main
        chunks = [slice(c, c + step) for c in range(0, tokens, step)]

        def fold(value, op):
            return op(value.reshape(step // 8, 8, width), axis=0)

        top = None
        for c in chunks:
            part = fold(scores[slot, c, :width], jnp.max)
            top = part if top is None else jnp.maximum(top, part)
        top = jnp.max(top, 0, keepdims=True)
        total = jnp.zeros((8, width), F32)
        for c in chunks:
            e = jnp.exp2((scores[slot, c, :width] - top) * to_exp2)
            scores[slot, c, :width] = e
            total = total + fold(e, jnp.sum)
        scale = 1.0 / jnp.sum(total, 0, keepdims=True)
        delta = jnp.zeros((8, width), F32)
        for c in chunks:
            p = scores[slot, c, :width] * scale
            p_low[slot, c, :width] = p.astype(BF16)
            delta = delta + fold(d_probs[slot, c, :width] * p, jnp.sum)
        delta = jnp.sum(delta, 0, keepdims=True)
        scale = scale * inv_root
        for c in chunks:
            p = scores[slot, c, :width] * scale
            d_low[slot, c, :width] = (p * (d_probs[slot, c, :width] - delta)).astype(BF16)

    def collect(slot, g, h):
        nt = ((1,), (1,))
        if h is None:
            rows = slice(128 * g, 128 * (g + 1))
            later = slice(feat + 128 * g, feat + 128 * (g + 1))
            width = ext - main
            keep_own = diag[...].astype(F32)
            p, d = p_low[slot, :, :width], d_low[slot, :, :width]
            attn_t[rows, main:ext] = (dot(kv_t[later, :], p) * keep_own).astype(BF16)
            dq_t[rows, main:ext] = (dot(kv_t[rows, :], d) * keep_own).astype(BF16)
            acc[0] = dot(operand(q_t, g, h), d, nt)
            acc[1] = dot(operand(do_t, g, h), p, nt)
            return
        rows = slice(128 * g + size * h, 128 * g + size * (h + 1))
        later = slice(feat + rows.start, feat + rows.stop)
        own = slice(size * h, size * (h + 1))
        p, d = p_low[slot], d_low[slot]
        attn_t[rows, :main] = dot(kv_t[later, :], p).astype(BF16)
        dq_t[rows, :main] = dot(kv_t[rows, :], d).astype(BF16)
        dkv_t[rows, :] = (dot(q_t[rows, :main], d, nt) + acc[0, own, :]).astype(BF16)
        dkv_t[later, :] = (dot(do_t[rows, :main], p, nt) + acc[1, own, :]).astype(BF16)

    blocks = [(g, h) for g in range(HEADS // per) for h in (None, *range(per))]
    score(0, *blocks[0])
    for n, (g, h) in enumerate(blocks):
        if n + 1 < len(blocks):
            score((n + 1) % 2, *blocks[n + 1])
        soften(n % 2, h)
        if n > 0:
            collect((n - 1) % 2, *blocks[n - 1])
    collect((len(blocks) - 1) % 2, *blocks[-1])

    from_q = dot(wqkv[:, :feat], dq_t[...])
    from_kv = dot(wqkv[:, feat:], dkv_t[...])
    back[:main, :] = (from_q[:, :main] + from_kv[:, :main]).T.astype(BF16)
    rest = from_q[:, main:].T
    last = from_kv[:, main:].T
    for j in range(per):
        last = last + rest[j * left : (j + 1) * left]
    back[main:, :] = last.astype(BF16)
    part_gain = jnp.sum(back[...].astype(F32) * wide[...], 0, keepdims=True)
    column = jnp.broadcast_to(part_gain, (128, feat)).T
    gain_col[...] = jnp.where(lanes(column.shape) < 2, column, 0.0)

    rows = feat // 2
    mine = pl.multiple_of(ids[1] * rows, rows)
    theirs = pl.multiple_of((1 - ids[1]) * rows, rows)

    def partial_sums(start):
        pick = pl.ds(start, rows)
        return (
            dot(normed_t[pick, :], dq_t[...], ((1,), (1,))),
            dot(normed_t[pick, :tokens], dkv_t[:feat, :], ((1,), (1,))),
            dot(normed_t[pick, :tokens], dkv_t[feat:, :], ((1,), (1,))),
            dot(attn_t[pick, :], g_low[...]),
        )

    for block, value in enumerate(partial_sums(theirs)):
        send[:, block * feat : (block + 1) * feat] = value.astype(BF16)
    for block, value in enumerate(partial_sums(mine)):
        keep[:, block * feat : (block + 1) * feat] = value
    send[:, 4 * feat :] = gain_col[pl.ds(theirs, rows), :].astype(BF16)
    keep[:, 4 * feat :] = gain_col[pl.ds(mine, rows), :]


def grads_scratch(tokens, feat):
    ext = tokens // 128 * 128 + 128
    return [
        pltpu.VMEM((tokens, feat), F32),
        pltpu.VMEM((ext, feat), BF16),
        pltpu.VMEM((feat, ext), BF16),
        pltpu.VMEM((ext, feat), BF16),
        pltpu.VMEM((feat, ext), BF16),
        pltpu.VMEM((2 * feat, tokens), BF16),
        pltpu.VMEM((tokens, 2 * feat), BF16),
        pltpu.VMEM((feat, ext), BF16),
        pltpu.VMEM((feat, ext), BF16),
        pltpu.VMEM((2 * feat, tokens), BF16),
        pltpu.VMEM((feat, 128), F32),
        pltpu.VMEM((128, 128), BF16),
        pltpu.VMEM((tokens, 128), BF16),
        pltpu.VMEM((128, ext), BF16),
        pltpu.VMEM((2, tokens, 256), F32),
        pltpu.VMEM((2, tokens, 256), F32),
        pltpu.VMEM((2, tokens, 256), BF16),
        pltpu.VMEM((2, tokens, 256), BF16),
        pltpu.VMEM((2, 128, tokens), F32),
    ]


def tokens_kernel(q0, q1, q2, q3, gain, wout, attn_t, back, o0, o1, o2, o3, wide):
    quads, outs = (q0, q1, q2, q3), (o0, o1, o2, o3)
    rows = q0.shape[1]
    gather_quads(quads, 0, wide)
    tok = wide[...]
    main = tok.shape[0] // 128 * 128
    left = tok.shape[0] - main
    added = dot(attn_t[...], wout[...], ((0,), (0,)))
    last = added[main : main + left]
    for at in range(main + left, added.shape[0], left):
        last = last + added[at : at + left]
    mixed = tok + jnp.concatenate([added[:main], last], 0)
    for j, out in enumerate(outs):
        out[0] = mixed[j * rows : (j + 1) * rows].astype(BF16)
    xhat, inv = normalise(tok)
    scaled = back[...].astype(F32) * gain[...]
    inner = (
        scaled
        - jnp.mean(scaled, -1, keepdims=True)
        - xhat * jnp.mean(scaled * xhat, -1, keepdims=True)
    )
    gather_quads(quads, 1, wide)
    grad = wide[...] + inv * inner
    for j, out in enumerate(outs):
        out[1] = grad[j * rows : (j + 1) * rows].astype(BF16)


def gain_total(tile):
    return jnp.where(lanes(tile.shape) == 0, jnp.sum(tile, -1, keepdims=True), 0.0)


def add_pair(keep, other):
    total = keep + other.astype(F32)
    rest = total - lax.reduce_precision(total, 8, 7)
    return jnp.where(lanes(total.shape) == total.shape[1] - 127, rest, total).astype(BF16)


def final_piece_kernel(factor, parts, _, out):
    main = parts.shape[2] - 128
    total = jnp.sum(parts[...], 0) * factor
    out[:, :main] = total[:, :main].astype(BF16)
    out[:, main:] = split_low(gain_total(total[:, main:]), 3)


def finish_kernel(ids, mine, theirs, grad_qkv, grad_out, gain_grad, tails, sems):
    rows = mine.shape[0]
    wide = grad_qkv.shape[1]
    main = wide + grad_out.shape[1]
    copies = []
    for n, half in enumerate((mine, theirs)):
        at = pl.multiple_of((ids[1] if n == 0 else 1 - ids[1]) * rows, rows)
        for m, (src, dst) in enumerate(
            (
                (half.at[:, main:], tails.at[n]),
                (half.at[:, :wide], grad_qkv.at[pl.ds(at, rows), :]),
                (half.at[:, wide:main], grad_out.at[pl.ds(at, rows), :]),
            )
        ):
            copy = pltpu.make_async_copy(src, dst, sems.at[3 * n + m])
            copy.start()
            copies.append((m, copy))
    for m, copy in copies:
        if m == 0:
            copy.wait()
    for n in range(2):
        at = pl.multiple_of((ids[1] if n == 0 else 1 - ids[1]) * rows, rows)
        column = tails[n].astype(F32).T
        gain_grad[:, pl.ds(at, rows)] = column[0:1] + column[1:2] + column[2:3]
    for m, copy in copies:
        if m > 0:
            copy.wait()


def shards(tokens, layer_norm_gain, cotangent, w_qkv, w_out):
    _, lat_rows, lon_cols, levels, feat = tokens.shape
    lat_n, lon_n = lax.axis_size(LAT), lax.axis_size(LON)
    quad_tokens = SHIFT * SHIFT * levels
    n_tokens = 4 * quad_tokens
    keep_part, go_part = slice(SHIFT, lat_rows), slice(0, SHIFT)

    def pairs(d_lat, d_lon):
        return [
            (a * lon_n + o, (a + d_lat) % lat_n * lon_n + (o + d_lon) % lon_n)
            for a in range(lat_n)
            for o in range(lon_n)
        ]

    def quad(rows, cols):
        both = jnp.stack([tokens[0, rows, cols], cotangent[0, rows, cols]])
        return both.reshape(2, quad_tokens, feat)

    shifts = ((0, 0), (0, 1), (1, 0), (1, 1))
    cuts = [(go_part if a else keep_part, go_part if o else keep_part) for a, o in shifts]
    with jax.named_scope("window_in"):
        quads = [quad(*cut) for cut in cuts]
        quads = [
            q if s == (0, 0) else lax.ppermute(q, EVERY, pairs(-s[0], -s[1]))
            for q, s in zip(quads, shifts)
        ]
    gain_row = layer_norm_gain[None, :]
    core = lax.axis_index("core")
    ids = jnp.stack([(lax.axis_index(LAT) == lat_n - 1).astype(jnp.int32), core.astype(jnp.int32)])
    vmem = pl.BlockSpec(memory_space=pltpu.VMEM)
    smem = pl.BlockSpec(memory_space=pltpu.SMEM)
    hbm = pl.BlockSpec(memory_space=pl.ANY)
    params = pltpu.CompilerParams(vmem_limit_bytes=40 * 1024 * 1024)
    rows, width = feat // 2, 4 * feat + 128
    with jax.named_scope("weights"):
        w_qkv_t, w_out_near = pl.pallas_call(
            weights_kernel,
            in_specs=[vmem] * 2,
            out_specs=[vmem] * 2,
            out_shape=[
                jax.ShapeDtypeStruct((3 * feat, feat), BF16),
                jax.ShapeDtypeStruct((feat, feat), BF16),
            ],
            compiler_params=params,
        )(w_qkv, w_out)
    with jax.named_scope("window_grads"):
        keep, send, attn_t, back = pl.pallas_call(
            grads_kernel,
            in_specs=[smem] + [vmem] * 8,
            out_specs=[vmem] * 4,
            out_shape=[
                jax.ShapeDtypeStruct((rows, width), F32),
                jax.ShapeDtypeStruct((rows, width), BF16),
                jax.ShapeDtypeStruct((feat, n_tokens // 128 * 128 + 128), BF16),
                jax.ShapeDtypeStruct((n_tokens, feat), BF16),
            ],
            scratch_shapes=grads_scratch(n_tokens, feat),
            compiler_params=params,
        )(ids, *quads, gain_row, w_qkv, w_qkv_t, w_out_near)
    swap = [(0, 1), (1, 0)]
    with jax.named_scope("sum_cores"):
        other = lax.ppermute(send, "core", swap)
    with jax.named_scope("window_tokens"):
        outs = pl.pallas_call(
            tokens_kernel,
            in_specs=[vmem] * 8,
            out_specs=[vmem] * 4,
            out_shape=[jax.ShapeDtypeStruct((2, quad_tokens, feat), BF16)] * 4,
            scratch_shapes=[pltpu.VMEM((n_tokens, feat), F32)],
            compiler_params=params,
        )(*quads, gain_row, w_out, attn_t, back)
    with jax.named_scope("sum_cores"):
        pair_sum = add_pair(keep, other)
    near, far = lax.axis_size(NEAR), lax.axis_size(FAR)
    factor = 1.0 / math.sqrt(lat_n * lat_rows * lon_n * lon_cols * levels)
    chunk = rows // near
    with jax.named_scope("sum_near"):
        pieces = lax.all_to_all(pair_sum.reshape(near, chunk, width), NEAR, 0, 0)
        piece = jnp.sum(pieces.astype(F32), 0)
        piece = jnp.broadcast_to(piece[None], (far, chunk, width))
    after, *outs = lax.optimization_barrier((piece, *outs))
    with jax.named_scope("sum_far"):
        parts = lax.all_to_all(piece, FAR, 0, 0)
    with jax.named_scope("window_out"):
        outs = [
            q if s == (0, 0) else lax.ppermute(q, EVERY, pairs(s[0], s[1]))
            for q, s in zip(outs, shifts)
        ]
    with jax.named_scope("sum_far"):
        piece = pl.pallas_call(
            functools.partial(final_piece_kernel, factor),
            in_specs=[vmem, hbm],
            out_specs=vmem,
            out_shape=jax.ShapeDtypeStruct((chunk, width), BF16),
            compiler_params=params,
        )(parts, after)
    piece, *outs = lax.optimization_barrier((piece, *outs))
    with jax.named_scope("share"):
        mine = lax.all_to_all(jnp.broadcast_to(piece[None], (near,) + piece.shape), NEAR, 0, 0)
        mine = mine.reshape(rows, width)
        theirs = lax.ppermute(mine, "core", swap)
    outs = lax.optimization_barrier((mine, *outs))[1:]
    with jax.named_scope("window_out"):
        blocks = [o.reshape(2, SHIFT, SHIFT, levels, feat) for o in outs]
        lower = jnp.concatenate([blocks[1], blocks[0]], 2)
        upper = jnp.concatenate([blocks[3], blocks[2]], 2)
        both = jnp.concatenate([upper, lower], 1)
        mixed, grad_tokens = both[0][None], both[1][None]
    final = [
        jax.ShapeDtypeStruct((feat, 3 * feat), BF16),
        jax.ShapeDtypeStruct((feat, feat), BF16),
        jax.ShapeDtypeStruct((1, feat), F32),
    ]
    with jax.named_scope("finish"):
        grad_qkv, grad_out, gain_gradient = pl.pallas_call(
            finish_kernel,
            in_specs=[smem, hbm, hbm],
            out_specs=[hbm, hbm, vmem],
            out_shape=final,
            scratch_shapes=[pltpu.VMEM((2, rows, 128), BF16), pltpu.SemaphoreType.DMA((6,))],
            compiler_params=params,
        )(ids, mine, theirs)
    return mixed, grad_tokens, gain_gradient[0], grad_qkv, grad_out


def solution(mesh):
    fine = Mesh(mesh.devices.reshape(2, 4, 4, 2, 2, 2), EVERY)
    grid = P(None, LAT, LON, None, None)
    return jax.shard_map(
        shards,
        mesh=fine,
        in_specs=(grid, P(), grid, P(), P()),
        out_specs=(grid, grid, P(), P(), P()),
        check_vma=False,
    )
```

```python
import functools
import math

import jax
import jax.numpy as jnp
from jax import lax
from jax.experimental import pallas as pl
from jax.experimental.pallas import tpu as pltpu
from jax.sharding import Mesh
from jax.sharding import PartitionSpec as P

HEADS = 16
WIN = 12
SHIFT = 6
EPS = 1e-05
MASKED = -1e30
F32 = jnp.float32
BF16 = jnp.bfloat16

LAT = ("xh", "y")
LON = ("zh", "zl", "xl", "core")
NEAR = ("xh", "y", "zl", "xl")
FAR = "zh"
EVERY = LAT + LON


def dot(a, b, dims=((1,), (0,))):
    return lax.dot_general(a, b, (dims, ((), ())), preferred_element_type=F32)


def normalise(tok):
    mean = jnp.mean(tok, -1, keepdims=True)
    centred = tok - mean
    inv = lax.rsqrt(jnp.mean(centred * centred, -1, keepdims=True) + EPS)
    return centred * inv, inv


def gather_quads(refs, which, out):
    rows = refs[0].shape[1]
    for j, ref in enumerate(refs):
        out[j * rows : (j + 1) * rows, :] = ref[which].astype(F32)


def lanes(shape):
    return lax.broadcasted_iota(jnp.int32, shape, len(shape) - 1)


def split_low(value, terms):
    lane = lanes(value.shape)
    out = jnp.zeros_like(value)
    rest = value
    for i in range(terms):
        part = rest.astype(BF16).astype(F32)
        out = jnp.where(lane == i, part, out)
        rest = rest - part
    return out.astype(BF16)


def weights_kernel(wqkv, wout, wqkv_t, wout_near):
    wqkv_t[...] = wqkv[...].T
    wout_near[...] = wout[...]


def grads_kernel(
    q0, q1, q2, q3, gain, wqkv, wqkv_t, wout,
    keep, send, attn_t, back,
    wide, normed, normed_t, g_low, q_t, kv_t, kv, do_t, dq_t, dkv_t, gain_col,
    diag, side, bias, scores, d_probs, p_low, d_low, acc,
):
    quads = (q0, q1, q2, q3)
    tokens, feat = wide.shape
    main = tokens // 128 * 128
    left = tokens - main
    ext = normed.shape[0]
    size = feat // HEADS
    per = 128 // size
    half = tokens // 2
    edge = lax.axis_index(LAT) == lax.axis_size(LAT) - 1
    core = lax.axis_index("core")
    inv_root = 1.0 / math.sqrt(size)
    to_exp2 = inv_root * math.log2(math.e)

    def repeat_left(ref):
        for j in range(1, per):
            ref[tokens + (j - 1) * left : tokens + j * left, :] = ref[main:tokens, :]

    gather_quads(quads, 1, wide)
    g_low[:tokens, :] = wide[...].astype(BF16)
    repeat_left(g_low)
    do_t[...] = dot(wout[...], g_low[...], ((1,), (1,))).astype(BF16)
    gather_quads(quads, 0, wide)
    xhat, _ = normalise(wide[...])
    wide[...] = xhat
    normed[:tokens, :] = (xhat * gain[...]).astype(BF16)
    repeat_left(normed)
    q_t[...] = dot(wqkv_t[:feat, :], normed[...], ((1,), (1,))).astype(BF16)
    kv_t[...] = dot(wqkv_t[feat:, :], normed[:tokens, :], ((1,), (1,))).astype(BF16)
    kv[...] = dot(normed[:tokens, :], wqkv[:, feat:]).astype(BF16)
    normed_t[...] = normed[...].T

    row_head = lax.broadcasted_iota(jnp.int32, (128, 128), 0) // size
    diag[...] = jnp.where(row_head == lanes((128, 128)) // left, 1.0, 0.0).astype(BF16)
    late_key = lax.broadcasted_iota(jnp.int32, (tokens, 128), 0) >= half
    lane = lanes((tokens, 128))
    side[...] = jnp.where(
        jnp.logical_or(
            jnp.logical_and(lane == 0, late_key),
            jnp.logical_and(lane == 1, jnp.logical_not(late_key)),
        ),
        1.0,
        0.0,
    ).astype(BF16)
    which = lax.broadcasted_iota(jnp.int32, (128, ext), 0)
    late_query = lanes((128, ext)) >= half
    blocked = jnp.logical_or(
        jnp.logical_and(which == 0, jnp.logical_not(late_query)),
        jnp.logical_and(which == 1, late_query),
    )
    bias[...] = jnp.where(jnp.logical_and(blocked, edge), MASKED, 0.0).astype(BF16)

    def spread(block, h):
        parts = []
        if h > 0:
            parts.append(jnp.zeros((h * size, block.shape[1]), BF16))
        parts.append(block)
        if h < per - 1:
            parts.append(jnp.zeros(((per - 1 - h) * size, block.shape[1]), BF16))
        return jnp.concatenate(parts, 0)

    def operand(ref, g, h):
        rows = slice(128 * g, 128 * (g + 1))
        if h is None:
            return ref[rows, main:ext] * diag[...]
        return spread(ref[128 * g + size * h : 128 * g + size * (h + 1), :main], h)

    def score(slot, g, h):
        cols = slice(128 * g, 128 * (g + 1))
        at, width = (slice(main, ext), ext - main) if h is None else (slice(0, main), main)
        keys = jnp.concatenate([kv[:, cols], side[...]], 1)
        queries = jnp.concatenate([operand(q_t, g, h), bias[:, at]], 0)
        scores[slot, :, :width] = dot(keys, queries)
        values = kv[:, feat + 128 * g : feat + 128 * (g + 1)]
        d_probs[slot, :, :width] = dot(values, operand(do_t, g, h))

    step = 32

    def soften(slot, h):
        width = ext - main if h is None else main
        chunks = [slice(c, c + step) for c in range(0, tokens, step)]

        def fold(value, op):
            return op(value.reshape(step // 8, 8, width), axis=0)

        top = None
        for c in chunks:
            part = fold(scores[slot, c, :width], jnp.max)
            top = part if top is None else jnp.maximum(top, part)
        top = jnp.max(top, 0, keepdims=True)
        total = jnp.zeros((8, width), F32)
        for c in chunks:
            e = jnp.exp2((scores[slot, c, :width] - top) * to_exp2)
            scores[slot, c, :width] = e
            total = total + fold(e, jnp.sum)
        scale = 1.0 / jnp.sum(total, 0, keepdims=True)
        delta = jnp.zeros((8, width), F32)
        for c in chunks:
            p = scores[slot, c, :width] * scale
            p_low[slot, c, :width] = p.astype(BF16)
            delta = delta + fold(d_probs[slot, c, :width] * p, jnp.sum)
        delta = jnp.sum(delta, 0, keepdims=True)
        scale = scale * inv_root
        for c in chunks:
            p = scores[slot, c, :width] * scale
            d_low[slot, c, :width] = (p * (d_probs[slot, c, :width] - delta)).astype(BF16)

    def collect(slot, g, h):
        nt = ((1,), (1,))
        if h is None:
            rows = slice(128 * g, 128 * (g + 1))
            later = slice(feat + 128 * g, feat + 128 * (g + 1))
            width = ext - main
            keep_own = diag[...].astype(F32)
            p, d = p_low[slot, :, :width], d_low[slot, :, :width]
            attn_t[rows, main:ext] = (dot(kv_t[later, :], p) * keep_own).astype(BF16)
            dq_t[rows, main:ext] = (dot(kv_t[rows, :], d) * keep_own).astype(BF16)
            acc[0] = dot(operand(q_t, g, h), d, nt)
            acc[1] = dot(operand(do_t, g, h), p, nt)
            return
        rows = slice(128 * g + size * h, 128 * g + size * (h + 1))
        later = slice(feat + rows.start, feat + rows.stop)
        own = slice(size * h, size * (h + 1))
        p, d = p_low[slot], d_low[slot]
        attn_t[rows, :main] = dot(kv_t[later, :], p).astype(BF16)
        dq_t[rows, :main] = dot(kv_t[rows, :], d).astype(BF16)
        dkv_t[rows, :] = (dot(q_t[rows, :main], d, nt) + acc[0, own, :]).astype(BF16)
        dkv_t[later, :] = (dot(do_t[rows, :main], p, nt) + acc[1, own, :]).astype(BF16)

    blocks = [(g, h) for g in range(HEADS // per) for h in (None, *range(per))]
    score(0, *blocks[0])
    for n, (g, h) in enumerate(blocks):
        if n + 1 < len(blocks):
            score((n + 1) % 2, *blocks[n + 1])
        soften(n % 2, h)
        if n > 0:
            collect((n - 1) % 2, *blocks[n - 1])
    collect((len(blocks) - 1) % 2, *blocks[-1])

    from_q = dot(wqkv[:, :feat], dq_t[...])
    from_kv = dot(wqkv[:, feat:], dkv_t[...])
    back[:main, :] = (from_q[:, :main] + from_kv[:, :main]).T.astype(BF16)
    rest = from_q[:, main:].T
    last = from_kv[:, main:].T
    for j in range(per):
        last = last + rest[j * left : (j + 1) * left]
    back[main:, :] = last.astype(BF16)
    part_gain = jnp.sum(back[...].astype(F32) * wide[...], 0, keepdims=True)
    column = jnp.broadcast_to(part_gain, (128, feat)).T
    gain_col[...] = jnp.where(lanes(column.shape) < 2, column, 0.0)

    rows = feat // 2
    mine = pl.multiple_of(core * rows, rows)
    theirs = pl.multiple_of((1 - core) * rows, rows)

    def partial_sums(start):
        pick = pl.ds(start, rows)
        return (
            dot(normed_t[pick, :], dq_t[...], ((1,), (1,))),
            dot(normed_t[pick, :tokens], dkv_t[:feat, :], ((1,), (1,))),
            dot(normed_t[pick, :tokens], dkv_t[feat:, :], ((1,), (1,))),
            dot(attn_t[pick, :], g_low[...]),
        )

    for block, value in enumerate(partial_sums(theirs)):
        send[:, block * feat : (block + 1) * feat] = value.astype(BF16)
    for block, value in enumerate(partial_sums(mine)):
        keep[:, block * feat : (block + 1) * feat] = value
    send[:, 4 * feat :] = gain_col[pl.ds(theirs, rows), :].astype(BF16)
    keep[:, 4 * feat :] = gain_col[pl.ds(mine, rows), :]


def grads_scratch(tokens, feat):
    ext = tokens // 128 * 128 + 128
    return [
        pltpu.VMEM((tokens, feat), F32),
        pltpu.VMEM((ext, feat), BF16),
        pltpu.VMEM((feat, ext), BF16),
        pltpu.VMEM((ext, feat), BF16),
        pltpu.VMEM((feat, ext), BF16),
        pltpu.VMEM((2 * feat, tokens), BF16),
        pltpu.VMEM((tokens, 2 * feat), BF16),
        pltpu.VMEM((feat, ext), BF16),
        pltpu.VMEM((feat, ext), BF16),
        pltpu.VMEM((2 * feat, tokens), BF16),
        pltpu.VMEM((feat, 128), F32),
        pltpu.VMEM((128, 128), BF16),
        pltpu.VMEM((tokens, 128), BF16),
        pltpu.VMEM((128, ext), BF16),
        pltpu.VMEM((2, tokens, 256), F32),
        pltpu.VMEM((2, tokens, 256), F32),
        pltpu.VMEM((2, tokens, 256), BF16),
        pltpu.VMEM((2, tokens, 256), BF16),
        pltpu.VMEM((2, 128, tokens), F32),
    ]


def tokens_kernel(q0, q1, q2, q3, gain, wout, attn_t, back, o0, o1, o2, o3, wide):
    quads, outs = (q0, q1, q2, q3), (o0, o1, o2, o3)
    rows = q0.shape[1]
    gather_quads(quads, 0, wide)
    tok = wide[...]
    main = tok.shape[0] // 128 * 128
    left = tok.shape[0] - main
    added = dot(attn_t[...], wout[...], ((0,), (0,)))
    last = added[main : main + left]
    for at in range(main + left, added.shape[0], left):
        last = last + added[at : at + left]
    mixed = tok + jnp.concatenate([added[:main], last], 0)
    for j, out in enumerate(outs):
        out[0] = mixed[j * rows : (j + 1) * rows].astype(BF16).reshape(out.shape[1:])
    xhat, inv = normalise(tok)
    scaled = back[...].astype(F32) * gain[...]
    inner = (
        scaled
        - jnp.mean(scaled, -1, keepdims=True)
        - xhat * jnp.mean(scaled * xhat, -1, keepdims=True)
    )
    gather_quads(quads, 1, wide)
    grad = wide[...] + inv * inner
    for j, out in enumerate(outs):
        out[1] = grad[j * rows : (j + 1) * rows].astype(BF16).reshape(out.shape[1:])


def gain_total(tile):
    return jnp.where(lanes(tile.shape) == 0, jnp.sum(tile, -1, keepdims=True), 0.0)


def pair_kernel(keep, other, out):
    main = keep.shape[1] - 128
    for at in range(0, keep.shape[0], 16):
        rows = slice(at, at + 16)
        out[rows, :main] = (keep[rows, :main] + other[rows, :main].astype(F32)).astype(BF16)
        total = keep[rows, main:] + other[rows, main:].astype(F32)
        rest = total - total.astype(BF16).astype(F32)
        out[rows, main:] = jnp.where(lanes(total.shape) == 1, rest, total).astype(BF16)


def final_piece_kernel(factor, parts, out):
    main = parts.shape[2] - 128
    total = jnp.sum(parts[...], 0) * factor
    out[:, :main] = total[:, :main].astype(BF16)
    out[:, main:] = split_low(gain_total(total[:, main:]), 3)


def finish_kernel(
    mine, theirs, o0, o1, o2, o3, mixed, grad_tokens, grad_qkv, grad_out, gain_grad, gains, sems
):
    rows = mine.shape[0]
    wide = grad_qkv.shape[1]
    main = wide + grad_out.shape[1]
    core = lax.axis_index("core")
    copies = []

    def copy(src, dst):
        item = pltpu.make_async_copy(src, dst, sems.at[len(copies)])
        item.start()
        copies.append(item)

    for n, half in enumerate((mine, theirs)):
        at = pl.multiple_of((core if n == 0 else 1 - core) * rows, rows)
        copy(half.at[:, :wide], grad_qkv.at[pl.ds(at, rows), :])
        copy(half.at[:, wide:main], grad_out.at[pl.ds(at, rows), :])
        column = half[:, main:].astype(F32).T
        gains[:, pl.ds(at, rows)] = column[0:1] + column[1:2] + column[2:3]
    copy(gains, gain_grad)
    for n, quad in enumerate((o0, o1, o2, o3)):
        lat = slice(0, SHIFT) if n // 2 else slice(SHIFT, 2 * SHIFT)
        lon = slice(0, SHIFT) if n % 2 else slice(SHIFT, 2 * SHIFT)
        copy(quad.at[0], mixed.at[0, lat, lon])
        copy(quad.at[1], grad_tokens.at[0, lat, lon])
    for item in copies:
        item.wait()


def shards(tokens, layer_norm_gain, cotangent, w_qkv, w_out):
    _, lat_rows, lon_cols, levels, feat = tokens.shape
    lat_n, lon_n = lax.axis_size(LAT), lax.axis_size(LON)
    quad_tokens = SHIFT * SHIFT * levels
    n_tokens = 4 * quad_tokens
    keep_part, go_part = slice(SHIFT, lat_rows), slice(0, SHIFT)

    def pairs(d_lat, d_lon):
        return [
            (a * lon_n + o, (a + d_lat) % lat_n * lon_n + (o + d_lon) % lon_n)
            for a in range(lat_n)
            for o in range(lon_n)
        ]

    def quad(rows, cols):
        both = jnp.stack([tokens[0, rows, cols], cotangent[0, rows, cols]])
        return both.reshape(2, quad_tokens, feat)

    shifts = ((0, 0), (0, 1), (1, 0), (1, 1))
    cuts = [(go_part if a else keep_part, go_part if o else keep_part) for a, o in shifts]
    with jax.named_scope("window_in"):
        quads = [quad(*cut) for cut in cuts]
        quads = [
            q if s == (0, 0) else lax.ppermute(q, EVERY, pairs(-s[0], -s[1]))
            for q, s in zip(quads, shifts)
        ]
    gain_row = layer_norm_gain[None, :]
    vmem = pl.BlockSpec(memory_space=pltpu.VMEM)
    hbm = pl.BlockSpec(memory_space=pl.ANY)
    params = pltpu.CompilerParams(vmem_limit_bytes=40 * 1024 * 1024)
    rows, width = feat // 2, 4 * feat + 128
    with jax.named_scope("weights"):
        w_qkv_t, w_out_near = pl.pallas_call(
            weights_kernel,
            in_specs=[vmem] * 2,
            out_specs=[vmem] * 2,
            out_shape=[
                jax.ShapeDtypeStruct((3 * feat, feat), BF16),
                jax.ShapeDtypeStruct((feat, feat), BF16),
            ],
            compiler_params=params,
        )(w_qkv, w_out)
    with jax.named_scope("window_grads"):
        keep, send, attn_t, back = pl.pallas_call(
            grads_kernel,
            in_specs=[vmem] * 8,
            out_specs=[vmem] * 4,
            out_shape=[
                jax.ShapeDtypeStruct((rows, width), F32),
                jax.ShapeDtypeStruct((rows, width), BF16),
                jax.ShapeDtypeStruct((feat, n_tokens // 128 * 128 + 128), BF16),
                jax.ShapeDtypeStruct((n_tokens, feat), BF16),
            ],
            scratch_shapes=grads_scratch(n_tokens, feat),
            compiler_params=params,
        )(*quads, gain_row, w_qkv, w_qkv_t, w_out_near)
    swap = [(0, 1), (1, 0)]
    with jax.named_scope("sum_cores"):
        other = lax.ppermute(send, "core", swap)
    with jax.named_scope("window_tokens"):
        outs = pl.pallas_call(
            tokens_kernel,
            in_specs=[vmem] * 8,
            out_specs=[vmem] * 4,
            out_shape=[jax.ShapeDtypeStruct((2, SHIFT, SHIFT, levels, feat), BF16)] * 4,
            scratch_shapes=[pltpu.VMEM((n_tokens, feat), F32)],
            compiler_params=params,
        )(*quads, gain_row, w_out, attn_t, back)
    with jax.named_scope("sum_cores"):
        pair_sum = pl.pallas_call(
            pair_kernel,
            in_specs=[vmem] * 2,
            out_specs=vmem,
            out_shape=jax.ShapeDtypeStruct((rows, width), BF16),
            compiler_params=params,
        )(keep, other)
    pair_sum, *outs = lax.optimization_barrier((pair_sum, *outs))
    with jax.named_scope("window_out"):
        outs = [
            q if s == (0, 0) else lax.ppermute(q, EVERY, pairs(s[0], s[1]))
            for q, s in zip(outs, shifts)
        ]
    near, far = lax.axis_size(NEAR), lax.axis_size(FAR)
    factor = 1.0 / math.sqrt(lat_n * lat_rows * lon_n * lon_cols * levels)
    chunk = rows // near
    with jax.named_scope("sum_near"):
        pieces = lax.all_to_all(pair_sum.reshape(near, chunk, width), NEAR, 0, 0)
        pieces, *outs = lax.optimization_barrier((pieces, *outs))
        piece = jnp.sum(pieces.astype(F32), 0)
        piece = jnp.broadcast_to(piece[None], (far, chunk, width))
    with jax.named_scope("sum_far"):
        parts = lax.all_to_all(piece, FAR, 0, 0)
    with jax.named_scope("sum_far"):
        piece = pl.pallas_call(
            functools.partial(final_piece_kernel, factor),
            in_specs=[vmem],
            out_specs=vmem,
            out_shape=jax.ShapeDtypeStruct((chunk, width), BF16),
            compiler_params=params,
        )(parts)
    with jax.named_scope("share"):
        mine = lax.all_to_all(jnp.broadcast_to(piece[None], (near,) + piece.shape), NEAR, 0, 0)
        mine = mine.reshape(rows, width)
        theirs = lax.ppermute(mine, "core", swap)
    with jax.named_scope("finish"):
        shape = (1, 2 * SHIFT, 2 * SHIFT, levels, feat)
        mixed, grad_tokens, grad_qkv, grad_out, gain_gradient = pl.pallas_call(
            finish_kernel,
            in_specs=[vmem] * 2 + [hbm] * 4,
            out_specs=[hbm] * 5,
            out_shape=[
                jax.ShapeDtypeStruct(shape, BF16),
                jax.ShapeDtypeStruct(shape, BF16),
                jax.ShapeDtypeStruct((feat, 3 * feat), BF16),
                jax.ShapeDtypeStruct((feat, feat), BF16),
                jax.ShapeDtypeStruct((1, feat), F32),
            ],
            scratch_shapes=[pltpu.VMEM((1, feat), F32), pltpu.SemaphoreType.DMA((13,))],
            compiler_params=params,
        )(mine, theirs, *outs)
    return mixed, grad_tokens, gain_gradient[0], grad_qkv, grad_out


def solution(mesh):
    fine = Mesh(mesh.devices.reshape(2, 4, 4, 2, 2, 2), EVERY)
    grid = P(None, LAT, LON, None, None)
    return jax.shard_map(
        shards,
        mesh=fine,
        in_specs=(grid, P(), grid, P(), P()),
        out_specs=(grid, grid, P(), P(), P()),
        check_vma=False,
    )
```

```python
import functools
import math

import jax
import jax.numpy as jnp
from jax import lax
from jax.experimental import pallas as pl
from jax.experimental.pallas import tpu as pltpu
from jax.sharding import Mesh
from jax.sharding import PartitionSpec as P

HEADS = 16
WIN = 12
SHIFT = 6
EPS = 1e-05
MASKED = -1e30
F32 = jnp.float32
BF16 = jnp.bfloat16

LAT = ("xh", "y")
LON = ("zh", "zl", "xl", "core")
NEAR = ("xh", "y", "zl", "xl")
FAR = "zh"
EVERY = LAT + LON


def dot(a, b, dims=((1,), (0,))):
    return lax.dot_general(a, b, (dims, ((), ())), preferred_element_type=F32)


def normalise(tok):
    mean = jnp.mean(tok, -1, keepdims=True)
    centred = tok - mean
    inv = lax.rsqrt(jnp.mean(centred * centred, -1, keepdims=True) + EPS)
    return centred * inv, inv


def gather_quads(refs, which, out):
    rows = refs[0].shape[1]
    for j, ref in enumerate(refs):
        out[j * rows : (j + 1) * rows, :] = ref[which].astype(F32)


def lanes(shape):
    return lax.broadcasted_iota(jnp.int32, shape, len(shape) - 1)


def split_low(value, terms):
    lane = lanes(value.shape)
    out = jnp.zeros_like(value)
    rest = value
    for i in range(terms):
        part = rest.astype(BF16).astype(F32)
        out = jnp.where(lane == i, part, out)
        rest = rest - part
    return out.astype(BF16)


def weights_kernel(wqkv, wout, wqkv_t, wout_near):
    wqkv_t[...] = wqkv[...].T
    wout_near[...] = wout[...]


def grads_kernel(
    q0, q1, q2, q3, gain, wqkv, wqkv_t, wout,
    keep, send, attn_t, back,
    wide, normed, normed_t, g_low, q_t, kv_t, kv, do_t, dq_t, dkv_t, gain_col,
    diag, side, bias, scores, d_probs, p_low, d_low, acc,
):
    quads = (q0, q1, q2, q3)
    tokens, feat = wide.shape
    main = tokens // 128 * 128
    left = tokens - main
    ext = normed.shape[0]
    size = feat // HEADS
    per = 128 // size
    half = tokens // 2
    edge = lax.axis_index(LAT) == lax.axis_size(LAT) - 1
    core = lax.axis_index("core")
    inv_root = 1.0 / math.sqrt(size)
    to_exp2 = inv_root * math.log2(math.e)

    def repeat_left(ref):
        for j in range(1, per):
            ref[tokens + (j - 1) * left : tokens + j * left, :] = ref[main:tokens, :]

    gather_quads(quads, 1, wide)
    g_low[:tokens, :] = wide[...].astype(BF16)
    repeat_left(g_low)
    do_t[...] = dot(wout[...], g_low[...], ((1,), (1,))).astype(BF16)
    gather_quads(quads, 0, wide)
    xhat, _ = normalise(wide[...])
    wide[...] = xhat
    normed[:tokens, :] = (xhat * gain[...]).astype(BF16)
    repeat_left(normed)
    q_t[...] = dot(wqkv_t[:feat, :], normed[...], ((1,), (1,))).astype(BF16)
    kv_t[...] = dot(wqkv_t[feat:, :], normed[:tokens, :], ((1,), (1,))).astype(BF16)
    kv[...] = dot(normed[:tokens, :], wqkv[:, feat:]).astype(BF16)
    normed_t[...] = normed[...].T

    row_head = lax.broadcasted_iota(jnp.int32, (128, 128), 0) // size
    diag[...] = jnp.where(row_head == lanes((128, 128)) // left, 1.0, 0.0).astype(BF16)
    late_key = lax.broadcasted_iota(jnp.int32, (tokens, 128), 0) >= half
    lane = lanes((tokens, 128))
    side[...] = jnp.where(
        jnp.logical_or(
            jnp.logical_and(lane == 0, late_key),
            jnp.logical_and(lane == 1, jnp.logical_not(late_key)),
        ),
        1.0,
        0.0,
    ).astype(BF16)
    which = lax.broadcasted_iota(jnp.int32, (128, ext), 0)
    late_query = lanes((128, ext)) >= half
    blocked = jnp.logical_or(
        jnp.logical_and(which == 0, jnp.logical_not(late_query)),
        jnp.logical_and(which == 1, late_query),
    )
    bias[...] = jnp.where(jnp.logical_and(blocked, edge), MASKED, 0.0).astype(BF16)

    def spread(block, h):
        parts = []
        if h > 0:
            parts.append(jnp.zeros((h * size, block.shape[1]), BF16))
        parts.append(block)
        if h < per - 1:
            parts.append(jnp.zeros(((per - 1 - h) * size, block.shape[1]), BF16))
        return jnp.concatenate(parts, 0)

    def operand(ref, g, h):
        rows = slice(128 * g, 128 * (g + 1))
        if h is None:
            return ref[rows, main:ext] * diag[...]
        return spread(ref[128 * g + size * h : 128 * g + size * (h + 1), :main], h)

    def score(slot, g, h):
        cols = slice(128 * g, 128 * (g + 1))
        at, width = (slice(main, ext), ext - main) if h is None else (slice(0, main), main)
        keys = jnp.concatenate([kv[:, cols], side[...]], 1)
        queries = jnp.concatenate([operand(q_t, g, h), bias[:, at]], 0)
        scores[slot, :, :width] = dot(keys, queries)
        values = kv[:, feat + 128 * g : feat + 128 * (g + 1)]
        d_probs[slot, :, :width] = dot(values, operand(do_t, g, h))

    step = 32

    def soften(slot, h):
        width = ext - main if h is None else main
        chunks = [slice(c, c + step) for c in range(0, tokens, step)]

        def fold(value, op):
            return op(value.reshape(step // 8, 8, width), axis=0)

        top = None
        for c in chunks:
            part = fold(scores[slot, c, :width], jnp.max)
            top = part if top is None else jnp.maximum(top, part)
        top = jnp.max(top, 0, keepdims=True)
        total = jnp.zeros((8, width), F32)
        for c in chunks:
            e = jnp.exp2((scores[slot, c, :width] - top) * to_exp2)
            scores[slot, c, :width] = e
            total = total + fold(e, jnp.sum)
        scale = 1.0 / jnp.sum(total, 0, keepdims=True)
        delta = jnp.zeros((8, width), F32)
        for c in chunks:
            p = scores[slot, c, :width] * scale
            p_low[slot, c, :width] = p.astype(BF16)
            delta = delta + fold(d_probs[slot, c, :width] * p, jnp.sum)
        delta = jnp.sum(delta, 0, keepdims=True)
        scale = scale * inv_root
        for c in chunks:
            p = scores[slot, c, :width] * scale
            d_low[slot, c, :width] = (p * (d_probs[slot, c, :width] - delta)).astype(BF16)

    def collect(slot, g, h):
        nt = ((1,), (1,))
        if h is None:
            rows = slice(128 * g, 128 * (g + 1))
            later = slice(feat + 128 * g, feat + 128 * (g + 1))
            width = ext - main
            keep_own = diag[...].astype(F32)
            p, d = p_low[slot, :, :width], d_low[slot, :, :width]
            attn_t[rows, main:ext] = (dot(kv_t[later, :], p) * keep_own).astype(BF16)
            dq_t[rows, main:ext] = (dot(kv_t[rows, :], d) * keep_own).astype(BF16)
            acc[0] = dot(operand(q_t, g, h), d, nt)
            acc[1] = dot(operand(do_t, g, h), p, nt)
            return
        rows = slice(128 * g + size * h, 128 * g + size * (h + 1))
        later = slice(feat + rows.start, feat + rows.stop)
        own = slice(size * h, size * (h + 1))
        p, d = p_low[slot], d_low[slot]
        attn_t[rows, :main] = dot(kv_t[later, :], p).astype(BF16)
        dq_t[rows, :main] = dot(kv_t[rows, :], d).astype(BF16)
        dkv_t[rows, :] = (dot(q_t[rows, :main], d, nt) + acc[0, own, :]).astype(BF16)
        dkv_t[later, :] = (dot(do_t[rows, :main], p, nt) + acc[1, own, :]).astype(BF16)

    blocks = [(g, h) for g in range(HEADS // per) for h in (None, *range(per))]
    score(0, *blocks[0])
    for n, (g, h) in enumerate(blocks):
        if n + 1 < len(blocks):
            score((n + 1) % 2, *blocks[n + 1])
        soften(n % 2, h)
        if n > 0:
            collect((n - 1) % 2, *blocks[n - 1])
    collect((len(blocks) - 1) % 2, *blocks[-1])

    from_q = dot(wqkv[:, :feat], dq_t[...])
    from_kv = dot(wqkv[:, feat:], dkv_t[...])
    back[:main, :] = (from_q[:, :main] + from_kv[:, :main]).T.astype(BF16)
    rest = from_q[:, main:].T
    last = from_kv[:, main:].T
    for j in range(per):
        last = last + rest[j * left : (j + 1) * left]
    back[main:, :] = last.astype(BF16)
    part_gain = jnp.sum(back[...].astype(F32) * wide[...], 0, keepdims=True)
    column = jnp.broadcast_to(part_gain, (128, feat)).T
    gain_col[...] = jnp.where(lanes(column.shape) < 2, column, 0.0)

    rows = feat // 2
    mine = pl.multiple_of(core * rows, rows)
    theirs = pl.multiple_of((1 - core) * rows, rows)

    def partial_sums(start):
        pick = pl.ds(start, rows)
        return (
            dot(normed_t[pick, :], dq_t[...], ((1,), (1,))),
            dot(normed_t[pick, :tokens], dkv_t[:feat, :], ((1,), (1,))),
            dot(normed_t[pick, :tokens], dkv_t[feat:, :], ((1,), (1,))),
            dot(attn_t[pick, :], g_low[...]),
        )

    for block, value in enumerate(partial_sums(theirs)):
        send[:, block * feat : (block + 1) * feat] = value.astype(BF16)
    for block, value in enumerate(partial_sums(mine)):
        keep[:, block * feat : (block + 1) * feat] = value
    send[:, 4 * feat :] = gain_col[pl.ds(theirs, rows), :].astype(BF16)
    keep[:, 4 * feat :] = gain_col[pl.ds(mine, rows), :]


def grads_scratch(tokens, feat):
    ext = tokens // 128 * 128 + 128
    return [
        pltpu.VMEM((tokens, feat), F32),
        pltpu.VMEM((ext, feat), BF16),
        pltpu.VMEM((feat, ext), BF16),
        pltpu.VMEM((ext, feat), BF16),
        pltpu.VMEM((feat, ext), BF16),
        pltpu.VMEM((2 * feat, tokens), BF16),
        pltpu.VMEM((tokens, 2 * feat), BF16),
        pltpu.VMEM((feat, ext), BF16),
        pltpu.VMEM((feat, ext), BF16),
        pltpu.VMEM((2 * feat, tokens), BF16),
        pltpu.VMEM((feat, 128), F32),
        pltpu.VMEM((128, 128), BF16),
        pltpu.VMEM((tokens, 128), BF16),
        pltpu.VMEM((128, ext), BF16),
        pltpu.VMEM((2, tokens, 256), F32),
        pltpu.VMEM((2, tokens, 256), F32),
        pltpu.VMEM((2, tokens, 256), BF16),
        pltpu.VMEM((2, tokens, 256), BF16),
        pltpu.VMEM((2, 128, tokens), F32),
    ]


def tokens_kernel(q0, q1, q2, q3, gain, wout, attn_t, back, o0, o1, o2, o3, wide):
    quads, outs = (q0, q1, q2, q3), (o0, o1, o2, o3)
    rows = q0.shape[1]
    gather_quads(quads, 0, wide)
    tok = wide[...]
    main = tok.shape[0] // 128 * 128
    left = tok.shape[0] - main
    added = dot(attn_t[...], wout[...], ((0,), (0,)))
    last = added[main : main + left]
    for at in range(main + left, added.shape[0], left):
        last = last + added[at : at + left]
    mixed = tok + jnp.concatenate([added[:main], last], 0)
    for j, out in enumerate(outs):
        out[0] = mixed[j * rows : (j + 1) * rows].astype(BF16).reshape(out.shape[1:])
    xhat, inv = normalise(tok)
    scaled = back[...].astype(F32) * gain[...]
    inner = (
        scaled
        - jnp.mean(scaled, -1, keepdims=True)
        - xhat * jnp.mean(scaled * xhat, -1, keepdims=True)
    )
    gather_quads(quads, 1, wide)
    grad = wide[...] + inv * inner
    for j, out in enumerate(outs):
        out[1] = grad[j * rows : (j + 1) * rows].astype(BF16).reshape(out.shape[1:])


def gain_total(tile):
    return jnp.where(lanes(tile.shape) == 0, jnp.sum(tile, -1, keepdims=True), 0.0)


def add_pair(keep, other):
    total = keep + other.astype(F32)
    rest = total - lax.reduce_precision(total, 8, 7)
    return jnp.where(lanes(total.shape) == total.shape[1] - 127, rest, total).astype(BF16)


def final_piece_kernel(factor, mine, next1, next2, next3, _, out):
    main = mine.shape[1] - 128
    total = ((mine[...] + next2[...]) + (next1[...] + next3[...])) * factor
    out[:, :main] = total[:, :main].astype(BF16)
    out[:, main:] = split_low(gain_total(total[:, main:]), 3)


def finish_kernel(
    mine, theirs, o0, o1, o2, o3, mixed, grad_tokens, grad_qkv, grad_out, gain_grad, gains, sems
):
    rows = mine.shape[0]
    wide = grad_qkv.shape[1]
    main = wide + grad_out.shape[1]
    core = lax.axis_index("core")
    copies = []

    def copy(src, dst):
        item = pltpu.make_async_copy(src, dst, sems.at[len(copies)])
        item.start()
        copies.append(item)

    for n, half in enumerate((mine, theirs)):
        at = pl.multiple_of((core if n == 0 else 1 - core) * rows, rows)
        copy(half.at[:, :wide], grad_qkv.at[pl.ds(at, rows), :])
        copy(half.at[:, wide:main], grad_out.at[pl.ds(at, rows), :])
        column = half[:, main:].astype(F32).T
        gains[:, pl.ds(at, rows)] = column[0:1] + column[1:2] + column[2:3]
    copy(gains, gain_grad)
    for n, quad in enumerate((o0, o1, o2, o3)):
        lat = slice(0, SHIFT) if n // 2 else slice(SHIFT, 2 * SHIFT)
        lon = slice(0, SHIFT) if n % 2 else slice(SHIFT, 2 * SHIFT)
        copy(quad.at[0], mixed.at[0, lat, lon])
        copy(quad.at[1], grad_tokens.at[0, lat, lon])
    for item in copies:
        item.wait()


def shards(tokens, layer_norm_gain, cotangent, w_qkv, w_out):
    _, lat_rows, lon_cols, levels, feat = tokens.shape
    lat_n, lon_n = lax.axis_size(LAT), lax.axis_size(LON)
    quad_tokens = SHIFT * SHIFT * levels
    n_tokens = 4 * quad_tokens
    keep_part, go_part = slice(SHIFT, lat_rows), slice(0, SHIFT)

    def pairs(d_lat, d_lon):
        return [
            (a * lon_n + o, (a + d_lat) % lat_n * lon_n + (o + d_lon) % lon_n)
            for a in range(lat_n)
            for o in range(lon_n)
        ]

    def quad(rows, cols):
        both = jnp.stack([tokens[0, rows, cols], cotangent[0, rows, cols]])
        return both.reshape(2, quad_tokens, feat)

    shifts = ((0, 0), (0, 1), (1, 0), (1, 1))
    cuts = [(go_part if a else keep_part, go_part if o else keep_part) for a, o in shifts]
    with jax.named_scope("window_in"):
        quads = [quad(*cut) for cut in cuts]
        quads = [
            q if s == (0, 0) else lax.ppermute(q, EVERY, pairs(-s[0], -s[1]))
            for q, s in zip(quads, shifts)
        ]
    gain_row = layer_norm_gain[None, :]
    vmem = pl.BlockSpec(memory_space=pltpu.VMEM)
    hbm = pl.BlockSpec(memory_space=pl.ANY)
    params = pltpu.CompilerParams(vmem_limit_bytes=40 * 1024 * 1024)
    rows, width = feat // 2, 4 * feat + 128
    with jax.named_scope("weights"):
        w_qkv_t, w_out_near = pl.pallas_call(
            weights_kernel,
            in_specs=[vmem] * 2,
            out_specs=[vmem] * 2,
            out_shape=[
                jax.ShapeDtypeStruct((3 * feat, feat), BF16),
                jax.ShapeDtypeStruct((feat, feat), BF16),
            ],
            compiler_params=params,
        )(w_qkv, w_out)
    with jax.named_scope("window_grads"):
        keep, send, attn_t, back = pl.pallas_call(
            grads_kernel,
            in_specs=[vmem] * 8,
            out_specs=[vmem] * 4,
            out_shape=[
                jax.ShapeDtypeStruct((rows, width), F32),
                jax.ShapeDtypeStruct((rows, width), BF16),
                jax.ShapeDtypeStruct((feat, n_tokens // 128 * 128 + 128), BF16),
                jax.ShapeDtypeStruct((n_tokens, feat), BF16),
            ],
            scratch_shapes=grads_scratch(n_tokens, feat),
            compiler_params=params,
        )(*quads, gain_row, w_qkv, w_qkv_t, w_out_near)
    swap = [(0, 1), (1, 0)]
    with jax.named_scope("sum_cores"):
        other = lax.ppermute(send, "core", swap)
    with jax.named_scope("window_tokens"):
        outs = pl.pallas_call(
            tokens_kernel,
            in_specs=[vmem] * 8,
            out_specs=[vmem] * 4,
            out_shape=[jax.ShapeDtypeStruct((2, SHIFT, SHIFT, levels, feat), BF16)] * 4,
            scratch_shapes=[pltpu.VMEM((n_tokens, feat), F32)],
            compiler_params=params,
        )(*quads, gain_row, w_out, attn_t, back)
    with jax.named_scope("sum_cores"):
        pair_sum = add_pair(keep, other)
    pair_sum, *outs = lax.optimization_barrier((pair_sum, *outs))
    near, far = lax.axis_size(NEAR), lax.axis_size(FAR)
    factor = 1.0 / math.sqrt(lat_n * lat_rows * lon_n * lon_cols * levels)
    chunk = rows // near
    with jax.named_scope("sum_near"):
        pieces = lax.all_to_all(pair_sum.reshape(near, chunk, width), NEAR, 0, 0)
        piece = jnp.sum(pieces.astype(F32), 0)
    with jax.named_scope("sum_far"):
        others = [
            lax.ppermute(piece, FAR, [(i, (i + by) % far) for i in range(far)])
            for by in range(1, far)
        ]
    after, *outs = lax.optimization_barrier((piece, *outs))
    with jax.named_scope("window_out"):
        outs = [
            q if s == (0, 0) else lax.ppermute(q, EVERY, pairs(s[0], s[1]))
            for q, s in zip(outs, shifts)
        ]
    with jax.named_scope("sum_far"):
        piece = pl.pallas_call(
            functools.partial(final_piece_kernel, factor),
            in_specs=[vmem] * far + [hbm],
            out_specs=vmem,
            out_shape=jax.ShapeDtypeStruct((chunk, width), BF16),
            compiler_params=params,
        )(piece, *others, after)
    piece, *outs = lax.optimization_barrier((piece, *outs))
    with jax.named_scope("share"):
        mine = lax.all_to_all(jnp.broadcast_to(piece[None], (near,) + piece.shape), NEAR, 0, 0)
        mine = mine.reshape(rows, width)
        theirs = lax.ppermute(mine, "core", swap)
    with jax.named_scope("finish"):
        shape = (1, 2 * SHIFT, 2 * SHIFT, levels, feat)
        mixed, grad_tokens, grad_qkv, grad_out, gain_gradient = pl.pallas_call(
            finish_kernel,
            in_specs=[vmem] * 2 + [hbm] * 4,
            out_specs=[hbm] * 5,
            out_shape=[
                jax.ShapeDtypeStruct(shape, BF16),
                jax.ShapeDtypeStruct(shape, BF16),
                jax.ShapeDtypeStruct((feat, 3 * feat), BF16),
                jax.ShapeDtypeStruct((feat, feat), BF16),
                jax.ShapeDtypeStruct((1, feat), F32),
            ],
            scratch_shapes=[pltpu.VMEM((1, feat), F32), pltpu.SemaphoreType.DMA((13,))],
            compiler_params=params,
        )(mine, theirs, *outs)
    return mixed, grad_tokens, gain_gradient[0], grad_qkv, grad_out


def solution(mesh):
    fine = Mesh(mesh.devices.reshape(2, 4, 4, 2, 2, 2), EVERY)
    grid = P(None, LAT, LON, None, None)
    return jax.shard_map(
        shards,
        mesh=fine,
        in_specs=(grid, P(), grid, P(), P()),
        out_specs=(grid, grid, P(), P(), P()),
        check_vma=False,
    )
```

```python
import functools
import math

import jax
import jax.numpy as jnp
from jax import lax
from jax.experimental import pallas as pl
from jax.experimental.pallas import tpu as pltpu
from jax.sharding import Mesh
from jax.sharding import PartitionSpec as P

HEADS = 16
WIN = 12
SHIFT = 6
EPS = 1e-05
MASKED = -1e30
F32 = jnp.float32
BF16 = jnp.bfloat16

LAT = ("xh", "y")
LON = ("zh", "zl", "xl", "core")
NEAR = ("xh", "y", "zl", "xl")
FAR = "zh"
EVERY = LAT + LON


def dot(a, b, dims=((1,), (0,))):
    return lax.dot_general(a, b, (dims, ((), ())), preferred_element_type=F32)


def normalise(tok):
    mean = jnp.mean(tok, -1, keepdims=True)
    centred = tok - mean
    inv = lax.rsqrt(jnp.mean(centred * centred, -1, keepdims=True) + EPS)
    return centred * inv, inv


def gather_quads(refs, which, out):
    rows = refs[0].shape[1]
    for j, ref in enumerate(refs):
        out[j * rows : (j + 1) * rows, :] = ref[which].astype(F32)


def lanes(shape):
    return lax.broadcasted_iota(jnp.int32, shape, len(shape) - 1)


def split_low(value, terms):
    lane = lanes(value.shape)
    out = jnp.zeros_like(value)
    rest = value
    for i in range(terms):
        part = rest.astype(BF16).astype(F32)
        out = jnp.where(lane == i, part, out)
        rest = rest - part
    return out.astype(BF16)


def weights_kernel(wqkv, wout, wqkv_t, wout_near):
    wqkv_t[...] = wqkv[...].T
    wout_near[...] = wout[...]


def grads_kernel(
    q0, q1, q2, q3, gain, wqkv, wqkv_t, wout,
    keep, send, attn_t, back,
    wide, normed, normed_t, g_low, q_t, kv_t, kv, do_t, dq_t, dkv_t, gain_col,
    diag, side, bias, scores, d_probs, p_low, d_low, acc,
):
    quads = (q0, q1, q2, q3)
    tokens, feat = wide.shape
    main = tokens // 128 * 128
    left = tokens - main
    ext = normed.shape[0]
    size = feat // HEADS
    per = 128 // size
    half = tokens // 2
    core = lax.axis_index("core")
    edge = lax.axis_index(LAT) == jnp.where(core == 0, lax.axis_size(LAT) - 1, 0)
    inv_root = 1.0 / math.sqrt(size)
    to_exp2 = inv_root * math.log2(math.e)

    def repeat_left(ref):
        for j in range(1, per):
            ref[tokens + (j - 1) * left : tokens + j * left, :] = ref[main:tokens, :]

    gather_quads(quads, 1, wide)
    g_low[:tokens, :] = wide[...].astype(BF16)
    repeat_left(g_low)
    do_t[...] = dot(wout[...], g_low[...], ((1,), (1,))).astype(BF16)
    gather_quads(quads, 0, wide)
    xhat, _ = normalise(wide[...])
    wide[...] = xhat
    normed[:tokens, :] = (xhat * gain[...]).astype(BF16)
    repeat_left(normed)
    q_t[...] = dot(wqkv_t[:feat, :], normed[...], ((1,), (1,))).astype(BF16)
    kv_t[...] = dot(wqkv_t[feat:, :], normed[:tokens, :], ((1,), (1,))).astype(BF16)
    kv[...] = dot(normed[:tokens, :], wqkv[:, feat:]).astype(BF16)
    normed_t[...] = normed[...].T

    row_head = lax.broadcasted_iota(jnp.int32, (128, 128), 0) // size
    diag[...] = jnp.where(row_head == lanes((128, 128)) // left, 1.0, 0.0).astype(BF16)
    late_key = lax.broadcasted_iota(jnp.int32, (tokens, 128), 0) >= half
    lane = lanes((tokens, 128))
    side[...] = jnp.where(
        jnp.logical_or(
            jnp.logical_and(lane == 0, late_key),
            jnp.logical_and(lane == 1, jnp.logical_not(late_key)),
        ),
        1.0,
        0.0,
    ).astype(BF16)
    which = lax.broadcasted_iota(jnp.int32, (128, ext), 0)
    late_query = lanes((128, ext)) >= half
    blocked = jnp.logical_or(
        jnp.logical_and(which == 0, jnp.logical_not(late_query)),
        jnp.logical_and(which == 1, late_query),
    )
    bias[...] = jnp.where(jnp.logical_and(blocked, edge), MASKED, 0.0).astype(BF16)

    def spread(block, h):
        parts = []
        if h > 0:
            parts.append(jnp.zeros((h * size, block.shape[1]), BF16))
        parts.append(block)
        if h < per - 1:
            parts.append(jnp.zeros(((per - 1 - h) * size, block.shape[1]), BF16))
        return jnp.concatenate(parts, 0)

    def operand(ref, g, h):
        rows = slice(128 * g, 128 * (g + 1))
        if h is None:
            return ref[rows, main:ext] * diag[...]
        return spread(ref[128 * g + size * h : 128 * g + size * (h + 1), :main], h)

    def score(slot, g, h):
        cols = slice(128 * g, 128 * (g + 1))
        at, width = (slice(main, ext), ext - main) if h is None else (slice(0, main), main)
        keys = jnp.concatenate([kv[:, cols], side[...]], 1)
        queries = jnp.concatenate([operand(q_t, g, h), bias[:, at]], 0)
        scores[slot, :, :width] = dot(keys, queries)
        values = kv[:, feat + 128 * g : feat + 128 * (g + 1)]
        d_probs[slot, :, :width] = dot(values, operand(do_t, g, h))

    step = 32

    def soften(slot, h):
        width = ext - main if h is None else main
        chunks = [slice(c, c + step) for c in range(0, tokens, step)]

        def fold(value, op):
            return op(value.reshape(step // 8, 8, width), axis=0)

        top = None
        for c in chunks:
            part = fold(scores[slot, c, :width], jnp.max)
            top = part if top is None else jnp.maximum(top, part)
        top = jnp.max(top, 0, keepdims=True)
        total = jnp.zeros((8, width), F32)
        for c in chunks:
            e = jnp.exp2((scores[slot, c, :width] - top) * to_exp2)
            scores[slot, c, :width] = e
            total = total + fold(e, jnp.sum)
        scale = 1.0 / jnp.sum(total, 0, keepdims=True)
        delta = jnp.zeros((8, width), F32)
        for c in chunks:
            p = scores[slot, c, :width] * scale
            p_low[slot, c, :width] = p.astype(BF16)
            delta = delta + fold(d_probs[slot, c, :width] * p, jnp.sum)
        delta = jnp.sum(delta, 0, keepdims=True)
        scale = scale * inv_root
        for c in chunks:
            p = scores[slot, c, :width] * scale
            d_low[slot, c, :width] = (p * (d_probs[slot, c, :width] - delta)).astype(BF16)

    def collect(slot, g, h):
        nt = ((1,), (1,))
        if h is None:
            rows = slice(128 * g, 128 * (g + 1))
            later = slice(feat + 128 * g, feat + 128 * (g + 1))
            width = ext - main
            keep_own = diag[...].astype(F32)
            p, d = p_low[slot, :, :width], d_low[slot, :, :width]
            attn_t[rows, main:ext] = (dot(kv_t[later, :], p) * keep_own).astype(BF16)
            dq_t[rows, main:ext] = (dot(kv_t[rows, :], d) * keep_own).astype(BF16)
            acc[0] = dot(operand(q_t, g, h), d, nt)
            acc[1] = dot(operand(do_t, g, h), p, nt)
            return
        rows = slice(128 * g + size * h, 128 * g + size * (h + 1))
        later = slice(feat + rows.start, feat + rows.stop)
        own = slice(size * h, size * (h + 1))
        p, d = p_low[slot], d_low[slot]
        attn_t[rows, :main] = dot(kv_t[later, :], p).astype(BF16)
        dq_t[rows, :main] = dot(kv_t[rows, :], d).astype(BF16)
        dkv_t[rows, :] = (dot(q_t[rows, :main], d, nt) + acc[0, own, :]).astype(BF16)
        dkv_t[later, :] = (dot(do_t[rows, :main], p, nt) + acc[1, own, :]).astype(BF16)

    blocks = [(g, h) for g in range(HEADS // per) for h in (None, *range(per))]
    score(0, *blocks[0])
    for n, (g, h) in enumerate(blocks):
        if n + 1 < len(blocks):
            score((n + 1) % 2, *blocks[n + 1])
        soften(n % 2, h)
        if n > 0:
            collect((n - 1) % 2, *blocks[n - 1])
    collect((len(blocks) - 1) % 2, *blocks[-1])

    from_q = dot(wqkv[:, :feat], dq_t[...])
    from_kv = dot(wqkv[:, feat:], dkv_t[...])
    back[:main, :] = (from_q[:, :main] + from_kv[:, :main]).T.astype(BF16)
    rest = from_q[:, main:].T
    last = from_kv[:, main:].T
    for j in range(per):
        last = last + rest[j * left : (j + 1) * left]
    back[main:, :] = last.astype(BF16)
    part_gain = jnp.sum(back[...].astype(F32) * wide[...], 0, keepdims=True)
    column = jnp.broadcast_to(part_gain, (128, feat)).T
    gain_col[...] = jnp.where(lanes(column.shape) < 2, column, 0.0)

    rows = feat // 2
    mine = pl.multiple_of(core * rows, rows)
    theirs = pl.multiple_of((1 - core) * rows, rows)

    def partial_sums(start):
        pick = pl.ds(start, rows)
        return (
            dot(normed_t[pick, :], dq_t[...], ((1,), (1,))),
            dot(normed_t[pick, :tokens], dkv_t[:feat, :], ((1,), (1,))),
            dot(normed_t[pick, :tokens], dkv_t[feat:, :], ((1,), (1,))),
            dot(attn_t[pick, :], g_low[...]),
        )

    for block, value in enumerate(partial_sums(theirs)):
        send[:, block * feat : (block + 1) * feat] = value.astype(BF16)
    for block, value in enumerate(partial_sums(mine)):
        keep[:, block * feat : (block + 1) * feat] = value
    send[:, 4 * feat :] = gain_col[pl.ds(theirs, rows), :].astype(BF16)
    keep[:, 4 * feat :] = gain_col[pl.ds(mine, rows), :]


def grads_scratch(tokens, feat):
    ext = tokens // 128 * 128 + 128
    return [
        pltpu.VMEM((tokens, feat), F32),
        pltpu.VMEM((ext, feat), BF16),
        pltpu.VMEM((feat, ext), BF16),
        pltpu.VMEM((ext, feat), BF16),
        pltpu.VMEM((feat, ext), BF16),
        pltpu.VMEM((2 * feat, tokens), BF16),
        pltpu.VMEM((tokens, 2 * feat), BF16),
        pltpu.VMEM((feat, ext), BF16),
        pltpu.VMEM((feat, ext), BF16),
        pltpu.VMEM((2 * feat, tokens), BF16),
        pltpu.VMEM((feat, 128), F32),
        pltpu.VMEM((128, 128), BF16),
        pltpu.VMEM((tokens, 128), BF16),
        pltpu.VMEM((128, ext), BF16),
        pltpu.VMEM((2, tokens, 256), F32),
        pltpu.VMEM((2, tokens, 256), F32),
        pltpu.VMEM((2, tokens, 256), BF16),
        pltpu.VMEM((2, tokens, 256), BF16),
        pltpu.VMEM((2, 128, tokens), F32),
    ]


def tokens_kernel(q0, q1, q2, q3, gain, wout, attn_t, back, own, east, north, wide):
    quads, outs = (q0, q1, q2, q3), (own, east, north.at[0], north.at[1])
    rows = q0.shape[1]
    gather_quads(quads, 0, wide)
    tok = wide[...]
    main = tok.shape[0] // 128 * 128
    left = tok.shape[0] - main
    added = dot(attn_t[...], wout[...], ((0,), (0,)))
    last = added[main : main + left]
    for at in range(main + left, added.shape[0], left):
        last = last + added[at : at + left]
    mixed = tok + jnp.concatenate([added[:main], last], 0)
    for j, out in enumerate(outs):
        out[0] = mixed[j * rows : (j + 1) * rows].astype(BF16).reshape(out.shape[1:])
    xhat, inv = normalise(tok)
    scaled = back[...].astype(F32) * gain[...]
    inner = (
        scaled
        - jnp.mean(scaled, -1, keepdims=True)
        - xhat * jnp.mean(scaled * xhat, -1, keepdims=True)
    )
    gather_quads(quads, 1, wide)
    grad = wide[...] + inv * inner
    for j, out in enumerate(outs):
        out[1] = grad[j * rows : (j + 1) * rows].astype(BF16).reshape(out.shape[1:])


def gain_total(tile):
    return jnp.where(lanes(tile.shape) == 0, jnp.sum(tile, -1, keepdims=True), 0.0)


def add_pair(keep, other):
    total = keep + other.astype(F32)
    rest = total - lax.reduce_precision(total, 8, 7)
    return jnp.where(lanes(total.shape) == total.shape[1] - 127, rest, total).astype(BF16)


def final_piece_kernel(factor, mine, next1, next2, next3, _, out):
    main = mine.shape[1] - 128
    total = ((mine[...] + next2[...]) + (next1[...] + next3[...])) * factor
    out[:, :main] = total[:, :main].astype(BF16)
    out[:, main:] = split_low(gain_total(total[:, main:]), 3)


def half_rows(core):
    first = jnp.where(core == 0, SHIFT, 0)
    return first, SHIFT - first


def finish_kernel(
    mine, theirs, own, north, east,
    mixed, grad_tokens, grad_qkv, grad_out, gain_grad, gains, sems,
):
    rows = mine.shape[0]
    wide = grad_qkv.shape[1]
    main = wide + grad_out.shape[1]
    core = lax.axis_index("core")
    copies = []

    def copy(src, dst):
        item = pltpu.make_async_copy(src, dst, sems.at[len(copies)])
        item.start()
        copies.append(item)

    for n, half in enumerate((mine, theirs)):
        at = pl.multiple_of((core if n == 0 else 1 - core) * rows, rows)
        copy(half.at[:, :wide], grad_qkv.at[pl.ds(at, rows), :])
        copy(half.at[:, wide:main], grad_out.at[pl.ds(at, rows), :])
        column = half[:, main:].astype(F32).T
        gains[:, pl.ds(at, rows)] = column[0:1] + column[1:2] + column[2:3]
    copy(gains, gain_grad)
    own_rows, other_rows = half_rows(core)
    for quad, at, lon in (
        (own, own_rows, SHIFT),
        (north.at[0], other_rows, SHIFT),
        (east.at[0], other_rows, 0),
        (east.at[1], own_rows, 0),
    ):
        block = (0, pl.ds(at, SHIFT), pl.ds(lon, SHIFT))
        copy(quad.at[0], mixed.at[block])
        copy(quad.at[1], grad_tokens.at[block])
    for item in copies:
        item.wait()


def shards(tokens, layer_norm_gain, cotangent, w_qkv, w_out):
    _, lat_rows, lon_cols, levels, feat = tokens.shape
    lat_n, lon_n = lax.axis_size(LAT), lax.axis_size(LON)
    quad_tokens = SHIFT * SHIFT * levels
    n_tokens = 4 * quad_tokens
    own_rows, other_rows = half_rows(lax.axis_index("core"))

    def towards(lon):
        return 1 if lon % 2 == 0 else -1

    def pairs(target):
        return [
            (a * lon_n + o, target(a, o)[0] % lat_n * lon_n + target(a, o)[1] % lon_n)
            for a in range(lat_n)
            for o in range(lon_n)
        ]

    def quad(first, cols):
        both = [
            lax.dynamic_slice_in_dim(full[0, :, cols], first, SHIFT, 0)
            for full in (tokens, cotangent)
        ]
        return jnp.stack(both).reshape(2, quad_tokens, feat)

    near_cols, far_cols = slice(SHIFT, lon_cols), slice(0, SHIFT)
    with jax.named_scope("window_in"):
        quads = [
            quad(own_rows, near_cols),
            lax.ppermute(quad(other_rows, far_cols), EVERY, pairs(lambda a, o: (a, o - 1))),
            lax.ppermute(
                quad(other_rows, near_cols), EVERY, pairs(lambda a, o: (a - towards(o), o))
            ),
            lax.ppermute(
                quad(own_rows, far_cols), EVERY, pairs(lambda a, o: (a - towards(o - 1), o - 1))
            ),
        ]
    gain_row = layer_norm_gain[None, :]
    vmem = pl.BlockSpec(memory_space=pltpu.VMEM)
    hbm = pl.BlockSpec(memory_space=pl.ANY)
    params = pltpu.CompilerParams(vmem_limit_bytes=40 * 1024 * 1024)
    rows, width = feat // 2, 4 * feat + 128
    with jax.named_scope("weights"):
        w_qkv_t, w_out_near = pl.pallas_call(
            weights_kernel,
            in_specs=[vmem] * 2,
            out_specs=[vmem] * 2,
            out_shape=[
                jax.ShapeDtypeStruct((3 * feat, feat), BF16),
                jax.ShapeDtypeStruct((feat, feat), BF16),
            ],
            compiler_params=params,
        )(w_qkv, w_out)
    with jax.named_scope("window_grads"):
        keep, send, attn_t, back = pl.pallas_call(
            grads_kernel,
            in_specs=[vmem] * 8,
            out_specs=[vmem] * 4,
            out_shape=[
                jax.ShapeDtypeStruct((rows, width), F32),
                jax.ShapeDtypeStruct((rows, width), BF16),
                jax.ShapeDtypeStruct((feat, n_tokens // 128 * 128 + 128), BF16),
                jax.ShapeDtypeStruct((n_tokens, feat), BF16),
            ],
            scratch_shapes=grads_scratch(n_tokens, feat),
            compiler_params=params,
        )(*quads, gain_row, w_qkv, w_qkv_t, w_out_near)
    swap = [(0, 1), (1, 0)]
    with jax.named_scope("sum_cores"):
        other = lax.ppermute(send, "core", swap)
    with jax.named_scope("window_tokens"):
        own, east, north = pl.pallas_call(
            tokens_kernel,
            in_specs=[vmem] * 8,
            out_specs=[vmem] * 3,
            out_shape=[
                jax.ShapeDtypeStruct(lead + (2, SHIFT, SHIFT, levels, feat), BF16)
                for lead in ((), (), (2,))
            ],
            scratch_shapes=[pltpu.VMEM((n_tokens, feat), F32)],
            compiler_params=params,
        )(*quads, gain_row, w_out, attn_t, back)
    with jax.named_scope("sum_cores"):
        pair_sum = add_pair(keep, other)
    pair_sum, north = lax.optimization_barrier((pair_sum, north))
    near, far = lax.axis_size(NEAR), lax.axis_size(FAR)
    factor = 1.0 / math.sqrt(lat_n * lat_rows * lon_n * lon_cols * levels)
    chunk = rows // near
    with jax.named_scope("sum_near"):
        pieces = lax.all_to_all(pair_sum.reshape(near, chunk, width), NEAR, 0, 0)
        piece = jnp.sum(pieces.astype(F32), 0)
    with jax.named_scope("sum_far"):
        others = [
            lax.ppermute(piece, FAR, [(i, (i + by) % far) for i in range(far)])
            for by in range(1, far)
        ]
    after, north = lax.optimization_barrier((piece, north))
    with jax.named_scope("window_out"):
        north = lax.ppermute(north, EVERY, pairs(lambda a, o: (a + towards(o), o)))
    with jax.named_scope("sum_far"):
        piece = pl.pallas_call(
            functools.partial(final_piece_kernel, factor),
            in_specs=[vmem] * far + [hbm],
            out_specs=vmem,
            out_shape=jax.ShapeDtypeStruct((chunk, width), BF16),
            compiler_params=params,
        )(piece, *others, after)
    piece, north = lax.optimization_barrier((piece, north))
    with jax.named_scope("window_out"):
        east = jnp.stack([east, north[1]])
        east = lax.ppermute(east, EVERY, pairs(lambda a, o: (a, o + 1)))
    with jax.named_scope("share"):
        mine = lax.all_to_all(jnp.broadcast_to(piece[None], (near,) + piece.shape), NEAR, 0, 0)
        mine = mine.reshape(rows, width)
        theirs = lax.ppermute(mine, "core", swap)
    with jax.named_scope("finish"):
        shape = (1, 2 * SHIFT, 2 * SHIFT, levels, feat)
        mixed, grad_tokens, grad_qkv, grad_out, gain_gradient = pl.pallas_call(
            finish_kernel,
            in_specs=[vmem] * 2 + [hbm] * 3,
            out_specs=[hbm] * 5,
            out_shape=[
                jax.ShapeDtypeStruct(shape, BF16),
                jax.ShapeDtypeStruct(shape, BF16),
                jax.ShapeDtypeStruct((feat, 3 * feat), BF16),
                jax.ShapeDtypeStruct((feat, feat), BF16),
                jax.ShapeDtypeStruct((1, feat), F32),
            ],
            scratch_shapes=[pltpu.VMEM((1, feat), F32), pltpu.SemaphoreType.DMA((13,))],
            compiler_params=params,
        )(mine, theirs, own, north, east)
    return mixed, grad_tokens, gain_gradient[0], grad_qkv, grad_out


def solution(mesh):
    fine = Mesh(mesh.devices.reshape(2, 4, 4, 2, 2, 2), EVERY)
    grid = P(None, LAT, LON, None, None)
    return jax.shard_map(
        shards,
        mesh=fine,
        in_specs=(grid, P(), grid, P(), P()),
        out_specs=(grid, grid, P(), P(), P()),
        check_vma=False,
    )
```

```python
import functools
import math

import jax
import jax.numpy as jnp
from jax import lax
from jax.experimental import pallas as pl
from jax.experimental.pallas import tpu as pltpu
from jax.sharding import Mesh
from jax.sharding import PartitionSpec as P

HEADS = 16
WIN = 12
SHIFT = 6
EPS = 1e-05
MASKED = -1e30
F32 = jnp.float32
BF16 = jnp.bfloat16

LAT = ("xh", "y")
LON = ("zh", "zl", "xl", "core")
NEAR = ("xh", "y", "zl", "xl")
FAR = "zh"
EVERY = LAT + LON


def dot(a, b, dims=((1,), (0,))):
    return lax.dot_general(a, b, (dims, ((), ())), preferred_element_type=F32)


def normalise(tok):
    mean = jnp.mean(tok, -1, keepdims=True)
    centred = tok - mean
    inv = lax.rsqrt(jnp.mean(centred * centred, -1, keepdims=True) + EPS)
    return centred * inv, inv


def gather_quads(refs, which, out):
    rows = refs[0].shape[1]
    for j, ref in enumerate(refs):
        out[j * rows : (j + 1) * rows, :] = ref[which].astype(F32)


def lanes(shape):
    return lax.broadcasted_iota(jnp.int32, shape, len(shape) - 1)


def split_low(value, terms):
    lane = lanes(value.shape)
    out = jnp.zeros_like(value)
    rest = value
    for i in range(terms):
        part = rest.astype(BF16).astype(F32)
        out = jnp.where(lane == i, part, out)
        rest = rest - part
    return out.astype(BF16)


def weights_kernel(wqkv, wout, wqkv_t, wout_near):
    wqkv_t[...] = wqkv[...].T
    wout_near[...] = wout[...]


def grads_kernel(
    q0, q1, q2, q3, gain, wqkv, wqkv_t, wout,
    keep, send, attn_t, back,
    wide, normed, normed_t, g_low, q_t, kv_t, kv, do_t, dq_t, dkv_t, gain_col,
    diag, side, bias, scores, d_probs, p_low, d_low, acc,
):
    quads = (q0, q1, q2, q3)
    tokens, feat = wide.shape
    main = tokens // 128 * 128
    left = tokens - main
    ext = normed.shape[0]
    size = feat // HEADS
    per = 128 // size
    half = tokens // 2
    core = lax.axis_index("core")
    edge = lax.axis_index(LAT) == jnp.where(core == 0, lax.axis_size(LAT) - 1, 0)
    inv_root = 1.0 / math.sqrt(size)
    to_exp2 = inv_root * math.log2(math.e)

    def repeat_left(ref):
        for j in range(1, per):
            ref[tokens + (j - 1) * left : tokens + j * left, :] = ref[main:tokens, :]

    gather_quads(quads, 1, wide)
    g_low[:tokens, :] = wide[...].astype(BF16)
    repeat_left(g_low)
    do_t[...] = dot(wout[...], g_low[...], ((1,), (1,))).astype(BF16)
    gather_quads(quads, 0, wide)
    xhat, _ = normalise(wide[...])
    wide[...] = xhat
    normed[:tokens, :] = (xhat * gain[...]).astype(BF16)
    repeat_left(normed)
    q_t[...] = dot(wqkv_t[:feat, :], normed[...], ((1,), (1,))).astype(BF16)
    kv_t[...] = dot(wqkv_t[feat:, :], normed[:tokens, :], ((1,), (1,))).astype(BF16)
    kv[...] = dot(normed[:tokens, :], wqkv[:, feat:]).astype(BF16)
    normed_t[...] = normed[...].T

    row_head = lax.broadcasted_iota(jnp.int32, (128, 128), 0) // size
    diag[...] = jnp.where(row_head == lanes((128, 128)) // left, 1.0, 0.0).astype(BF16)
    late_key = lax.broadcasted_iota(jnp.int32, (tokens, 128), 0) >= half
    lane = lanes((tokens, 128))
    side[...] = jnp.where(
        jnp.logical_or(
            jnp.logical_and(lane == 0, late_key),
            jnp.logical_and(lane == 1, jnp.logical_not(late_key)),
        ),
        1.0,
        0.0,
    ).astype(BF16)
    which = lax.broadcasted_iota(jnp.int32, (128, ext), 0)
    late_query = lanes((128, ext)) >= half
    blocked = jnp.logical_or(
        jnp.logical_and(which == 0, jnp.logical_not(late_query)),
        jnp.logical_and(which == 1, late_query),
    )
    bias[...] = jnp.where(jnp.logical_and(blocked, edge), MASKED, 0.0).astype(BF16)

    def spread(block, h):
        parts = []
        if h > 0:
            parts.append(jnp.zeros((h * size, block.shape[1]), BF16))
        parts.append(block)
        if h < per - 1:
            parts.append(jnp.zeros(((per - 1 - h) * size, block.shape[1]), BF16))
        return jnp.concatenate(parts, 0)

    def operand(ref, g, h):
        rows = slice(128 * g, 128 * (g + 1))
        if h is None:
            return ref[rows, main:ext] * diag[...]
        return spread(ref[128 * g + size * h : 128 * g + size * (h + 1), :main], h)

    def score(slot, g, h):
        cols = slice(128 * g, 128 * (g + 1))
        at, width = (slice(main, ext), ext - main) if h is None else (slice(0, main), main)
        keys = jnp.concatenate([kv[:, cols], side[...]], 1)
        queries = jnp.concatenate([operand(q_t, g, h), bias[:, at]], 0)
        scores[slot, :, :width] = dot(keys, queries)
        values = kv[:, feat + 128 * g : feat + 128 * (g + 1)]
        d_probs[slot, :, :width] = dot(values, operand(do_t, g, h))

    step = 32

    def soften(slot, h):
        width = ext - main if h is None else main
        chunks = [slice(c, c + step) for c in range(0, tokens, step)]

        def fold(value, op):
            return op(value.reshape(step // 8, 8, width), axis=0)

        top = None
        for c in chunks:
            part = fold(scores[slot, c, :width], jnp.max)
            top = part if top is None else jnp.maximum(top, part)
        top = jnp.max(top, 0, keepdims=True)
        total = jnp.zeros((8, width), F32)
        for c in chunks:
            e = jnp.exp2((scores[slot, c, :width] - top) * to_exp2)
            scores[slot, c, :width] = e
            total = total + fold(e, jnp.sum)
        scale = 1.0 / jnp.sum(total, 0, keepdims=True)
        delta = jnp.zeros((8, width), F32)
        for c in chunks:
            p = scores[slot, c, :width] * scale
            p_low[slot, c, :width] = p.astype(BF16)
            delta = delta + fold(d_probs[slot, c, :width] * p, jnp.sum)
        delta = jnp.sum(delta, 0, keepdims=True)
        scale = scale * inv_root
        for c in chunks:
            p = scores[slot, c, :width] * scale
            d_low[slot, c, :width] = (p * (d_probs[slot, c, :width] - delta)).astype(BF16)

    def collect(slot, g, h):
        nt = ((1,), (1,))
        if h is None:
            rows = slice(128 * g, 128 * (g + 1))
            later = slice(feat + 128 * g, feat + 128 * (g + 1))
            width = ext - main
            keep_own = diag[...].astype(F32)
            p, d = p_low[slot, :, :width], d_low[slot, :, :width]
            attn_t[rows, main:ext] = (dot(kv_t[later, :], p) * keep_own).astype(BF16)
            dq_t[rows, main:ext] = (dot(kv_t[rows, :], d) * keep_own).astype(BF16)
            acc[0] = dot(operand(q_t, g, h), d, nt)
            acc[1] = dot(operand(do_t, g, h), p, nt)
            return
        rows = slice(128 * g + size * h, 128 * g + size * (h + 1))
        later = slice(feat + rows.start, feat + rows.stop)
        own = slice(size * h, size * (h + 1))
        p, d = p_low[slot], d_low[slot]
        attn_t[rows, :main] = dot(kv_t[later, :], p).astype(BF16)
        dq_t[rows, :main] = dot(kv_t[rows, :], d).astype(BF16)
        dkv_t[rows, :] = (dot(q_t[rows, :main], d, nt) + acc[0, own, :]).astype(BF16)
        dkv_t[later, :] = (dot(do_t[rows, :main], p, nt) + acc[1, own, :]).astype(BF16)

    blocks = [(g, h) for g in range(HEADS // per) for h in (None, *range(per))]
    score(0, *blocks[0])
    for n, (g, h) in enumerate(blocks):
        if n + 1 < len(blocks):
            score((n + 1) % 2, *blocks[n + 1])
        soften(n % 2, h)
        if n > 0:
            collect((n - 1) % 2, *blocks[n - 1])
    collect((len(blocks) - 1) % 2, *blocks[-1])

    from_q = dot(wqkv[:, :feat], dq_t[...])
    from_kv = dot(wqkv[:, feat:], dkv_t[...])
    back[:main, :] = (from_q[:, :main] + from_kv[:, :main]).T.astype(BF16)
    rest = from_q[:, main:].T
    last = from_kv[:, main:].T
    for j in range(per):
        last = last + rest[j * left : (j + 1) * left]
    back[main:, :] = last.astype(BF16)
    part_gain = jnp.sum(back[...].astype(F32) * wide[...], 0, keepdims=True)
    column = jnp.broadcast_to(part_gain, (128, feat)).T
    gain_col[...] = jnp.where(lanes(column.shape) < 2, column, 0.0)

    rows = feat // 2
    mine = pl.multiple_of(core * rows, rows)
    theirs = pl.multiple_of((1 - core) * rows, rows)

    def partial_sums(start):
        pick = pl.ds(start, rows)
        return (
            dot(normed_t[pick, :], dq_t[...], ((1,), (1,))),
            dot(normed_t[pick, :tokens], dkv_t[:feat, :], ((1,), (1,))),
            dot(normed_t[pick, :tokens], dkv_t[feat:, :], ((1,), (1,))),
            dot(attn_t[pick, :], g_low[...]),
        )

    for block, value in enumerate(partial_sums(theirs)):
        send[:, block * feat : (block + 1) * feat] = value.astype(BF16)
    for block, value in enumerate(partial_sums(mine)):
        keep[:, block * feat : (block + 1) * feat] = value
    send[:, 4 * feat :] = gain_col[pl.ds(theirs, rows), :].astype(BF16)
    keep[:, 4 * feat :] = gain_col[pl.ds(mine, rows), :]


def grads_scratch(tokens, feat):
    ext = tokens // 128 * 128 + 128
    return [
        pltpu.VMEM((tokens, feat), F32),
        pltpu.VMEM((ext, feat), BF16),
        pltpu.VMEM((feat, ext), BF16),
        pltpu.VMEM((ext, feat), BF16),
        pltpu.VMEM((feat, ext), BF16),
        pltpu.VMEM((2 * feat, tokens), BF16),
        pltpu.VMEM((tokens, 2 * feat), BF16),
        pltpu.VMEM((feat, ext), BF16),
        pltpu.VMEM((feat, ext), BF16),
        pltpu.VMEM((2 * feat, tokens), BF16),
        pltpu.VMEM((feat, 128), F32),
        pltpu.VMEM((128, 128), BF16),
        pltpu.VMEM((tokens, 128), BF16),
        pltpu.VMEM((128, ext), BF16),
        pltpu.VMEM((2, tokens, 256), F32),
        pltpu.VMEM((2, tokens, 256), F32),
        pltpu.VMEM((2, tokens, 256), BF16),
        pltpu.VMEM((2, tokens, 256), BF16),
        pltpu.VMEM((2, 128, tokens), F32),
    ]


def tokens_kernel(q0, q1, q2, q3, gain, wout, attn_t, back, own, east, north, wide):
    quads, outs = (q0, q1, q2, q3), (own, east, north.at[0], north.at[1])
    rows = q0.shape[1]
    gather_quads(quads, 0, wide)
    tok = wide[...]
    main = tok.shape[0] // 128 * 128
    left = tok.shape[0] - main
    added = dot(attn_t[...], wout[...], ((0,), (0,)))
    last = added[main : main + left]
    for at in range(main + left, added.shape[0], left):
        last = last + added[at : at + left]
    mixed = tok + jnp.concatenate([added[:main], last], 0)
    for j, out in enumerate(outs):
        out[0] = mixed[j * rows : (j + 1) * rows].astype(BF16).reshape(out.shape[1:])
    xhat, inv = normalise(tok)
    scaled = back[...].astype(F32) * gain[...]
    inner = (
        scaled
        - jnp.mean(scaled, -1, keepdims=True)
        - xhat * jnp.mean(scaled * xhat, -1, keepdims=True)
    )
    gather_quads(quads, 1, wide)
    grad = wide[...] + inv * inner
    for j, out in enumerate(outs):
        out[1] = grad[j * rows : (j + 1) * rows].astype(BF16).reshape(out.shape[1:])


def gain_total(tile):
    return jnp.where(lanes(tile.shape) == 0, jnp.sum(tile, -1, keepdims=True), 0.0)


def add_pair(keep, other):
    total = keep + other.astype(F32)
    rest = total - lax.reduce_precision(total, 8, 7)
    return jnp.where(lanes(total.shape) == total.shape[1] - 127, rest, total).astype(BF16)


def final_piece_kernel(factor, mine, next1, next2, next3, _, out):
    main = mine.shape[1] - 128
    total = ((mine[...] + next2[...]) + (next1[...] + next3[...])) * factor
    out[:, :main] = total[:, :main].astype(BF16)
    out[:, main:] = split_low(gain_total(total[:, main:]), 3)


def half_rows(core):
    first = jnp.where(core == 0, SHIFT, 0)
    return first, SHIFT - first


def finish_kernel(
    mine, theirs, own, north, east,
    mixed, grad_tokens, grad_qkv, grad_out, gain_grad, gains, sems,
):
    rows = mine.shape[0]
    wide = grad_qkv.shape[1]
    main = wide + grad_out.shape[1]
    core = lax.axis_index("core")
    copies = []

    def copy(src, dst):
        item = pltpu.make_async_copy(src, dst, sems.at[len(copies)])
        item.start()
        copies.append(item)

    for n, half in enumerate((mine, theirs)):
        at = pl.multiple_of((core if n == 0 else 1 - core) * rows, rows)
        copy(half.at[:, :wide], grad_qkv.at[pl.ds(at, rows), :])
        copy(half.at[:, wide:main], grad_out.at[pl.ds(at, rows), :])
        column = half[:, main:].astype(F32).T
        gains[:, pl.ds(at, rows)] = column[0:1] + column[1:2] + column[2:3]
    copy(gains, gain_grad)
    own_rows, other_rows = half_rows(core)
    for quad, at, lon in (
        (own, own_rows, SHIFT),
        (north.at[0], other_rows, SHIFT),
        (east.at[0], other_rows, 0),
        (east.at[1], own_rows, 0),
    ):
        block = (0, pl.ds(at, SHIFT), pl.ds(lon, SHIFT))
        copy(quad.at[0], mixed.at[block])
        copy(quad.at[1], grad_tokens.at[block])
    for item in copies:
        item.wait()


def shards(tokens, layer_norm_gain, cotangent, w_qkv, w_out):
    _, lat_rows, lon_cols, levels, feat = tokens.shape
    lat_n, lon_n = lax.axis_size(LAT), lax.axis_size(LON)
    quad_tokens = SHIFT * SHIFT * levels
    n_tokens = 4 * quad_tokens
    own_rows, other_rows = half_rows(lax.axis_index("core"))

    def towards(lon):
        return 1 if lon % 2 == 0 else -1

    def pairs(target):
        return [
            (a * lon_n + o, target(a, o)[0] % lat_n * lon_n + target(a, o)[1] % lon_n)
            for a in range(lat_n)
            for o in range(lon_n)
        ]

    low_first = own_rows == 0

    def quad(own, cols):
        low, high = (
            jnp.stack([full[0, rows, cols] for full in (tokens, cotangent)])
            for rows in (slice(0, SHIFT), slice(SHIFT, lat_rows))
        )
        both = jnp.where(low_first == own, low, high)
        return both.reshape(2, quad_tokens, feat)

    near_cols, far_cols = slice(SHIFT, lon_cols), slice(0, SHIFT)
    with jax.named_scope("window_in"):
        north = lax.ppermute(
            quad(False, near_cols), EVERY, pairs(lambda a, o: (a - towards(o), o))
        )
        corner = lax.ppermute(
            quad(True, far_cols), EVERY, pairs(lambda a, o: (a - towards(o - 1), o - 1))
        )
        east = lax.ppermute(quad(False, far_cols), EVERY, pairs(lambda a, o: (a, o - 1)))
        quads = [quad(True, near_cols), east, north, corner]
    gain_row = layer_norm_gain[None, :]
    vmem = pl.BlockSpec(memory_space=pltpu.VMEM)
    hbm = pl.BlockSpec(memory_space=pl.ANY)
    params = pltpu.CompilerParams(vmem_limit_bytes=40 * 1024 * 1024)
    rows, width = feat // 2, 4 * feat + 128
    with jax.named_scope("weights"):
        w_qkv_t, w_out_near = pl.pallas_call(
            weights_kernel,
            in_specs=[vmem] * 2,
            out_specs=[vmem] * 2,
            out_shape=[
                jax.ShapeDtypeStruct((3 * feat, feat), BF16),
                jax.ShapeDtypeStruct((feat, feat), BF16),
            ],
            compiler_params=params,
        )(w_qkv, w_out)
    with jax.named_scope("window_grads"):
        keep, send, attn_t, back = pl.pallas_call(
            grads_kernel,
            in_specs=[vmem] * 8,
            out_specs=[vmem] * 4,
            out_shape=[
                jax.ShapeDtypeStruct((rows, width), F32),
                jax.ShapeDtypeStruct((rows, width), BF16),
                jax.ShapeDtypeStruct((feat, n_tokens // 128 * 128 + 128), BF16),
                jax.ShapeDtypeStruct((n_tokens, feat), BF16),
            ],
            scratch_shapes=grads_scratch(n_tokens, feat),
            compiler_params=params,
        )(*quads, gain_row, w_qkv, w_qkv_t, w_out_near)
    swap = [(0, 1), (1, 0)]
    with jax.named_scope("sum_cores"):
        other = lax.ppermute(send, "core", swap)
    with jax.named_scope("window_tokens"):
        own, east, north = pl.pallas_call(
            tokens_kernel,
            in_specs=[vmem] * 8,
            out_specs=[vmem] * 3,
            out_shape=[
                jax.ShapeDtypeStruct(lead + (2, SHIFT, SHIFT, levels, feat), BF16)
                for lead in ((), (), (2,))
            ],
            scratch_shapes=[pltpu.VMEM((n_tokens, feat), F32)],
            compiler_params=params,
        )(*quads, gain_row, w_out, attn_t, back)
    with jax.named_scope("sum_cores"):
        pair_sum = add_pair(keep, other)
    pair_sum, north = lax.optimization_barrier((pair_sum, north))
    near, far = lax.axis_size(NEAR), lax.axis_size(FAR)
    factor = 1.0 / math.sqrt(lat_n * lat_rows * lon_n * lon_cols * levels)
    chunk = rows // near
    with jax.named_scope("sum_near"):
        pieces = lax.all_to_all(pair_sum.reshape(near, chunk, width), NEAR, 0, 0)
        piece = jnp.sum(pieces.astype(F32), 0)
    with jax.named_scope("sum_far"):
        others = [
            lax.ppermute(piece, FAR, [(i, (i + by) % far) for i in range(far)])
            for by in range(1, far)
        ]
    after, north = lax.optimization_barrier((piece, north))
    with jax.named_scope("window_out"):
        north = lax.ppermute(north, EVERY, pairs(lambda a, o: (a + towards(o), o)))
    with jax.named_scope("sum_far"):
        piece = pl.pallas_call(
            functools.partial(final_piece_kernel, factor),
            in_specs=[vmem] * far + [hbm],
            out_specs=vmem,
            out_shape=jax.ShapeDtypeStruct((chunk, width), BF16),
            compiler_params=params,
        )(piece, *others, after)
    piece, north = lax.optimization_barrier((piece, north))
    with jax.named_scope("window_out"):
        east = jnp.stack([east, north[1]])
        east = lax.ppermute(east, EVERY, pairs(lambda a, o: (a, o + 1)))
    with jax.named_scope("share"):
        mine = lax.all_to_all(jnp.broadcast_to(piece[None], (near,) + piece.shape), NEAR, 0, 0)
        mine = mine.reshape(rows, width)
        mine, east = lax.optimization_barrier((mine, east))
        theirs = lax.ppermute(mine, "core", swap)
    with jax.named_scope("finish"):
        shape = (1, 2 * SHIFT, 2 * SHIFT, levels, feat)
        mixed, grad_tokens, grad_qkv, grad_out, gain_gradient = pl.pallas_call(
            finish_kernel,
            in_specs=[vmem] * 2 + [hbm] * 3,
            out_specs=[hbm] * 5,
            out_shape=[
                jax.ShapeDtypeStruct(shape, BF16),
                jax.ShapeDtypeStruct(shape, BF16),
                jax.ShapeDtypeStruct((feat, 3 * feat), BF16),
                jax.ShapeDtypeStruct((feat, feat), BF16),
                jax.ShapeDtypeStruct((1, feat), F32),
            ],
            scratch_shapes=[pltpu.VMEM((1, feat), F32), pltpu.SemaphoreType.DMA((13,))],
            compiler_params=params,
        )(mine, theirs, own, north, east)
    return mixed, grad_tokens, gain_gradient[0], grad_qkv, grad_out


def solution(mesh):
    fine = Mesh(mesh.devices.reshape(2, 4, 4, 2, 2, 2), EVERY)
    grid = P(None, LAT, LON, None, None)
    return jax.shard_map(
        shards,
        mesh=fine,
        in_specs=(grid, P(), grid, P(), P()),
        out_specs=(grid, grid, P(), P(), P()),
        check_vma=False,
    )
```

```python
import functools
import math

import jax
import jax.numpy as jnp
from jax import lax
from jax.experimental import pallas as pl
from jax.experimental.pallas import tpu as pltpu
from jax.sharding import Mesh
from jax.sharding import PartitionSpec as P

HEADS = 16
WIN = 12
SHIFT = 6
EPS = 1e-05
MASKED = -1e30
F32 = jnp.float32
BF16 = jnp.bfloat16

LAT = ("xh", "y")
LON = ("zh", "zl", "xl", "core")
NEAR = ("xh", "y", "zl", "xl")
FAR = "zh"
EVERY = LAT + LON


def dot(a, b, dims=((1,), (0,))):
    return lax.dot_general(a, b, (dims, ((), ())), preferred_element_type=F32)


def normalise(tok):
    mean = jnp.mean(tok, -1, keepdims=True)
    centred = tok - mean
    inv = lax.rsqrt(jnp.mean(centred * centred, -1, keepdims=True) + EPS)
    return centred * inv, inv


def gather_quads(refs, which, out):
    rows = refs[0].shape[1]
    for j, ref in enumerate(refs):
        out[j * rows : (j + 1) * rows, :] = ref[which].astype(F32)


def lanes(shape):
    return lax.broadcasted_iota(jnp.int32, shape, len(shape) - 1)


def split_low(value, terms):
    lane = lanes(value.shape)
    out = jnp.zeros_like(value)
    rest = value
    for i in range(terms):
        part = rest.astype(BF16).astype(F32)
        out = jnp.where(lane == i, part, out)
        rest = rest - part
    return out.astype(BF16)


def weights_kernel(wqkv, wout, wqkv_t, wout_near):
    wqkv_t[...] = wqkv[...].T
    wout_near[...] = wout[...]


def partial_sums(start, normed_t, g_low, dq_t, dkv_t, attn_t):
    feat = attn_t.shape[0]
    tokens = dkv_t.shape[1]
    pick = pl.ds(start, feat // 2)
    return (
        dot(normed_t[pick, :], dq_t[...], ((1,), (1,))),
        dot(normed_t[pick, :tokens], dkv_t[:feat, :], ((1,), (1,))),
        dot(normed_t[pick, :tokens], dkv_t[feat:, :], ((1,), (1,))),
        dot(attn_t[pick, :], g_low[...]),
    )


def grads_kernel(
    q0, q1, q2, q3, gain, wqkv, wqkv_t, wout,
    send, attn_t, back, normed_t, g_low, dq_t, dkv_t, gain_col,
    wide, normed, q_t, kv_t, kv, do_t,
    diag, side, bias, scores, d_probs, p_low, d_low, acc,
):
    quads = (q0, q1, q2, q3)
    tokens, feat = wide.shape
    main = tokens // 128 * 128
    left = tokens - main
    ext = normed.shape[0]
    size = feat // HEADS
    per = 128 // size
    half = tokens // 2
    core = lax.axis_index("core")
    edge = lax.axis_index(LAT) == lax.axis_size(LAT) - 1
    inv_root = 1.0 / math.sqrt(size)
    to_exp2 = inv_root * math.log2(math.e)

    def repeat_left(ref):
        for j in range(1, per):
            ref[tokens + (j - 1) * left : tokens + j * left, :] = ref[main:tokens, :]

    gather_quads(quads, 1, wide)
    g_low[:tokens, :] = wide[...].astype(BF16)
    repeat_left(g_low)
    do_t[...] = dot(wout[...], g_low[...], ((1,), (1,))).astype(BF16)
    gather_quads(quads, 0, wide)
    xhat, _ = normalise(wide[...])
    wide[...] = xhat
    normed[:tokens, :] = (xhat * gain[...]).astype(BF16)
    repeat_left(normed)
    q_t[...] = dot(wqkv_t[:feat, :], normed[...], ((1,), (1,))).astype(BF16)
    kv_t[...] = dot(wqkv_t[feat:, :], normed[:tokens, :], ((1,), (1,))).astype(BF16)
    kv[...] = dot(normed[:tokens, :], wqkv[:, feat:]).astype(BF16)
    normed_t[...] = normed[...].T

    row_head = lax.broadcasted_iota(jnp.int32, (128, 128), 0) // size
    diag[...] = jnp.where(row_head == lanes((128, 128)) // left, 1.0, 0.0).astype(BF16)
    late_key = lax.broadcasted_iota(jnp.int32, (tokens, 128), 0) >= half
    lane = lanes((tokens, 128))
    side[...] = jnp.where(
        jnp.logical_or(
            jnp.logical_and(lane == 0, late_key),
            jnp.logical_and(lane == 1, jnp.logical_not(late_key)),
        ),
        1.0,
        0.0,
    ).astype(BF16)
    which = lax.broadcasted_iota(jnp.int32, (128, ext), 0)
    late_query = lanes((128, ext)) >= half
    blocked = jnp.logical_or(
        jnp.logical_and(which == 0, jnp.logical_not(late_query)),
        jnp.logical_and(which == 1, late_query),
    )
    bias[...] = jnp.where(jnp.logical_and(blocked, edge), MASKED, 0.0).astype(BF16)

    def spread(block, h):
        parts = []
        if h > 0:
            parts.append(jnp.zeros((h * size, block.shape[1]), BF16))
        parts.append(block)
        if h < per - 1:
            parts.append(jnp.zeros(((per - 1 - h) * size, block.shape[1]), BF16))
        return jnp.concatenate(parts, 0)

    def operand(ref, g, h):
        rows = slice(128 * g, 128 * (g + 1))
        if h is None:
            return ref[rows, main:ext] * diag[...]
        return spread(ref[128 * g + size * h : 128 * g + size * (h + 1), :main], h)

    def score(slot, g, h):
        cols = slice(128 * g, 128 * (g + 1))
        at, width = (slice(main, ext), ext - main) if h is None else (slice(0, main), main)
        keys = jnp.concatenate([kv[:, cols], side[...]], 1)
        queries = jnp.concatenate([operand(q_t, g, h), bias[:, at]], 0)
        scores[slot, :, :width] = dot(keys, queries)
        values = kv[:, feat + 128 * g : feat + 128 * (g + 1)]
        d_probs[slot, :, :width] = dot(values, operand(do_t, g, h))

    step = 32

    def soften(slot, h):
        width = ext - main if h is None else main
        chunks = [slice(c, c + step) for c in range(0, tokens, step)]

        def fold(value, op):
            return op(value.reshape(step // 8, 8, width), axis=0)

        top = None
        for c in chunks:
            part = fold(scores[slot, c, :width], jnp.max)
            top = part if top is None else jnp.maximum(top, part)
        top = jnp.max(top, 0, keepdims=True)
        total = jnp.zeros((8, width), F32)
        for c in chunks:
            e = jnp.exp2((scores[slot, c, :width] - top) * to_exp2)
            scores[slot, c, :width] = e
            total = total + fold(e, jnp.sum)
        scale = 1.0 / jnp.sum(total, 0, keepdims=True)
        delta = jnp.zeros((8, width), F32)
        for c in chunks:
            p = scores[slot, c, :width] * scale
            p_low[slot, c, :width] = p.astype(BF16)
            delta = delta + fold(d_probs[slot, c, :width] * p, jnp.sum)
        delta = jnp.sum(delta, 0, keepdims=True)
        scale = scale * inv_root
        for c in chunks:
            p = scores[slot, c, :width] * scale
            d_low[slot, c, :width] = (p * (d_probs[slot, c, :width] - delta)).astype(BF16)

    def collect(slot, g, h):
        nt = ((1,), (1,))
        if h is None:
            rows = slice(128 * g, 128 * (g + 1))
            later = slice(feat + 128 * g, feat + 128 * (g + 1))
            width = ext - main
            keep_own = diag[...].astype(F32)
            p, d = p_low[slot, :, :width], d_low[slot, :, :width]
            attn_t[rows, main:ext] = (dot(kv_t[later, :], p) * keep_own).astype(BF16)
            dq_t[rows, main:ext] = (dot(kv_t[rows, :], d) * keep_own).astype(BF16)
            acc[0] = dot(operand(q_t, g, h), d, nt)
            acc[1] = dot(operand(do_t, g, h), p, nt)
            return
        rows = slice(128 * g + size * h, 128 * g + size * (h + 1))
        later = slice(feat + rows.start, feat + rows.stop)
        own = slice(size * h, size * (h + 1))
        p, d = p_low[slot], d_low[slot]
        attn_t[rows, :main] = dot(kv_t[later, :], p).astype(BF16)
        dq_t[rows, :main] = dot(kv_t[rows, :], d).astype(BF16)
        dkv_t[rows, :] = (dot(q_t[rows, :main], d, nt) + acc[0, own, :]).astype(BF16)
        dkv_t[later, :] = (dot(do_t[rows, :main], p, nt) + acc[1, own, :]).astype(BF16)

    blocks = [(g, h) for g in range(HEADS // per) for h in (None, *range(per))]
    score(0, *blocks[0])
    for n, (g, h) in enumerate(blocks):
        if n + 1 < len(blocks):
            score((n + 1) % 2, *blocks[n + 1])
        soften(n % 2, h)
        if n > 0:
            collect((n - 1) % 2, *blocks[n - 1])
    collect((len(blocks) - 1) % 2, *blocks[-1])

    from_q = dot(wqkv[:, :feat], dq_t[...])
    from_kv = dot(wqkv[:, feat:], dkv_t[...])
    back[:main, :] = (from_q[:, :main] + from_kv[:, :main]).T.astype(BF16)
    rest = from_q[:, main:].T
    last = from_kv[:, main:].T
    for j in range(per):
        last = last + rest[j * left : (j + 1) * left]
    back[main:, :] = last.astype(BF16)
    part_gain = jnp.sum(back[...].astype(F32) * wide[...], 0, keepdims=True)
    column = jnp.broadcast_to(part_gain, (128, feat)).T
    gain_col[...] = jnp.where(lanes(column.shape) < 2, column, 0.0)

    rows = feat // 2
    theirs = pl.multiple_of((1 - core) * rows, rows)
    for block, value in enumerate(partial_sums(theirs, normed_t, g_low, dq_t, dkv_t, attn_t)):
        send[:, block * feat : (block + 1) * feat] = value.astype(BF16)
    send[:, 4 * feat :] = gain_col[pl.ds(theirs, rows), :].astype(BF16)


def grads_scratch(tokens, feat):
    ext = tokens // 128 * 128 + 128
    return [
        pltpu.VMEM((tokens, feat), F32),
        pltpu.VMEM((ext, feat), BF16),
        pltpu.VMEM((feat, ext), BF16),
        pltpu.VMEM((2 * feat, tokens), BF16),
        pltpu.VMEM((tokens, 2 * feat), BF16),
        pltpu.VMEM((feat, ext), BF16),
        pltpu.VMEM((128, 128), BF16),
        pltpu.VMEM((tokens, 128), BF16),
        pltpu.VMEM((128, ext), BF16),
        pltpu.VMEM((2, tokens, 256), F32),
        pltpu.VMEM((2, tokens, 256), F32),
        pltpu.VMEM((2, tokens, 256), BF16),
        pltpu.VMEM((2, tokens, 256), BF16),
        pltpu.VMEM((2, 128, tokens), F32),
    ]


def tokens_kernel(
    q0, q1, q2, q3, gain, wout, attn_t, back, normed_t, g_low, dq_t, dkv_t, gain_col,
    keep, own, east, north, wide,
):
    feat = attn_t.shape[0]
    half = feat // 2
    mine = pl.multiple_of(lax.axis_index("core") * half, half)
    for block, value in enumerate(partial_sums(mine, normed_t, g_low, dq_t, dkv_t, attn_t)):
        keep[:, block * feat : (block + 1) * feat] = value
    keep[:, 4 * feat :] = gain_col[pl.ds(mine, half), :]
    quads, outs = (q0, q1, q2, q3), (own, east, north.at[0], north.at[1])
    rows = q0.shape[1]
    gather_quads(quads, 0, wide)
    tok = wide[...]
    main = tok.shape[0] // 128 * 128
    left = tok.shape[0] - main
    added = dot(attn_t[...], wout[...], ((0,), (0,)))
    last = added[main : main + left]
    for at in range(main + left, added.shape[0], left):
        last = last + added[at : at + left]
    mixed = tok + jnp.concatenate([added[:main], last], 0)
    for j, out in enumerate(outs):
        out[0] = mixed[j * rows : (j + 1) * rows].astype(BF16).reshape(out.shape[1:])
    xhat, inv = normalise(tok)
    scaled = back[...].astype(F32) * gain[...]
    inner = (
        scaled
        - jnp.mean(scaled, -1, keepdims=True)
        - xhat * jnp.mean(scaled * xhat, -1, keepdims=True)
    )
    gather_quads(quads, 1, wide)
    grad = wide[...] + inv * inner
    for j, out in enumerate(outs):
        out[1] = grad[j * rows : (j + 1) * rows].astype(BF16).reshape(out.shape[1:])


def gain_total(tile):
    return jnp.where(lanes(tile.shape) == 0, jnp.sum(tile, -1, keepdims=True), 0.0)


def add_pair(keep, other):
    total = keep + other.astype(F32)
    rest = total - lax.reduce_precision(total, 8, 7)
    return jnp.where(lanes(total.shape) == total.shape[1] - 127, rest, total).astype(BF16)


def final_piece_kernel(factor, mine, next1, next2, next3, _, out):
    main = mine.shape[1] - 128
    total = ((mine[...] + next2[...]) + (next1[...] + next3[...])) * factor
    out[:, :main] = total[:, :main].astype(BF16)
    out[:, main:] = split_low(gain_total(total[:, main:]), 3)


def finish_kernel(
    mine, theirs, own, north, east,
    mixed, grad_tokens, grad_qkv, grad_out, gain_grad, gains, sems,
):
    rows = mine.shape[0]
    wide = grad_qkv.shape[1]
    main = wide + grad_out.shape[1]
    core = lax.axis_index("core")
    copies = []

    def copy(src, dst):
        item = pltpu.make_async_copy(src, dst, sems.at[len(copies)])
        item.start()
        copies.append(item)

    for n, half in enumerate((mine, theirs)):
        at = pl.multiple_of((core if n == 0 else 1 - core) * rows, rows)
        copy(half.at[:, :wide], grad_qkv.at[pl.ds(at, rows), :])
        copy(half.at[:, wide:main], grad_out.at[pl.ds(at, rows), :])
        column = half[:, main:].astype(F32).T
        gains[:, pl.ds(at, rows)] = column[0:1] + column[1:2] + column[2:3]
    copy(gains, gain_grad)
    for quad, at, lon in (
        (own, SHIFT, SHIFT),
        (north.at[0], 0, SHIFT),
        (east.at[0], SHIFT, 0),
        (east.at[1], 0, 0),
    ):
        block = (0, pl.ds(at, SHIFT), pl.ds(lon, SHIFT))
        copy(quad.at[0], mixed.at[block])
        copy(quad.at[1], grad_tokens.at[block])
    for item in copies:
        item.wait()


def shards(tokens, layer_norm_gain, cotangent, w_qkv, w_out):
    _, lat_rows, lon_cols, levels, feat = tokens.shape
    lat_n, lon_n = lax.axis_size(LAT), lax.axis_size(LON)
    quad_tokens = SHIFT * SHIFT * levels
    n_tokens = 4 * quad_tokens

    def pairs(target):
        return [
            (a * lon_n + o, target(a, o)[0] % lat_n * lon_n + target(a, o)[1] % lon_n)
            for a in range(lat_n)
            for o in range(lon_n)
        ]

    vmem = pl.BlockSpec(memory_space=pltpu.VMEM)
    hbm = pl.BlockSpec(memory_space=pl.ANY)
    params = pltpu.CompilerParams(vmem_limit_bytes=40 * 1024 * 1024)
    with jax.named_scope("window_in"):

        def quad(rows, cols):
            both = jnp.stack([tokens[0, rows, cols], cotangent[0, rows, cols]])
            return both.reshape(2, quad_tokens, feat)

        low, high = slice(0, SHIFT), slice(SHIFT, 2 * SHIFT)
        own, east = quad(high, high), quad(high, low)
        north, corner = quad(low, high), quad(low, low)
        east = lax.ppermute(east, EVERY, pairs(lambda a, o: (a, o - 1)))
        north = lax.ppermute(north, EVERY, pairs(lambda a, o: (a - 1, o)))
        corner = lax.ppermute(corner, EVERY, pairs(lambda a, o: (a - 1, o - 1)))
        quads = [own, east, north, corner]
    gain_row = layer_norm_gain[None, :]
    rows, width = feat // 2, 4 * feat + 128
    ext = n_tokens // 128 * 128 + 128
    with jax.named_scope("weights"):
        w_qkv_t, w_out_near = pl.pallas_call(
            weights_kernel,
            in_specs=[vmem] * 2,
            out_specs=[vmem] * 2,
            out_shape=[
                jax.ShapeDtypeStruct((3 * feat, feat), BF16),
                jax.ShapeDtypeStruct((feat, feat), BF16),
            ],
            compiler_params=params,
        )(w_qkv, w_out)
    with jax.named_scope("window_grads"):
        send, *shared = pl.pallas_call(
            grads_kernel,
            in_specs=[vmem] * 8,
            out_specs=[vmem] * 8,
            out_shape=[
                jax.ShapeDtypeStruct((rows, width), BF16),
                jax.ShapeDtypeStruct((feat, ext), BF16),
                jax.ShapeDtypeStruct((n_tokens, feat), BF16),
                jax.ShapeDtypeStruct((feat, ext), BF16),
                jax.ShapeDtypeStruct((ext, feat), BF16),
                jax.ShapeDtypeStruct((feat, ext), BF16),
                jax.ShapeDtypeStruct((2 * feat, n_tokens), BF16),
                jax.ShapeDtypeStruct((feat, 128), F32),
            ],
            scratch_shapes=grads_scratch(n_tokens, feat),
            compiler_params=params,
        )(*quads, gain_row, w_qkv, w_qkv_t, w_out_near)
    swap = [(0, 1), (1, 0)]
    with jax.named_scope("sum_cores"):
        other = lax.ppermute(send, "core", swap)
    with jax.named_scope("window_tokens"):
        keep, own, east, north = pl.pallas_call(
            tokens_kernel,
            in_specs=[vmem] * 13,
            out_specs=[vmem] * 4,
            out_shape=[
                jax.ShapeDtypeStruct((rows, width), F32),
                *(
                    jax.ShapeDtypeStruct(lead + (2, SHIFT, SHIFT, levels, feat), BF16)
                    for lead in ((), (), (2,))
                ),
            ],
            scratch_shapes=[pltpu.VMEM((n_tokens, feat), F32)],
            compiler_params=params,
        )(*quads, gain_row, w_out, *shared)
    with jax.named_scope("sum_cores"):
        pair_sum = add_pair(keep, other)
    pair_sum, north = lax.optimization_barrier((pair_sum, north))
    near, far = lax.axis_size(NEAR), lax.axis_size(FAR)
    factor = 1.0 / math.sqrt(lat_n * lat_rows * lon_n * lon_cols * levels)
    chunk = rows // near
    with jax.named_scope("sum_near"):
        pieces = lax.all_to_all(pair_sum.reshape(near, chunk, width), NEAR, 0, 0)
        piece = jnp.sum(pieces.astype(F32), 0)
    with jax.named_scope("sum_far"):
        others = [
            lax.ppermute(piece, FAR, [(i, (i + by) % far) for i in range(far)])
            for by in range(1, far)
        ]
    after, north = lax.optimization_barrier((piece, north))
    with jax.named_scope("window_out"):
        north = lax.ppermute(north, EVERY, pairs(lambda a, o: (a + 1, o)))
    with jax.named_scope("sum_far"):
        piece = pl.pallas_call(
            functools.partial(final_piece_kernel, factor),
            in_specs=[vmem] * far + [hbm],
            out_specs=vmem,
            out_shape=jax.ShapeDtypeStruct((chunk, width), BF16),
            compiler_params=params,
        )(piece, *others, after)
    piece, north = lax.optimization_barrier((piece, north))
    with jax.named_scope("window_out"):
        east = jnp.stack([east, north[1]])
        east = lax.ppermute(east, EVERY, pairs(lambda a, o: (a, o + 1)))
    with jax.named_scope("share"):
        mine = lax.all_to_all(jnp.broadcast_to(piece[None], (near,) + piece.shape), NEAR, 0, 0)
        mine = mine.reshape(rows, width)
        mine, east = lax.optimization_barrier((mine, east))
        theirs = lax.ppermute(mine, "core", swap)
    with jax.named_scope("finish"):
        shape = (1, 2 * SHIFT, 2 * SHIFT, levels, feat)
        mixed, grad_tokens, grad_qkv, grad_out, gain_gradient = pl.pallas_call(
            finish_kernel,
            in_specs=[vmem] * 2 + [hbm] * 3,
            out_specs=[hbm] * 5,
            out_shape=[
                jax.ShapeDtypeStruct(shape, BF16),
                jax.ShapeDtypeStruct(shape, BF16),
                jax.ShapeDtypeStruct((feat, 3 * feat), BF16),
                jax.ShapeDtypeStruct((feat, feat), BF16),
                jax.ShapeDtypeStruct((1, feat), F32),
            ],
            scratch_shapes=[pltpu.VMEM((1, feat), F32), pltpu.SemaphoreType.DMA((13,))],
            compiler_params=params,
        )(mine, theirs, own, north, east)
    return mixed, grad_tokens, gain_gradient[0], grad_qkv, grad_out


def solution(mesh):
    fine = Mesh(mesh.devices.reshape(2, 4, 4, 2, 2, 2), EVERY)
    grid = P(None, LAT, LON, None, None)
    return jax.shard_map(
        shards,
        mesh=fine,
        in_specs=(grid, P(), grid, P(), P()),
        out_specs=(grid, grid, P(), P(), P()),
        check_vma=False,
    )
```

```python
import functools
import math

import jax
import jax.numpy as jnp
from jax import lax
from jax.experimental import pallas as pl
from jax.experimental.pallas import tpu as pltpu
from jax.sharding import Mesh
from jax.sharding import PartitionSpec as P

HEADS = 16
WIN = 12
SHIFT = 6
EPS = 1e-05
MASKED = -1e30
F32 = jnp.float32
BF16 = jnp.bfloat16

LAT = ("xh", "y")
LON = ("zh", "zl", "xl", "core")
NEAR = ("xh", "y", "zl", "xl")
FAR = "zh"
EVERY = LAT + LON


def dot(a, b, dims=((1,), (0,))):
    return lax.dot_general(a, b, (dims, ((), ())), preferred_element_type=F32)


def normalise(tok):
    mean = jnp.mean(tok, -1, keepdims=True)
    centred = tok - mean
    inv = lax.rsqrt(jnp.mean(centred * centred, -1, keepdims=True) + EPS)
    return centred * inv, inv


def gather_quads(refs, which, out):
    rows = refs[0].shape[1]
    for j, ref in enumerate(refs):
        out[j * rows : (j + 1) * rows, :] = ref[which].astype(F32)


def lanes(shape):
    return lax.broadcasted_iota(jnp.int32, shape, len(shape) - 1)


def split_low(value, terms):
    lane = lanes(value.shape)
    out = jnp.zeros_like(value)
    rest = value
    for i in range(terms):
        part = rest.astype(BF16).astype(F32)
        out = jnp.where(lane == i, part, out)
        rest = rest - part
    return out.astype(BF16)


def weights_kernel(wqkv, wout, wqkv_t, wout_near):
    wqkv_t[...] = wqkv[...].T
    wout_near[...] = wout[...]


def partial_sums(start, normed_t, g_low, dq_t, dkv_t, attn_t):
    feat = attn_t.shape[0]
    tokens = dkv_t.shape[1]
    pick = pl.ds(start, feat // 2)
    return (
        dot(normed_t[pick, :], dq_t[...], ((1,), (1,))),
        dot(normed_t[pick, :tokens], dkv_t[:feat, :], ((1,), (1,))),
        dot(normed_t[pick, :tokens], dkv_t[feat:, :], ((1,), (1,))),
        dot(attn_t[pick, :], g_low[...]),
    )


def grads_kernel(
    q0, q1, q2, q3, gain, wqkv, wqkv_t, wout,
    send, attn_t, back, normed_t, g_low, dq_t, dkv_t, gain_col,
    wide, normed, q_t, kv_t, kv, do_t,
    diag, side, bias, scores, d_probs, p_low, d_low, acc,
):
    quads = (q0, q1, q2, q3)
    tokens, feat = wide.shape
    main = tokens // 128 * 128
    left = tokens - main
    ext = normed.shape[0]
    size = feat // HEADS
    per = 128 // size
    half = tokens // 2
    core = lax.axis_index("core")
    edge = lax.axis_index(LAT) == lax.axis_size(LAT) - 1
    inv_root = 1.0 / math.sqrt(size)
    to_exp2 = inv_root * math.log2(math.e)

    def repeat_left(ref):
        for j in range(1, per):
            ref[tokens + (j - 1) * left : tokens + j * left, :] = ref[main:tokens, :]

    gather_quads(quads, 1, wide)
    g_low[:tokens, :] = wide[...].astype(BF16)
    repeat_left(g_low)
    do_t[...] = dot(wout[...], g_low[...], ((1,), (1,))).astype(BF16)
    gather_quads(quads, 0, wide)
    xhat, _ = normalise(wide[...])
    wide[...] = xhat
    normed[:tokens, :] = (xhat * gain[...]).astype(BF16)
    repeat_left(normed)
    q_t[...] = dot(wqkv_t[:feat, :], normed[...], ((1,), (1,))).astype(BF16)
    kv_t[...] = dot(wqkv_t[feat:, :], normed[:tokens, :], ((1,), (1,))).astype(BF16)
    kv[...] = dot(normed[:tokens, :], wqkv[:, feat:]).astype(BF16)
    normed_t[...] = normed[...].T

    row_head = lax.broadcasted_iota(jnp.int32, (128, 128), 0) // size
    diag[...] = jnp.where(row_head == lanes((128, 128)) // left, 1.0, 0.0).astype(BF16)
    late_key = lax.broadcasted_iota(jnp.int32, (tokens, 128), 0) >= half
    lane = lanes((tokens, 128))
    side[...] = jnp.where(
        jnp.logical_or(
            jnp.logical_and(lane == 0, late_key),
            jnp.logical_and(lane == 1, jnp.logical_not(late_key)),
        ),
        1.0,
        0.0,
    ).astype(BF16)
    which = lax.broadcasted_iota(jnp.int32, (128, ext), 0)
    late_query = lanes((128, ext)) >= half
    blocked = jnp.logical_or(
        jnp.logical_and(which == 0, jnp.logical_not(late_query)),
        jnp.logical_and(which == 1, late_query),
    )
    bias[...] = jnp.where(jnp.logical_and(blocked, edge), MASKED, 0.0).astype(BF16)

    def spread(block, h):
        parts = []
        if h > 0:
            parts.append(jnp.zeros((h * size, block.shape[1]), BF16))
        parts.append(block)
        if h < per - 1:
            parts.append(jnp.zeros(((per - 1 - h) * size, block.shape[1]), BF16))
        return jnp.concatenate(parts, 0)

    def operand(ref, g, h):
        rows = slice(128 * g, 128 * (g + 1))
        if h is None:
            return ref[rows, main:ext] * diag[...]
        return spread(ref[128 * g + size * h : 128 * g + size * (h + 1), :main], h)

    def score(slot, g, h):
        cols = slice(128 * g, 128 * (g + 1))
        at, width = (slice(main, ext), ext - main) if h is None else (slice(0, main), main)
        keys = jnp.concatenate([kv[:, cols], side[...]], 1)
        queries = jnp.concatenate([operand(q_t, g, h), bias[:, at]], 0)
        scores[slot, :, :width] = dot(keys, queries)
        values = kv[:, feat + 128 * g : feat + 128 * (g + 1)]
        d_probs[slot, :, :width] = dot(values, operand(do_t, g, h))

    step = 32

    def soften(slot, h):
        width = ext - main if h is None else main
        chunks = [slice(c, c + step) for c in range(0, tokens, step)]

        def fold(value, op):
            return op(value.reshape(step // 8, 8, width), axis=0)

        top = None
        for c in chunks:
            part = fold(scores[slot, c, :width], jnp.max)
            top = part if top is None else jnp.maximum(top, part)
        top = jnp.max(top, 0, keepdims=True)
        total = jnp.zeros((8, width), F32)
        for c in chunks:
            e = jnp.exp2((scores[slot, c, :width] - top) * to_exp2)
            scores[slot, c, :width] = e
            total = total + fold(e, jnp.sum)
        scale = 1.0 / jnp.sum(total, 0, keepdims=True)
        delta = jnp.zeros((8, width), F32)
        for c in chunks:
            p = scores[slot, c, :width] * scale
            p_low[slot, c, :width] = p.astype(BF16)
            delta = delta + fold(d_probs[slot, c, :width] * p, jnp.sum)
        delta = jnp.sum(delta, 0, keepdims=True)
        scale = scale * inv_root
        for c in chunks:
            p = scores[slot, c, :width] * scale
            d_low[slot, c, :width] = (p * (d_probs[slot, c, :width] - delta)).astype(BF16)

    def collect(slot, g, h):
        nt = ((1,), (1,))
        if h is None:
            rows = slice(128 * g, 128 * (g + 1))
            later = slice(feat + 128 * g, feat + 128 * (g + 1))
            width = ext - main
            keep_own = diag[...].astype(F32)
            p, d = p_low[slot, :, :width], d_low[slot, :, :width]
            attn_t[rows, main:ext] = (dot(kv_t[later, :], p) * keep_own).astype(BF16)
            dq_t[rows, main:ext] = (dot(kv_t[rows, :], d) * keep_own).astype(BF16)
            acc[0] = dot(operand(q_t, g, h), d, nt)
            acc[1] = dot(operand(do_t, g, h), p, nt)
            return
        rows = slice(128 * g + size * h, 128 * g + size * (h + 1))
        later = slice(feat + rows.start, feat + rows.stop)
        own = slice(size * h, size * (h + 1))
        p, d = p_low[slot], d_low[slot]
        attn_t[rows, :main] = dot(kv_t[later, :], p).astype(BF16)
        dq_t[rows, :main] = dot(kv_t[rows, :], d).astype(BF16)
        dkv_t[rows, :] = (dot(q_t[rows, :main], d, nt) + acc[0, own, :]).astype(BF16)
        dkv_t[later, :] = (dot(do_t[rows, :main], p, nt) + acc[1, own, :]).astype(BF16)

    blocks = [(g, h) for g in range(HEADS // per) for h in (None, *range(per))]
    score(0, *blocks[0])
    for n, (g, h) in enumerate(blocks):
        if n + 1 < len(blocks):
            score((n + 1) % 2, *blocks[n + 1])
        soften(n % 2, h)
        if n > 0:
            collect((n - 1) % 2, *blocks[n - 1])
    collect((len(blocks) - 1) % 2, *blocks[-1])

    from_q = dot(wqkv[:, :feat], dq_t[...])
    from_kv = dot(wqkv[:, feat:], dkv_t[...])
    back[:main, :] = (from_q[:, :main] + from_kv[:, :main]).T.astype(BF16)
    rest = from_q[:, main:].T
    last = from_kv[:, main:].T
    for j in range(per):
        last = last + rest[j * left : (j + 1) * left]
    back[main:, :] = last.astype(BF16)
    part_gain = jnp.sum(back[...].astype(F32) * wide[...], 0, keepdims=True)
    column = jnp.broadcast_to(part_gain, (128, feat)).T
    gain_col[...] = jnp.where(lanes(column.shape) < 2, column, 0.0)

    rows = feat // 2
    theirs = pl.multiple_of((1 - core) * rows, rows)
    for block, value in enumerate(partial_sums(theirs, normed_t, g_low, dq_t, dkv_t, attn_t)):
        send[:, block * feat : (block + 1) * feat] = value.astype(BF16)
    send[:, 4 * feat :] = gain_col[pl.ds(theirs, rows), :].astype(BF16)


def grads_scratch(tokens, feat):
    ext = tokens // 128 * 128 + 128
    return [
        pltpu.VMEM((tokens, feat), F32),
        pltpu.VMEM((ext, feat), BF16),
        pltpu.VMEM((feat, ext), BF16),
        pltpu.VMEM((2 * feat, tokens), BF16),
        pltpu.VMEM((tokens, 2 * feat), BF16),
        pltpu.VMEM((feat, ext), BF16),
        pltpu.VMEM((128, 128), BF16),
        pltpu.VMEM((tokens, 128), BF16),
        pltpu.VMEM((128, ext), BF16),
        pltpu.VMEM((2, tokens, 256), F32),
        pltpu.VMEM((2, tokens, 256), F32),
        pltpu.VMEM((2, tokens, 256), BF16),
        pltpu.VMEM((2, tokens, 256), BF16),
        pltpu.VMEM((2, 128, tokens), F32),
    ]


def tokens_kernel(
    q0, q1, q2, q3, gain, wout, attn_t, back, normed_t, g_low, dq_t, dkv_t, gain_col,
    keep, own, east, north, wide,
):
    feat = attn_t.shape[0]
    half = feat // 2
    mine = pl.multiple_of(lax.axis_index("core") * half, half)
    for block, value in enumerate(partial_sums(mine, normed_t, g_low, dq_t, dkv_t, attn_t)):
        keep[:, block * feat : (block + 1) * feat] = value
    keep[:, 4 * feat :] = gain_col[pl.ds(mine, half), :]
    quads, outs = (q0, q1, q2, q3), (own, east, north.at[0], north.at[1])
    rows = q0.shape[1]
    gather_quads(quads, 0, wide)
    tok = wide[...]
    main = tok.shape[0] // 128 * 128
    left = tok.shape[0] - main
    added = dot(attn_t[...], wout[...], ((0,), (0,)))
    last = added[main : main + left]
    for at in range(main + left, added.shape[0], left):
        last = last + added[at : at + left]
    mixed = tok + jnp.concatenate([added[:main], last], 0)
    for j, out in enumerate(outs):
        out[0] = mixed[j * rows : (j + 1) * rows].astype(BF16).reshape(out.shape[1:])
    xhat, inv = normalise(tok)
    scaled = back[...].astype(F32) * gain[...]
    inner = (
        scaled
        - jnp.mean(scaled, -1, keepdims=True)
        - xhat * jnp.mean(scaled * xhat, -1, keepdims=True)
    )
    gather_quads(quads, 1, wide)
    grad = wide[...] + inv * inner
    for j, out in enumerate(outs):
        out[1] = grad[j * rows : (j + 1) * rows].astype(BF16).reshape(out.shape[1:])


def gain_total(tile):
    return jnp.where(lanes(tile.shape) == 0, jnp.sum(tile, -1, keepdims=True), 0.0)


def add_pair(keep, other):
    total = keep + other.astype(F32)
    rest = total - lax.reduce_precision(total, 8, 7)
    return jnp.where(lanes(total.shape) == total.shape[1] - 127, rest, total).astype(BF16)


def final_piece_kernel(factor, mine, next1, next2, next3, _, out):
    main = mine.shape[1] - 128
    total = ((mine[...] + next2[...]) + (next1[...] + next3[...])) * factor
    out[:, :main] = total[:, :main].astype(BF16)
    out[:, main:] = split_low(gain_total(total[:, main:]), 3)


def write_half(half, at, grad_qkv, grad_out, gain_grad, gains, copy):
    rows = half.shape[0]
    wide = grad_qkv.shape[1]
    main = wide + grad_out.shape[1]
    at = pl.multiple_of(at * rows, rows)
    copy(half.at[:, :wide], grad_qkv.at[pl.ds(at, rows), :])
    copy(half.at[:, wide:main], grad_out.at[pl.ds(at, rows), :])
    column = half[:, main:].astype(F32).T
    gains[...] = column[0:1] + column[1:2] + column[2:3]
    copy(gains, gain_grad.at[:, pl.ds(at, rows)])


def copier(sems, copies):
    def copy(src, dst):
        item = pltpu.make_async_copy(src, dst, sems.at[len(copies)])
        item.start()
        copies.append(item)

    return copy


def first_finish_kernel(
    mine, own, north, east, mixed, grad_tokens, grad_qkv, grad_out, gain_grad, gains, sems
):
    copies = []
    copy = copier(sems, copies)
    write_half(mine, lax.axis_index("core"), grad_qkv, grad_out, gain_grad, gains, copy)
    for quad, at, lon in (
        (own, SHIFT, SHIFT),
        (north.at[0], 0, SHIFT),
        (east.at[0], SHIFT, 0),
        (east.at[1], 0, 0),
    ):
        block = (0, pl.ds(at, SHIFT), pl.ds(lon, SHIFT))
        copy(quad.at[0], mixed.at[block])
        copy(quad.at[1], grad_tokens.at[block])
    for item in copies:
        item.wait()


def last_finish_kernel(theirs, _, __, ___, grad_qkv, grad_out, gain_grad, gains, sems):
    copies = []
    copy = copier(sems, copies)
    write_half(theirs, 1 - lax.axis_index("core"), grad_qkv, grad_out, gain_grad, gains, copy)
    for item in copies:
        item.wait()


def shards(tokens, layer_norm_gain, cotangent, w_qkv, w_out):
    _, lat_rows, lon_cols, levels, feat = tokens.shape
    lat_n, lon_n = lax.axis_size(LAT), lax.axis_size(LON)
    quad_tokens = SHIFT * SHIFT * levels
    n_tokens = 4 * quad_tokens

    def pairs(target):
        return [
            (a * lon_n + o, target(a, o)[0] % lat_n * lon_n + target(a, o)[1] % lon_n)
            for a in range(lat_n)
            for o in range(lon_n)
        ]

    vmem = pl.BlockSpec(memory_space=pltpu.VMEM)
    hbm = pl.BlockSpec(memory_space=pl.ANY)
    params = pltpu.CompilerParams(vmem_limit_bytes=40 * 1024 * 1024)
    with jax.named_scope("window_in"):

        def quad(rows, cols):
            both = jnp.stack([tokens[0, rows, cols], cotangent[0, rows, cols]])
            return both.reshape(2, quad_tokens, feat)

        low, high = slice(0, SHIFT), slice(SHIFT, 2 * SHIFT)
        own, east = quad(high, high), quad(high, low)
        north, corner = quad(low, high), quad(low, low)
        east = lax.ppermute(east, EVERY, pairs(lambda a, o: (a, o - 1)))
        north = lax.ppermute(north, EVERY, pairs(lambda a, o: (a - 1, o)))
        corner = lax.ppermute(corner, EVERY, pairs(lambda a, o: (a - 1, o - 1)))
        quads = [own, east, north, corner]
    gain_row = layer_norm_gain[None, :]
    rows, width = feat // 2, 4 * feat + 128
    ext = n_tokens // 128 * 128 + 128
    with jax.named_scope("weights"):
        w_qkv_t, w_out_near = pl.pallas_call(
            weights_kernel,
            in_specs=[vmem] * 2,
            out_specs=[vmem] * 2,
            out_shape=[
                jax.ShapeDtypeStruct((3 * feat, feat), BF16),
                jax.ShapeDtypeStruct((feat, feat), BF16),
            ],
            compiler_params=params,
        )(w_qkv, w_out)
    with jax.named_scope("window_grads"):
        send, *shared = pl.pallas_call(
            grads_kernel,
            in_specs=[vmem] * 8,
            out_specs=[vmem] * 8,
            out_shape=[
                jax.ShapeDtypeStruct((rows, width), BF16),
                jax.ShapeDtypeStruct((feat, ext), BF16),
                jax.ShapeDtypeStruct((n_tokens, feat), BF16),
                jax.ShapeDtypeStruct((feat, ext), BF16),
                jax.ShapeDtypeStruct((ext, feat), BF16),
                jax.ShapeDtypeStruct((feat, ext), BF16),
                jax.ShapeDtypeStruct((2 * feat, n_tokens), BF16),
                jax.ShapeDtypeStruct((feat, 128), F32),
            ],
            scratch_shapes=grads_scratch(n_tokens, feat),
            compiler_params=params,
        )(*quads, gain_row, w_qkv, w_qkv_t, w_out_near)
    swap = [(0, 1), (1, 0)]
    with jax.named_scope("sum_cores"):
        other = lax.ppermute(send, "core", swap)
    with jax.named_scope("window_tokens"):
        keep, own, east, north = pl.pallas_call(
            tokens_kernel,
            in_specs=[vmem] * 13,
            out_specs=[vmem] * 4,
            out_shape=[
                jax.ShapeDtypeStruct((rows, width), F32),
                *(
                    jax.ShapeDtypeStruct(lead + (2, SHIFT, SHIFT, levels, feat), BF16)
                    for lead in ((), (), (2,))
                ),
            ],
            scratch_shapes=[pltpu.VMEM((n_tokens, feat), F32)],
            compiler_params=params,
        )(*quads, gain_row, w_out, *shared)
    with jax.named_scope("sum_cores"):
        pair_sum = add_pair(keep, other)
    pair_sum, north = lax.optimization_barrier((pair_sum, north))
    near, far = lax.axis_size(NEAR), lax.axis_size(FAR)
    factor = 1.0 / math.sqrt(lat_n * lat_rows * lon_n * lon_cols * levels)
    chunk = rows // near
    with jax.named_scope("sum_near"):
        pieces = lax.all_to_all(pair_sum.reshape(near, chunk, width), NEAR, 0, 0)
        piece = jnp.sum(pieces.astype(F32), 0)
    with jax.named_scope("sum_far"):
        others = [
            lax.ppermute(piece, FAR, [(i, (i + by) % far) for i in range(far)])
            for by in range(1, far)
        ]
    after, north = lax.optimization_barrier((piece, north))
    with jax.named_scope("window_out"):
        north = lax.ppermute(north, EVERY, pairs(lambda a, o: (a + 1, o)))
    with jax.named_scope("sum_far"):
        piece = pl.pallas_call(
            functools.partial(final_piece_kernel, factor),
            in_specs=[vmem] * far + [hbm],
            out_specs=vmem,
            out_shape=jax.ShapeDtypeStruct((chunk, width), BF16),
            compiler_params=params,
        )(piece, *others, after)
    piece, north = lax.optimization_barrier((piece, north))
    with jax.named_scope("window_out"):
        east = jnp.stack([east, north[1]])
        east = lax.ppermute(east, EVERY, pairs(lambda a, o: (a, o + 1)))
    with jax.named_scope("share"):
        mine = lax.all_to_all(jnp.broadcast_to(piece[None], (near,) + piece.shape), NEAR, 0, 0)
        mine = mine.reshape(rows, width)
        mine, east = lax.optimization_barrier((mine, east))
        theirs = lax.ppermute(mine, "core", swap)
    with jax.named_scope("finish"):
        shape = (1, 2 * SHIFT, 2 * SHIFT, levels, feat)
        final = [
            jax.ShapeDtypeStruct((feat, 3 * feat), BF16),
            jax.ShapeDtypeStruct((feat, feat), BF16),
            jax.ShapeDtypeStruct((1, feat), F32),
        ]
        mixed, grad_tokens, *halves = pl.pallas_call(
            first_finish_kernel,
            in_specs=[vmem] + [hbm] * 3,
            out_specs=[hbm] * 5,
            out_shape=[jax.ShapeDtypeStruct(shape, BF16)] * 2 + final,
            scratch_shapes=[pltpu.VMEM((1, rows), F32), pltpu.SemaphoreType.DMA((11,))],
            compiler_params=params,
        )(mine, own, north, east)
        grad_qkv, grad_out, gain_gradient = pl.pallas_call(
            last_finish_kernel,
            in_specs=[vmem] + [hbm] * 3,
            out_specs=[hbm] * 3,
            out_shape=final,
            input_output_aliases={1: 0, 2: 1, 3: 2},
            scratch_shapes=[pltpu.VMEM((1, rows), F32), pltpu.SemaphoreType.DMA((3,))],
            compiler_params=params,
        )(theirs, *halves)
    return mixed, grad_tokens, gain_gradient[0], grad_qkv, grad_out


def solution(mesh):
    fine = Mesh(mesh.devices.reshape(2, 4, 4, 2, 2, 2), EVERY)
    grid = P(None, LAT, LON, None, None)
    return jax.shard_map(
        shards,
        mesh=fine,
        in_specs=(grid, P(), grid, P(), P()),
        out_specs=(grid, grid, P(), P(), P()),
        check_vma=False,
    )
```

```python
import functools
import math

import jax
import jax.numpy as jnp
from jax import lax
from jax.experimental import pallas as pl
from jax.experimental.pallas import tpu as pltpu
from jax.sharding import Mesh
from jax.sharding import PartitionSpec as P

HEADS = 16
WIN = 12
SHIFT = 6
EPS = 1e-05
MASKED = -1e30
F32 = jnp.float32
BF16 = jnp.bfloat16

LAT = ("xh", "y")
LON = ("zh", "zl", "xl", "core")
NEAR = ("xh", "y", "zl", "xl")
FAR = "zh"
EVERY = LAT + LON


def dot(a, b, dims=((1,), (0,))):
    return lax.dot_general(a, b, (dims, ((), ())), preferred_element_type=F32)


def normalise(tok):
    mean = jnp.mean(tok, -1, keepdims=True)
    centred = tok - mean
    inv = lax.rsqrt(jnp.mean(centred * centred, -1, keepdims=True) + EPS)
    return centred * inv, inv


def gather_quads(refs, which, out):
    rows = refs[0].shape[1]
    for j, ref in enumerate(refs):
        out[j * rows : (j + 1) * rows, :] = ref[which].astype(F32)


def lanes(shape):
    return lax.broadcasted_iota(jnp.int32, shape, len(shape) - 1)


def split_low(tile):
    lane = lanes(tile.shape)
    out = jnp.zeros_like(tile)
    for first in (0, 2):
        held = jnp.where((lane == first) | (lane == first + 1), tile, 0.0)
        rest = jnp.broadcast_to(jnp.sum(held, -1, keepdims=True), tile.shape)
        for i in range(3):
            part = rest.astype(BF16).astype(F32)
            out = jnp.where(lane == first // 2 * 3 + i, part, out)
            rest = rest - part
    return out.astype(BF16)


def weights_kernel(wqkv, wout, wqkv_t, wout_near):
    wqkv_t[...] = wqkv[...].T
    wout_near[...] = wout[...]


def partial_sums(start, normed_t, g_low, dq_t, dkv_t, attn_t):
    feat = attn_t.shape[0]
    tokens = dkv_t.shape[1]
    pick = pl.ds(start, feat // 2)
    return (
        dot(normed_t[pick, :], dq_t[...], ((1,), (1,))),
        dot(normed_t[pick, :tokens], dkv_t[:feat, :], ((1,), (1,))),
        dot(normed_t[pick, :tokens], dkv_t[feat:, :], ((1,), (1,))),
        dot(attn_t[pick, :], g_low[...]),
    )


def grads_kernel(
    q0, q1, q2, q3, gain, wqkv, wqkv_t, wout,
    send, attn_t, normed_t, g_low, dq_t, dkv_t,
    wide, normed, q_t, kv_t, kv, do_t,
    diag, side, bias, scores, d_probs, p_low, d_low, acc,
):
    quads = (q0, q1, q2, q3)
    tokens, feat = wide.shape
    main = tokens // 128 * 128
    left = tokens - main
    ext = normed.shape[0]
    size = feat // HEADS
    per = 128 // size
    half = tokens // 2
    core = lax.axis_index("core")
    edge = lax.axis_index(LAT) == lax.axis_size(LAT) - 1
    inv_root = 1.0 / math.sqrt(size)
    to_exp2 = inv_root * math.log2(math.e)

    def repeat_left(ref):
        for j in range(1, per):
            ref[tokens + (j - 1) * left : tokens + j * left, :] = ref[main:tokens, :]

    gather_quads(quads, 1, wide)
    g_low[:tokens, :] = wide[...].astype(BF16)
    repeat_left(g_low)
    do_t[...] = dot(wout[...], g_low[...], ((1,), (1,))).astype(BF16)
    gather_quads(quads, 0, wide)
    xhat, _ = normalise(wide[...])
    wide[...] = xhat
    normed[:tokens, :] = (xhat * gain[...]).astype(BF16)
    repeat_left(normed)
    q_t[...] = dot(wqkv_t[:feat, :], normed[...], ((1,), (1,))).astype(BF16)
    kv_t[...] = dot(wqkv_t[feat:, :], normed[:tokens, :], ((1,), (1,))).astype(BF16)
    kv[...] = dot(normed[:tokens, :], wqkv[:, feat:]).astype(BF16)
    normed_t[...] = normed[...].T

    row_head = lax.broadcasted_iota(jnp.int32, (128, 128), 0) // size
    diag[...] = jnp.where(row_head == lanes((128, 128)) // left, 1.0, 0.0).astype(BF16)
    late_key = lax.broadcasted_iota(jnp.int32, (tokens, 128), 0) >= half
    lane = lanes((tokens, 128))
    side[...] = jnp.where(
        jnp.logical_or(
            jnp.logical_and(lane == 0, late_key),
            jnp.logical_and(lane == 1, jnp.logical_not(late_key)),
        ),
        1.0,
        0.0,
    ).astype(BF16)
    which = lax.broadcasted_iota(jnp.int32, (128, ext), 0)
    late_query = lanes((128, ext)) >= half
    blocked = jnp.logical_or(
        jnp.logical_and(which == 0, jnp.logical_not(late_query)),
        jnp.logical_and(which == 1, late_query),
    )
    bias[...] = jnp.where(jnp.logical_and(blocked, edge), MASKED, 0.0).astype(BF16)

    def spread(block, h):
        parts = []
        if h > 0:
            parts.append(jnp.zeros((h * size, block.shape[1]), BF16))
        parts.append(block)
        if h < per - 1:
            parts.append(jnp.zeros(((per - 1 - h) * size, block.shape[1]), BF16))
        return jnp.concatenate(parts, 0)

    def operand(ref, g, h):
        rows = slice(128 * g, 128 * (g + 1))
        if h is None:
            return ref[rows, main:ext] * diag[...]
        return spread(ref[128 * g + size * h : 128 * g + size * (h + 1), :main], h)

    def score(slot, g, h):
        cols = slice(128 * g, 128 * (g + 1))
        at, width = (slice(main, ext), ext - main) if h is None else (slice(0, main), main)
        keys = jnp.concatenate([kv[:, cols], side[...]], 1)
        queries = jnp.concatenate([operand(q_t, g, h), bias[:, at]], 0)
        scores[slot, :, :width] = dot(keys, queries)
        values = kv[:, feat + 128 * g : feat + 128 * (g + 1)]
        d_probs[slot, :, :width] = dot(values, operand(do_t, g, h))

    step = 32

    def soften(slot, h):
        width = ext - main if h is None else main
        chunks = [slice(c, c + step) for c in range(0, tokens, step)]

        def fold(value, op):
            return op(value.reshape(step // 8, 8, width), axis=0)

        top = None
        for c in chunks:
            part = fold(scores[slot, c, :width], jnp.max)
            top = part if top is None else jnp.maximum(top, part)
        top = jnp.max(top, 0, keepdims=True)
        total = jnp.zeros((8, width), F32)
        for c in chunks:
            e = jnp.exp2((scores[slot, c, :width] - top) * to_exp2)
            scores[slot, c, :width] = e
            total = total + fold(e, jnp.sum)
        scale = 1.0 / jnp.sum(total, 0, keepdims=True)
        delta = jnp.zeros((8, width), F32)
        for c in chunks:
            p = scores[slot, c, :width] * scale
            p_low[slot, c, :width] = p.astype(BF16)
            delta = delta + fold(d_probs[slot, c, :width] * p, jnp.sum)
        delta = jnp.sum(delta, 0, keepdims=True)
        scale = scale * inv_root
        for c in chunks:
            p = scores[slot, c, :width] * scale
            d_low[slot, c, :width] = (p * (d_probs[slot, c, :width] - delta)).astype(BF16)

    def collect(slot, g, h):
        nt = ((1,), (1,))
        if h is None:
            rows = slice(128 * g, 128 * (g + 1))
            later = slice(feat + 128 * g, feat + 128 * (g + 1))
            width = ext - main
            keep_own = diag[...].astype(F32)
            p, d = p_low[slot, :, :width], d_low[slot, :, :width]
            attn_t[rows, main:ext] = (dot(kv_t[later, :], p) * keep_own).astype(BF16)
            dq_t[rows, main:ext] = (dot(kv_t[rows, :], d) * keep_own).astype(BF16)
            acc[0] = dot(operand(q_t, g, h), d, nt)
            acc[1] = dot(operand(do_t, g, h), p, nt)
            return
        rows = slice(128 * g + size * h, 128 * g + size * (h + 1))
        later = slice(feat + rows.start, feat + rows.stop)
        own = slice(size * h, size * (h + 1))
        p, d = p_low[slot], d_low[slot]
        attn_t[rows, :main] = dot(kv_t[later, :], p).astype(BF16)
        dq_t[rows, :main] = dot(kv_t[rows, :], d).astype(BF16)
        dkv_t[rows, :] = (dot(q_t[rows, :main], d, nt) + acc[0, own, :]).astype(BF16)
        dkv_t[later, :] = (dot(do_t[rows, :main], p, nt) + acc[1, own, :]).astype(BF16)

    blocks = [(g, h) for g in range(HEADS // per) for h in (None, *range(per))]
    score(0, *blocks[0])
    for n, (g, h) in enumerate(blocks):
        if n + 1 < len(blocks):
            score((n + 1) % 2, *blocks[n + 1])
        soften(n % 2, h)
        if n > 0:
            collect((n - 1) % 2, *blocks[n - 1])
    collect((len(blocks) - 1) % 2, *blocks[-1])

    rows = feat // 2
    theirs = pl.multiple_of((1 - core) * rows, rows)
    for block, value in enumerate(partial_sums(theirs, normed_t, g_low, dq_t, dkv_t, attn_t)):
        send[:, block * feat : (block + 1) * feat] = value.astype(BF16)
    send[:, 4 * feat :] = jnp.zeros((rows, 128), BF16)


def grads_scratch(tokens, feat):
    ext = tokens // 128 * 128 + 128
    return [
        pltpu.VMEM((tokens, feat), F32),
        pltpu.VMEM((ext, feat), BF16),
        pltpu.VMEM((feat, ext), BF16),
        pltpu.VMEM((2 * feat, tokens), BF16),
        pltpu.VMEM((tokens, 2 * feat), BF16),
        pltpu.VMEM((feat, ext), BF16),
        pltpu.VMEM((128, 128), BF16),
        pltpu.VMEM((tokens, 128), BF16),
        pltpu.VMEM((128, ext), BF16),
        pltpu.VMEM((2, tokens, 256), F32),
        pltpu.VMEM((2, tokens, 256), F32),
        pltpu.VMEM((2, tokens, 256), BF16),
        pltpu.VMEM((2, tokens, 256), BF16),
        pltpu.VMEM((2, 128, tokens), F32),
    ]


def tokens_kernel(
    q0, q1, q2, q3, gain, wqkv, wout, attn_t, normed_t, g_low, dq_t, dkv_t,
    keep, own, east, north, wide, back, gain_col,
):
    feat = attn_t.shape[0]
    half = feat // 2
    mine = pl.multiple_of(lax.axis_index("core") * half, half)
    for block, value in enumerate(partial_sums(mine, normed_t, g_low, dq_t, dkv_t, attn_t)):
        keep[:, block * feat : (block + 1) * feat] = value
    quads, outs = (q0, q1, q2, q3), (own, east, north.at[0], north.at[1])
    rows = q0.shape[1]
    gather_quads(quads, 0, wide)
    tok = wide[...]
    main = tok.shape[0] // 128 * 128
    left = tok.shape[0] - main
    added = dot(attn_t[...], wout[...], ((0,), (0,)))
    last = added[main : main + left]
    for at in range(main + left, added.shape[0], left):
        last = last + added[at : at + left]
    mixed = tok + jnp.concatenate([added[:main], last], 0)
    for j, out in enumerate(outs):
        out[0] = mixed[j * rows : (j + 1) * rows].astype(BF16).reshape(out.shape[1:])
    xhat, inv = normalise(tok)
    per = 128 // (feat // HEADS)
    from_q = dot(wqkv[:, :feat], dq_t[...])
    from_kv = dot(wqkv[:, feat:], dkv_t[...])
    back[:main, :] = (from_q[:, :main] + from_kv[:, :main]).T.astype(BF16)
    rest = from_q[:, main:].T
    last = from_kv[:, main:].T
    for j in range(per):
        last = last + rest[j * left : (j + 1) * left]
    back[main:, :] = last.astype(BF16)
    part_gain = jnp.sum(back[...].astype(F32) * xhat, 0, keepdims=True)
    column = jnp.broadcast_to(part_gain, (128, feat)).T
    gain_col[...] = column

    theirs = pl.multiple_of((1 - lax.axis_index("core")) * half, half)
    lane = lanes((half, 128))
    other = jnp.where(lane < 4, gain_col[pl.ds(theirs, half), :], 0.0)
    keep[:, 4 * feat :] = jnp.where(lane < 2, gain_col[pl.ds(mine, half), :], other)
    scaled = back[...].astype(F32) * gain[...]
    inner = (
        scaled
        - jnp.mean(scaled, -1, keepdims=True)
        - xhat * jnp.mean(scaled * xhat, -1, keepdims=True)
    )
    gather_quads(quads, 1, wide)
    grad = wide[...] + inv * inner
    for j, out in enumerate(outs):
        out[1] = grad[j * rows : (j + 1) * rows].astype(BF16).reshape(out.shape[1:])


def add_pair(keep, other):
    total = keep + other.astype(F32)
    rest = total - lax.reduce_precision(total, 8, 7)
    lane = lanes(total.shape) - (total.shape[1] - 128)
    return jnp.where((lane == 1) | (lane == 3), rest, total).astype(BF16)


def final_piece_kernel(factor, mine, next1, next2, next3, _, out):
    main = mine.shape[1] - 128
    total = ((mine[...] + next2[...]) + (next1[...] + next3[...])) * factor
    out[:, :main] = total[:, :main].astype(BF16)
    out[:, main:] = split_low(total[:, main:])


def write_half(half, at, grad_qkv, grad_out, copy):
    rows = half.shape[0]
    wide = grad_qkv.shape[1]
    main = wide + grad_out.shape[1]
    at = pl.multiple_of(at * rows, rows)
    copy(half.at[:, :wide], grad_qkv.at[pl.ds(at, rows), :])
    copy(half.at[:, wide:main], grad_out.at[pl.ds(at, rows), :])


def copier(sems, copies):
    def copy(src, dst):
        item = pltpu.make_async_copy(src, dst, sems.at[len(copies)])
        item.start()
        copies.append(item)

    return copy


def first_finish_kernel(
    mine, own, north, east, mixed, grad_tokens, grad_qkv, grad_out, sems
):
    copies = []
    copy = copier(sems, copies)
    write_half(mine, lax.axis_index("core"), grad_qkv, grad_out, copy)
    for quad, at, lon in (
        (own, SHIFT, SHIFT),
        (north.at[0], 0, SHIFT),
        (east.at[0], SHIFT, 0),
        (east.at[1], 0, 0),
    ):
        block = (0, pl.ds(at, SHIFT), pl.ds(lon, SHIFT))
        copy(quad.at[0], mixed.at[block])
        copy(quad.at[1], grad_tokens.at[block])
    for item in copies:
        item.wait()


def last_finish_kernel(theirs, mine, _, __, grad_qkv, grad_out, gain_grad, gains, sems):
    copies = []
    copy = copier(sems, copies)
    core = lax.axis_index("core")
    rows = mine.shape[0]
    write_half(theirs, 1 - core, grad_qkv, grad_out, copy)
    main = mine.shape[1] - 128
    sums = []
    for half in (mine, theirs):
        column = half[:, main:].astype(F32).T
        sums.append([column[i : i + 1] + column[i + 1 : i + 2] + column[i + 2 : i + 3] for i in (0, 3)])
    gains[:, pl.ds(pl.multiple_of(core * rows, rows), rows)] = sums[0][0] + sums[1][1]
    gains[:, pl.ds(pl.multiple_of((1 - core) * rows, rows), rows)] = sums[1][0] + sums[0][1]
    copy(gains, gain_grad)
    for item in copies:
        item.wait()


def shards(tokens, layer_norm_gain, cotangent, w_qkv, w_out):
    _, lat_rows, lon_cols, levels, feat = tokens.shape
    lat_n, lon_n = lax.axis_size(LAT), lax.axis_size(LON)
    quad_tokens = SHIFT * SHIFT * levels
    n_tokens = 4 * quad_tokens

    def pairs(target):
        return [
            (a * lon_n + o, target(a, o)[0] % lat_n * lon_n + target(a, o)[1] % lon_n)
            for a in range(lat_n)
            for o in range(lon_n)
        ]

    vmem = pl.BlockSpec(memory_space=pltpu.VMEM)
    hbm = pl.BlockSpec(memory_space=pl.ANY)
    params = pltpu.CompilerParams(vmem_limit_bytes=40 * 1024 * 1024)
    with jax.named_scope("window_in"):

        def quad(rows, cols):
            both = jnp.stack([tokens[0, rows, cols], cotangent[0, rows, cols]])
            return both.reshape(2, quad_tokens, feat)

        low, high = slice(0, SHIFT), slice(SHIFT, 2 * SHIFT)
        own, east = quad(high, high), quad(high, low)
        north, corner = quad(low, high), quad(low, low)
        east = lax.ppermute(east, EVERY, pairs(lambda a, o: (a, o - 1)))
        north = lax.ppermute(north, EVERY, pairs(lambda a, o: (a - 1, o)))
        corner = lax.ppermute(corner, EVERY, pairs(lambda a, o: (a - 1, o - 1)))
        quads = [own, east, north, corner]
    gain_row = layer_norm_gain[None, :]
    rows, width = feat // 2, 4 * feat + 128
    ext = n_tokens // 128 * 128 + 128
    with jax.named_scope("weights"):
        w_qkv_t, w_out_near = pl.pallas_call(
            weights_kernel,
            in_specs=[vmem] * 2,
            out_specs=[vmem] * 2,
            out_shape=[
                jax.ShapeDtypeStruct((3 * feat, feat), BF16),
                jax.ShapeDtypeStruct((feat, feat), BF16),
            ],
            compiler_params=params,
        )(w_qkv, w_out)
    with jax.named_scope("window_grads"):
        send, *shared = pl.pallas_call(
            grads_kernel,
            in_specs=[vmem] * 8,
            out_specs=[vmem] * 6,
            out_shape=[
                jax.ShapeDtypeStruct((rows, width), BF16),
                jax.ShapeDtypeStruct((feat, ext), BF16),
                jax.ShapeDtypeStruct((feat, ext), BF16),
                jax.ShapeDtypeStruct((ext, feat), BF16),
                jax.ShapeDtypeStruct((feat, ext), BF16),
                jax.ShapeDtypeStruct((2 * feat, n_tokens), BF16),
            ],
            scratch_shapes=grads_scratch(n_tokens, feat),
            compiler_params=params,
        )(*quads, gain_row, w_qkv, w_qkv_t, w_out_near)
    swap = [(0, 1), (1, 0)]
    with jax.named_scope("sum_cores"):
        other = lax.ppermute(send, "core", swap)
    with jax.named_scope("window_tokens"):
        keep, own, east, north = pl.pallas_call(
            tokens_kernel,
            in_specs=[vmem] * 12,
            out_specs=[vmem] * 4,
            out_shape=[
                jax.ShapeDtypeStruct((rows, width), F32),
                *(
                    jax.ShapeDtypeStruct(lead + (2, SHIFT, SHIFT, levels, feat), BF16)
                    for lead in ((), (), (2,))
                ),
            ],
            scratch_shapes=[
                pltpu.VMEM((n_tokens, feat), F32),
                pltpu.VMEM((n_tokens, feat), BF16),
                pltpu.VMEM((feat, 128), F32),
            ],
            compiler_params=params,
        )(*quads, gain_row, w_qkv, w_out, *shared)
    with jax.named_scope("sum_cores"):
        pair_sum = add_pair(keep, other)
    pair_sum, north = lax.optimization_barrier((pair_sum, north))
    near, far = lax.axis_size(NEAR), lax.axis_size(FAR)
    factor = 1.0 / math.sqrt(lat_n * lat_rows * lon_n * lon_cols * levels)
    chunk = rows // near
    with jax.named_scope("sum_near"):
        pieces = lax.all_to_all(pair_sum.reshape(near, chunk, width), NEAR, 0, 0)
        piece = jnp.sum(pieces.astype(F32), 0)
    with jax.named_scope("sum_far"):
        others = [
            lax.ppermute(piece, FAR, [(i, (i + by) % far) for i in range(far)])
            for by in range(1, far)
        ]
    after, north = lax.optimization_barrier((piece, north))
    with jax.named_scope("window_out"):
        north = lax.ppermute(north, EVERY, pairs(lambda a, o: (a + 1, o)))
    with jax.named_scope("sum_far"):
        piece = pl.pallas_call(
            functools.partial(final_piece_kernel, factor),
            in_specs=[vmem] * far + [hbm],
            out_specs=vmem,
            out_shape=jax.ShapeDtypeStruct((chunk, width), BF16),
            compiler_params=params,
        )(piece, *others, after)
    piece, north = lax.optimization_barrier((piece, north))
    with jax.named_scope("window_out"):
        east = jnp.stack([east, north[1]])
        east = lax.ppermute(east, EVERY, pairs(lambda a, o: (a, o + 1)))
    with jax.named_scope("share"):
        mine = lax.all_to_all(jnp.broadcast_to(piece[None], (near,) + piece.shape), NEAR, 0, 0)
        mine = mine.reshape(rows, width)
        mine, east = lax.optimization_barrier((mine, east))
        theirs = lax.ppermute(mine, "core", swap)
    with jax.named_scope("finish"):
        shape = (1, 2 * SHIFT, 2 * SHIFT, levels, feat)
        final = [
            jax.ShapeDtypeStruct((feat, 3 * feat), BF16),
            jax.ShapeDtypeStruct((feat, feat), BF16),
            jax.ShapeDtypeStruct((1, feat), F32),
        ]
        mixed, grad_tokens, *halves = pl.pallas_call(
            first_finish_kernel,
            in_specs=[vmem] + [hbm] * 3,
            out_specs=[hbm] * 4,
            out_shape=[jax.ShapeDtypeStruct(shape, BF16)] * 2 + final[:2],
            scratch_shapes=[pltpu.SemaphoreType.DMA((10,))],
            compiler_params=params,
        )(mine, own, north, east)
        grad_qkv, grad_out, gain_gradient = pl.pallas_call(
            last_finish_kernel,
            in_specs=[vmem] * 2 + [hbm] * 2,
            out_specs=[hbm] * 3,
            out_shape=final,
            input_output_aliases={2: 0, 3: 1},
            scratch_shapes=[pltpu.VMEM((1, feat), F32), pltpu.SemaphoreType.DMA((3,))],
            compiler_params=params,
        )(theirs, mine, *halves)
    return mixed, grad_tokens, gain_gradient[0], grad_qkv, grad_out


def solution(mesh):
    fine = Mesh(mesh.devices.reshape(2, 4, 4, 2, 2, 2), EVERY)
    grid = P(None, LAT, LON, None, None)
    return jax.shard_map(
        shards,
        mesh=fine,
        in_specs=(grid, P(), grid, P(), P()),
        out_specs=(grid, grid, P(), P(), P()),
        check_vma=False,
    )
```
